32 devices in a mesh: dp: 16 (over z, y, x), pipe: 2 (over core).
Axes of the slice: x: 2, y: 2, z: 4, core: 2. Of those that a mesh axis runs over, the one named last changes fastest.
Arguments:
- text_states: bfloat16 [2, 1024, 4096], P('pipe', 'dp')
- image_states: bfloat16 [2, 512, 4096], P(None, ('dp', 'pipe'))
- image_start: int32 [2, 16], P(None, 'dp'), may hold values from 0 to 31
- w_query: bfloat16 [2, 4096, 512], P('pipe')
- w_key: bfloat16 [2, 4096, 128], P('pipe', 'dp')
- w_value: bfloat16 [2, 4096, 128], P('pipe', 'dp'), may hold values from -0.09375 to 0.09375
- w_out: bfloat16 [2, 512, 4096], P('pipe'), may hold values from -0.25 to 0.25
- query_gain: float32 [2, 128], P('pipe'), may hold values from 1 to 2.5
- key_gain: float32 [2, 128], P('pipe'), may hold values from 1 to 2
- cross_gate: float32 [2], P('pipe'), may hold values from 0.3 to 1.2
Outputs:
- final_states: bfloat16 [2, 1024, 4096], P('pipe', 'dp')
The draws below stay inside these ranges and needn't reach their ends.
All inputs are finite; a program needn't handle non-finite values.
Results may differ from the reference program's by a relative error of at most 0.013.
Values may be sent and summed in bfloat16 or wider, within the bound.
A program may use at most 64 MiB of HBM per device.

```python
import math
import jax
import jax.numpy as jnp
from jax import lax

D = 4096
HD = 128
QH = 4
TOK_DEV = 64
MICRO = 2
TOKENS = 1024
IMG_GROUP = 32
IMAGES = 512
N_DP = 16
N_PIPE = 2


def draw_text_states(key, part):
    key = jax.random.fold_in(key, 11)
    first, second, third = jax.random.split(key, 3)
    shape = (MICRO, TOKENS, D)
    base = jnp.clip(jax.random.normal(first, shape, jnp.float32), -4.0, 4.0)
    rows = jnp.exp(jax.random.uniform(second, (MICRO, TOKENS, 1), jnp.float32, math.log(0.5), math.log(4.0)))
    columns = jnp.exp(jax.random.uniform(third, (1, 1, D), jnp.float32, math.log(0.5), math.log(2.0)))
    return (base * rows * columns).astype(jnp.bfloat16)


def draw_image_states(key, part):
    key = jax.random.fold_in(key, 12)
    first, second, third = jax.random.split(key, 3)
    shape = (MICRO, IMAGES, D)
    base = jnp.clip(jax.random.normal(first, shape, jnp.float32), -4.0, 4.0)
    rows = jnp.exp(jax.random.uniform(second, (MICRO, IMAGES, 1), jnp.float32, math.log(0.5), math.log(4.0)))
    columns = jnp.exp(jax.random.uniform(third, (1, 1, D), jnp.float32, math.log(0.5), math.log(2.0)))
    return (base * rows * columns).astype(jnp.bfloat16)


def draw_w_query(key, part):
    key = jax.random.fold_in(key, 13)
    first, second = jax.random.split(key, 2)
    shape = (N_PIPE, D, QH * HD)
    base = jnp.clip(jax.random.normal(first, shape, jnp.float32), -4.0, 4.0)
    columns = jnp.exp(jax.random.uniform(second, (N_PIPE, 1, QH * HD), jnp.float32, 0.0, math.log(10.0)))
    return (base * columns / math.sqrt(D)).astype(jnp.bfloat16)


def draw_w_key(key, part):
    key = jax.random.fold_in(key, 14)
    first, second = jax.random.split(key, 2)
    shape = (N_PIPE, D, HD)
    base = jnp.clip(jax.random.normal(first, shape, jnp.float32), -4.0, 4.0)
    columns = jnp.exp(jax.random.uniform(second, (N_PIPE, 1, HD), jnp.float32, 0.0, math.log(10.0)))
    return (base * columns / math.sqrt(D)).astype(jnp.bfloat16)


def touch_ends(values, rng, least, top_value):
    dims = values.shape
    place = [jax.random.randint(jax.random.fold_in(rng, axis), (), 0, dims[axis]) for axis in range(len(dims))]
    values = values.at[tuple(place)].set(least)
    longest = dims.index(max(dims))
    place[longest] = (place[longest] + 1) % dims[longest]
    return values.at[tuple(place)].set(top_value)


def level_of(key, shape, shards, low, high):
    def one(position, blocks):
        draws = jax.random.uniform(jax.random.fold_in(jax.random.fold_in(key, 6), position), (blocks,), jnp.float32, low / len(shards), high / len(shards))
        return jnp.repeat(jnp.exp(draws), shape[position] // blocks).reshape((-1,) + (1,) * (len(shape) - position - 1))

    gain = one(*shards[0])
    for cut in shards[1:]:
        gain = gain * one(*cut)
    return gain


def centred(rng, dims, width, most, cuts=(), kind=jnp.bfloat16):
    result = jax.random.normal(rng, dims, jnp.float32) * width
    if len(cuts) > 0:
        result = level_of(rng, dims, cuts, -0.22, 0.18) * result
    return jnp.clip(result, min=-most, max=most).astype(kind)


def setup_inputs(seed: int = 0) -> dict:
    seeds = jax.random.split(jax.random.key(seed), 11)
    text_states = draw_text_states(jax.random.fold_in(seeds[10], 71), 0)
    image_states = draw_image_states(jax.random.fold_in(seeds[10], 71), 0)
    image_start = touch_ends(jax.random.randint(seeds[2], (MICRO, N_DP), 0, TOK_DEV // 2), jax.random.fold_in(seeds[2], 1), 0, (TOK_DEV // 2) - 1).astype(jnp.int32)
    w_query = draw_w_query(jax.random.fold_in(seeds[10], 71), 0)
    w_key = draw_w_key(jax.random.fold_in(seeds[10], 71), 0)
    w_value = centred(seeds[5], (N_PIPE, D, HD), D ** -0.5, 0.09375, ((0, 2), (1, 16)))
    w_out = centred(seeds[6], (N_PIPE, QH * HD, D), (QH * HD) ** -0.5, 0.25, ((0, 2),))
    query_gain = jnp.clip(1.0 + 1.5 * jax.random.uniform(seeds[7], (N_PIPE, HD), jnp.float32) ** level_of(seeds[7], (N_PIPE, HD), ((0, 2),), -0.2, 0.2), 1.0, 2.5)
    key_gain = jnp.clip(1.0 + 1.0 * jax.random.uniform(seeds[8], (N_PIPE, HD), jnp.float32) ** level_of(seeds[8], (N_PIPE, HD), ((0, 2),), -0.2, 0.2), 1.0, 2.0)
    cross_gate = jnp.clip(0.3 + 0.90000004 * jax.random.uniform(seeds[9], (N_PIPE,), jnp.float32) ** level_of(seeds[9], (N_PIPE,), ((0, 2),), -0.2, 0.2), 0.3, 1.2)
    return dict(text_states=text_states, image_states=image_states, image_start=image_start, w_query=w_query, w_key=w_key, w_value=w_value, w_out=w_out, query_gain=query_gain, key_gain=key_gain, cross_gate=cross_gate)


epsilon = 1e-06

def normalized(projected, scales):
    mean_square = lax.optimization_barrier(jnp.mean(projected * projected, axis=-1, keepdims=True))
    return projected * lax.rsqrt(mean_square + epsilon) * scales

def reference(text_states, image_states, image_start, w_query, w_key, w_value, w_out, query_gain, key_gain, cross_gate):
    positions = jnp.arange(TOK_DEV, dtype=jnp.int32)
    results = []
    for batch_index in range(MICRO):
        current = text_states[batch_index]
        pictures = image_states[batch_index]
        starts = image_start[batch_index].astype(jnp.int32)
        seen = (positions[None, :] >= starts[:, None]).astype(jnp.float32).reshape(TOKENS, 1)
        for layer_index in range(batch_index, N_PIPE):
            key_sums = jnp.dot(pictures, w_key[layer_index], preferred_element_type=jnp.float32)
            key_rows = normalized(key_sums, key_gain[layer_index]).astype(jnp.bfloat16).reshape(N_DP, IMG_GROUP, HD)
            value_rows = jnp.dot(pictures, w_value[layer_index], preferred_element_type=jnp.float32)
            value_rows = value_rows.astype(jnp.bfloat16).reshape(N_DP, IMG_GROUP, HD)
            query_sums = jnp.dot(current, w_query[layer_index], preferred_element_type=jnp.float32)
            query_sums = query_sums.reshape(N_DP, TOK_DEV, QH, HD)
            queries = normalized(query_sums, query_gain[layer_index]).astype(jnp.bfloat16)
            scores = jnp.einsum('gthc,gic->gthi', queries.astype(jnp.float32), key_rows.astype(jnp.float32)) / math.sqrt(HD)
            exponent = jnp.exp(scores)
            probs = (exponent / lax.optimization_barrier(jnp.sum(exponent, axis=-1, keepdims=True))).astype(jnp.bfloat16)
            attended = jnp.einsum('gthi,gic->gthc', probs.astype(jnp.float32), value_rows.astype(jnp.float32))
            attended = attended.astype(jnp.bfloat16).reshape(TOKENS, QH * HD)
            update = jnp.dot(attended, w_out[layer_index], preferred_element_type=jnp.float32)
            current = (current.astype(jnp.float32) + jnp.tanh(cross_gate[layer_index]) * seen * update).astype(jnp.bfloat16)
        results.append(current)
    return jnp.stack(results)
```

```python
import functools
import math

import jax
import jax.numpy as jnp
from jax import lax
from jax.experimental import pallas as pl
from jax.experimental.pallas import tpu as pltpu
from jax.sharding import PartitionSpec as P

epsilon = 1e-06
MESH = pl.DeviceIdType.MESH
QUAD = 4
PIECES = 4


def shifted(block, axis, distance):
    devices = range(lax.axis_size(axis))
    route = [((i - distance) % len(devices), i) for i in devices]
    return lax.ppermute(block, axis, route)


def normalized(projected, scales):
    mean_square = jnp.mean(projected * projected, axis=-1, keepdims=True)
    return projected * lax.rsqrt(mean_square + epsilon) * scales


def keep_state(current, holding):
    return current


def local(
    text_states,
    image_states,
    image_start,
    w_query,
    w_key,
    w_value,
    w_out,
    query_gain,
    key_gain,
    cross_gate,
):
    sections = lax.axis_size("pipe")
    section_index = lax.axis_index("pipe")
    pictures = lax.all_gather(image_states, "pipe", axis=1, tiled=True)
    batches, image_rows, width = pictures.shape
    flattened = pictures.reshape(batches * image_rows, width)
    head_size = w_key.shape[2]
    head_count = w_query.shape[2] // head_size
    key_full, value_full = (
        lax.all_gather(w_key, "dp", axis=1, tiled=True),
        lax.all_gather(w_value, "dp", axis=1, tiled=True),
    )
    key_sums = jnp.dot(flattened, key_full[0], preferred_element_type=jnp.float32)
    value_sums = jnp.dot(flattened, value_full[0], preferred_element_type=jnp.float32)
    key_rows = (
        normalized(key_sums, key_gain[0])
        .astype(jnp.bfloat16)
        .reshape(batches, image_rows, head_size)
    )
    value_rows = value_sums.astype(jnp.bfloat16).reshape(batches, image_rows, head_size)
    query_weight = w_query[0]
    out_weight = w_out[0]
    factor = jnp.tanh(cross_gate[0])
    tok_rows = text_states.shape[1]
    positions = jnp.arange(tok_rows, dtype=jnp.int32)
    root_size = math.sqrt(head_size)

    def apply_layer(current, holding):
        own_keys = lax.dynamic_index_in_dim(key_rows, holding, 0, keepdims=False)
        own_values = lax.dynamic_index_in_dim(value_rows, holding, 0, keepdims=False)
        query_sums = jnp.dot(current, query_weight, preferred_element_type=jnp.float32)
        query_sums = query_sums.reshape(tok_rows * head_count, head_size)
        queries = normalized(query_sums, query_gain[0]).astype(jnp.bfloat16)
        scores = jnp.dot(queries, own_keys.T, preferred_element_type=jnp.float32) / root_size
        exponent = jnp.exp(scores)
        probs = (exponent / jnp.sum(exponent, axis=-1, keepdims=True)).astype(jnp.bfloat16)
        attended = jnp.dot(probs, own_values, preferred_element_type=jnp.float32).astype(
            jnp.bfloat16
        )
        attended = attended.reshape(tok_rows, head_count * head_size)
        update = jnp.dot(attended, out_weight, preferred_element_type=jnp.float32)
        first_seen = lax.dynamic_index_in_dim(image_start[:, 0], holding, 0, keepdims=False)
        seen = (positions >= first_seen).astype(jnp.float32)[:, None]
        return (current.astype(jnp.float32) + factor * seen * update).astype(jnp.bfloat16)

    current = text_states[0]
    for moment in range(sections):
        holding = jnp.mod(section_index - moment, sections)
        current = lax.cond(moment <= section_index, apply_layer, keep_state, current, holding)
        current = shifted(current, "pipe", 1)
    return current[None]


def kernel(
    lines,
    text_ref,
    image_ref,
    start_ref,
    wq_ref,
    wk_ref,
    wv_ref,
    wo_ref,
    qg_ref,
    kg_ref,
    gate_ref,
    out_ref,
    text_v,
    wq_v,
    wo_v,
    wkv,
    img,
    part,
    part_out,
    part_in,
    query_v,
    small,
    load_sem,
    w_send,
    w_recv,
    i_send,
    i_recv,
    relay_send,
    relay_recv,
    big_send,
    big_recv,
    small_send,
    small_recv,
    p_send,
    p_recv,
):
    place = lax.axis_index("dp")
    core = lax.axis_index("pipe")
    other = 1 - core
    line = place // QUAD
    spot = place % QUAD
    depth = wk_ref.shape[1]
    head = wk_ref.shape[2]
    tokens, width = text_v.shape
    heads = wq_ref.shape[2] // head
    image_rows = image_ref.shape[1]
    span = QUAD * depth

    def quad_peer(distance):
        return line * QUAD + (spot + distance) % QUAD

    def line_peer(distance):
        return ((line + distance) % lines) * QUAD + spot

    def rows_of(index):
        return pl.ds(pl.multiple_of(index * depth, depth), depth)

    loads = [
        pltpu.make_async_copy(wk_ref.at[0], wkv.at[0, rows_of(spot), pl.ds(0, head)], load_sem.at[0]),
        pltpu.make_async_copy(wv_ref.at[0], wkv.at[0, rows_of(spot), pl.ds(head, head)], load_sem.at[1]),
        pltpu.make_async_copy(
            image_ref.at[core, :, pl.ds(pl.multiple_of(line * span, span), span)],
            img.at[line, pl.ds(pl.multiple_of(core * image_rows, image_rows), image_rows)],
            load_sem.at[2],
        ),
        pltpu.make_async_copy(text_ref.at[0], text_v, load_sem.at[3]),
        pltpu.make_async_copy(wq_ref.at[0], wq_v.at[0], load_sem.at[4]),
        pltpu.make_async_copy(wo_ref.at[0], wo_v.at[0], load_sem.at[5]),
    ]
    for load in loads:
        load.start()

    barrier = pltpu.get_barrier_semaphore()
    peers = [(quad_peer(d), core) for d in range(1, QUAD)]
    peers += [(line_peer(d), side) for d in range(1, lines) for side in (core, other)]
    peers += [(place, other)]
    for peer in peers:
        pl.semaphore_signal(barrier, inc=1, device_id=peer, device_id_type=MESH)
    pl.semaphore_wait(barrier, len(peers))

    image_copies = []
    for distance in range(lines):
        target = (line + distance) % lines
        columns = pl.ds(pl.multiple_of(target * span, span), span)
        for turn in range(2):
            if distance == 0 and turn == 0:
                continue
            side = core if turn == 0 else other
            copy = pltpu.make_async_remote_copy(
                src_ref=image_ref.at[side, :, columns],
                dst_ref=img.at[line, pl.ds(pl.multiple_of(core * image_rows, image_rows), image_rows)],
                send_sem=i_send.at[distance, turn],
                recv_sem=i_recv.at[distance, turn],
                device_id=(line_peer(distance), side),
                device_id_type=MESH,
            )
            copy.start()
            image_copies.append(copy)

    weight_copies = []
    for distance in range(1, QUAD):
        for which, ref in enumerate((wk_ref, wv_ref)):
            copy = pltpu.make_async_remote_copy(
                src_ref=ref.at[0],
                dst_ref=wkv.at[0, rows_of(spot), pl.ds(which * head, head)],
                send_sem=w_send.at[distance, which],
                recv_sem=w_recv.at[distance, which],
                device_id=(quad_peer(distance), core),
                device_id_type=MESH,
            )
            copy.start()
            weight_copies.append(copy)

    def across(src, dst, send, recv):
        return pltpu.make_async_remote_copy(
            src_ref=src,
            dst_ref=dst,
            send_sem=send,
            recv_sem=recv,
            device_id=(place, other),
            device_id_type=MESH,
        )

    query_rows = width // PIECES
    out_rows = wo_ref.shape[1] // PIECES
    query_pieces = [
        across(
            wq_ref.at[0, pl.ds(i * query_rows, query_rows)],
            wq_v.at[1, pl.ds(i * query_rows, query_rows)],
            big_send.at[0, i],
            big_recv.at[0, i],
        )
        for i in range(PIECES)
    ]
    out_pieces = [
        across(
            wo_ref.at[0, pl.ds(i * out_rows, out_rows)],
            wo_v.at[1, pl.ds(i * out_rows, out_rows)],
            big_send.at[1, i],
            big_recv.at[1, i],
        )
        for i in range(PIECES)
    ]
    small_copy = across(small.at[0], small.at[1], small_send, small_recv)

    def relay(distance):
        rows = rows_of((spot + QUAD - distance) % QUAD)
        return across(wkv.at[0, rows], wkv.at[1, rows], relay_send.at[distance], relay_recv.at[distance])

    small[0, 0:1] = qg_ref[...]
    small[0, 1:2] = kg_ref[...]
    small[0, 2:3] = jnp.full((1, head), gate_ref[0], jnp.float32)

    loads[0].wait()
    loads[1].wait()

    @pl.when(core == 1)
    def _():
        small_copy.start()
        relay(0).start()
        for piece in query_pieces:
            piece.start()
        for distance in range(1, QUAD):
            weight_copies[2 * distance - 2].wait_recv()
            weight_copies[2 * distance - 1].wait_recv()
            relay(distance).start()
        for piece in out_pieces:
            piece.start()

    chunk = 512

    def project(source, slot):
        steps = width // chunk

        def step(i, total):
            at = pl.ds(pl.multiple_of(i * chunk, chunk), chunk)
            return total + jnp.dot(source[:, at], wq_v[slot, at, :], preferred_element_type=jnp.float32)

        sums = lax.fori_loop(0, steps, step, jnp.zeros((tokens, heads * head), jnp.float32))
        for h in range(heads):
            query_v[h * tokens : (h + 1) * tokens, :] = normalized(
                sums[:, h * head : (h + 1) * head], small[slot, 0:1]
            ).astype(jnp.bfloat16)

    loads[3].wait()
    loads[4].wait()
    project(text_v, 0)

    loads[2].wait()
    for copy in image_copies:
        copy.wait_recv()

    def partial_sums(slot):
        groups = 2 * image_rows
        sums = jnp.dot(
            img[...].reshape(lines * groups, span), wkv[slot], preferred_element_type=jnp.float32
        )
        sums = sums.reshape(lines, groups, 2 * head)
        part[:, slot] = sums
        part_out[:, slot] = sums.astype(jnp.bfloat16)

    def partial_copy(slot, distance):
        return pltpu.make_async_remote_copy(
            src_ref=part_out.at[(line + distance) % lines, slot],
            dst_ref=part_in.at[line, slot],
            send_sem=p_send.at[slot, distance],
            recv_sem=p_recv.at[slot, distance],
            device_id=(line_peer(distance), core),
            device_id_type=MESH,
        )

    @pl.when(core == 0)
    def _():
        for copy in weight_copies:
            copy.wait_recv()

    partial_sums(0)
    for distance in range(1, lines):
        partial_copy(0, distance).start()

    @pl.when(core == 0)
    def _():
        for distance in range(QUAD):
            relay(distance).wait_recv()
        partial_sums(1)
        for distance in range(1, lines):
            partial_copy(1, distance).start()

    positions = lax.broadcasted_iota(jnp.int32, (tokens, chunk), 0)
    seen = (positions >= start_ref[core, 0]).astype(jnp.float32)
    root_size = math.sqrt(head)

    def attend(source, slot, ready):
        total = part[line, slot]
        for distance in range(1, lines):
            partial_copy(slot, distance).wait_recv()
            total += part_in[(line + lines - distance) % lines, slot].astype(jnp.float32)
        keys = normalized(total[:, :head], small[slot, 1:2]).astype(jnp.bfloat16)
        values = total[:, head:].astype(jnp.bfloat16)
        scores = (
            lax.dot_general(
                query_v[...], keys, (((1,), (1,)), ((), ())), preferred_element_type=jnp.float32
            )
            / root_size
        )
        exponent = jnp.exp(scores)
        probs = (exponent / jnp.sum(exponent, axis=-1, keepdims=True)).astype(jnp.bfloat16)
        attended = jnp.dot(probs, values, preferred_element_type=jnp.float32).astype(jnp.bfloat16)
        attended = jnp.concatenate(
            [attended[h * tokens : (h + 1) * tokens] for h in range(heads)], axis=1
        )
        factor = jnp.tanh(small[slot, 2:3])[:, 0:1] * seen
        ready()

        def step(i, carry):
            at = pl.ds(pl.multiple_of(i * chunk, chunk), chunk)
            update = jnp.dot(attended, wo_v[slot, :, at], preferred_element_type=jnp.float32)
            out_ref[0, :, at] = (source(at).astype(jnp.float32) + factor * update).astype(jnp.bfloat16)
            return carry

        lax.fori_loop(0, width // chunk, step, 0)

    attend(lambda at: text_v[:, at], 0, loads[5].wait)

    @pl.when(core == 0)
    def _():
        small_copy.wait_recv()
        for piece in query_pieces:
            piece.wait_recv()
        project(out_ref.at[0], 1)

        def ready():
            for piece in out_pieces:
                piece.wait_recv()

        attend(lambda at: out_ref[0, :, at], 1, ready)

    for copy in image_copies + weight_copies:
        copy.wait_send()
    for distance in range(1, lines):
        partial_copy(0, distance).wait_send()

    @pl.when(core == 0)
    def _():
        for distance in range(1, lines):
            partial_copy(1, distance).wait_send()

    @pl.when(core == 1)
    def _():
        small_copy.wait_send()
        for distance in range(QUAD):
            relay(distance).wait_send()
        for piece in query_pieces + out_pieces:
            piece.wait_send()


def local_fused(
    text_states,
    image_states,
    image_start,
    w_query,
    w_key,
    w_value,
    w_out,
    query_gain,
    key_gain,
    cross_gate,
):
    lines = lax.axis_size("dp") // QUAD
    tokens, width = text_states.shape[1:]
    image_rows = image_states.shape[1]
    depth, head = w_key.shape[1:]
    columns = w_query.shape[2]
    heads = columns // head
    span = QUAD * depth
    groups = 2 * image_rows
    anywhere = pl.BlockSpec(memory_space=pl.ANY)
    vmem = pl.BlockSpec(memory_space=pltpu.VMEM)
    smem = pl.BlockSpec(memory_space=pltpu.SMEM)
    dma = pltpu.SemaphoreType.DMA
    return pl.pallas_call(
        functools.partial(kernel, lines),
        out_shape=jax.ShapeDtypeStruct((1, tokens, width), jnp.bfloat16),
        in_specs=[anywhere, anywhere, smem, anywhere, anywhere, anywhere, anywhere, vmem, vmem, smem],
        out_specs=vmem,
        scratch_shapes=[
            pltpu.VMEM((tokens, width), jnp.bfloat16),
            pltpu.VMEM((2, width, columns), jnp.bfloat16),
            pltpu.VMEM((2, columns, width), jnp.bfloat16),
            pltpu.VMEM((2, span, 2 * head), jnp.bfloat16),
            pltpu.VMEM((lines, groups, span), jnp.bfloat16),
            pltpu.VMEM((lines, 2, groups, 2 * head), jnp.float32),
            pltpu.VMEM((lines, 2, groups, 2 * head), jnp.bfloat16),
            pltpu.VMEM((lines, 2, groups, 2 * head), jnp.bfloat16),
            pltpu.VMEM((heads * tokens, head), jnp.bfloat16),
            pltpu.VMEM((2, 8, head), jnp.float32),
            dma((6,)),
            dma((QUAD, 2)),
            dma((QUAD, 2)),
            dma((lines, 2)),
            dma((lines, 2)),
            dma((QUAD,)),
            dma((QUAD,)),
            dma((2, PIECES)),
            dma((2, PIECES)),
            dma,
            dma,
            dma((2, lines)),
            dma((2, lines)),
        ],
        compiler_params=pltpu.CompilerParams(
            collective_id=0, has_side_effects=True, vmem_limit_bytes=48 * 2**20
        ),
    )(
        text_states,
        image_states,
        image_start,
        w_query,
        w_key,
        w_value,
        w_out,
        query_gain,
        key_gain,
        cross_gate,
    )


def solution(mesh):
    placed = (
        P("pipe", "dp", None),
        P(None, ("dp", "pipe"), None),
        P(None, "dp"),
        P("pipe", None, None),
        P("pipe", "dp", None),
        P("pipe", "dp", None),
        P("pipe", None, None),
        P("pipe", None),
        P("pipe", None),
        P("pipe"),
    )
    fits = mesh.shape["pipe"] == 2 and mesh.shape["dp"] == QUAD * QUAD
    return jax.shard_map(
        local_fused if fits else local,
        mesh=mesh,
        in_specs=placed,
        out_specs=P("pipe", "dp", None),
        check_vma=False,
    )
```

```python
import functools
import math

import jax
import jax.numpy as jnp
from jax import lax
from jax.experimental import pallas as pl
from jax.experimental.pallas import tpu as pltpu
from jax.sharding import PartitionSpec as P

epsilon = 1e-06
MESH = pl.DeviceIdType.MESH
QUAD = 4
PIECES = 4


def shifted(block, axis, distance):
    devices = range(lax.axis_size(axis))
    route = [((i - distance) % len(devices), i) for i in devices]
    return lax.ppermute(block, axis, route)


def normalized(projected, scales):
    mean_square = jnp.mean(projected * projected, axis=-1, keepdims=True)
    return projected * lax.rsqrt(mean_square + epsilon) * scales


def keep_state(current, holding):
    return current


def local(
    text_states,
    image_states,
    image_start,
    w_query,
    w_key,
    w_value,
    w_out,
    query_gain,
    key_gain,
    cross_gate,
):
    sections = lax.axis_size("pipe")
    section_index = lax.axis_index("pipe")
    pictures = lax.all_gather(image_states, "pipe", axis=1, tiled=True)
    batches, image_rows, width = pictures.shape
    flattened = pictures.reshape(batches * image_rows, width)
    head_size = w_key.shape[2]
    head_count = w_query.shape[2] // head_size
    key_full, value_full = (
        lax.all_gather(w_key, "dp", axis=1, tiled=True),
        lax.all_gather(w_value, "dp", axis=1, tiled=True),
    )
    key_sums = jnp.dot(flattened, key_full[0], preferred_element_type=jnp.float32)
    value_sums = jnp.dot(flattened, value_full[0], preferred_element_type=jnp.float32)
    key_rows = (
        normalized(key_sums, key_gain[0])
        .astype(jnp.bfloat16)
        .reshape(batches, image_rows, head_size)
    )
    value_rows = value_sums.astype(jnp.bfloat16).reshape(batches, image_rows, head_size)
    query_weight = w_query[0]
    out_weight = w_out[0]
    factor = jnp.tanh(cross_gate[0])
    tok_rows = text_states.shape[1]
    positions = jnp.arange(tok_rows, dtype=jnp.int32)
    root_size = math.sqrt(head_size)

    def apply_layer(current, holding):
        own_keys = lax.dynamic_index_in_dim(key_rows, holding, 0, keepdims=False)
        own_values = lax.dynamic_index_in_dim(value_rows, holding, 0, keepdims=False)
        query_sums = jnp.dot(current, query_weight, preferred_element_type=jnp.float32)
        query_sums = query_sums.reshape(tok_rows * head_count, head_size)
        queries = normalized(query_sums, query_gain[0]).astype(jnp.bfloat16)
        scores = jnp.dot(queries, own_keys.T, preferred_element_type=jnp.float32) / root_size
        exponent = jnp.exp(scores)
        probs = (exponent / jnp.sum(exponent, axis=-1, keepdims=True)).astype(jnp.bfloat16)
        attended = jnp.dot(probs, own_values, preferred_element_type=jnp.float32).astype(
            jnp.bfloat16
        )
        attended = attended.reshape(tok_rows, head_count * head_size)
        update = jnp.dot(attended, out_weight, preferred_element_type=jnp.float32)
        first_seen = lax.dynamic_index_in_dim(image_start[:, 0], holding, 0, keepdims=False)
        seen = (positions >= first_seen).astype(jnp.float32)[:, None]
        return (current.astype(jnp.float32) + factor * seen * update).astype(jnp.bfloat16)

    current = text_states[0]
    for moment in range(sections):
        holding = jnp.mod(section_index - moment, sections)
        current = lax.cond(moment <= section_index, apply_layer, keep_state, current, holding)
        current = shifted(current, "pipe", 1)
    return current[None]


def kernel(
    lines,
    text_ref,
    image_ref,
    start_ref,
    wq_ref,
    wk_ref,
    wv_ref,
    wo_ref,
    qg_ref,
    kg_ref,
    gate_ref,
    out_ref,
    text_v,
    wq_v,
    wo_v,
    wkv,
    img,
    part,
    part_out,
    part_in,
    query_v,
    small,
    query_gain,
    key_gain,
    load_sem,
    w_send,
    w_recv,
    i_send,
    i_recv,
    relay_send,
    relay_recv,
    big_send,
    big_recv,
    small_send,
    small_recv,
    p_send,
    p_recv,
):
    place = lax.axis_index("dp")
    core = lax.axis_index("pipe")
    other = 1 - core
    line = place // QUAD
    spot = place % QUAD
    depth = wk_ref.shape[1]
    head = wk_ref.shape[2]
    tokens, width = text_v.shape
    heads = wq_ref.shape[2] // head
    image_rows = image_ref.shape[1]
    span = QUAD * depth

    def quad_peer(distance):
        return line * QUAD + (spot + distance) % QUAD

    def line_peer(distance):
        return ((line + distance) % lines) * QUAD + spot

    def rows_of(index):
        return pl.ds(pl.multiple_of(index * depth, depth), depth)

    loads = [
        pltpu.make_async_copy(wk_ref.at[0], wkv.at[0, rows_of(spot), pl.ds(0, head)], load_sem.at[0]),
        pltpu.make_async_copy(wv_ref.at[0], wkv.at[0, rows_of(spot), pl.ds(head, head)], load_sem.at[1]),
        pltpu.make_async_copy(
            image_ref.at[core, :, pl.ds(pl.multiple_of(line * span, span), span)],
            img.at[line, pl.ds(pl.multiple_of(core * image_rows, image_rows), image_rows)],
            load_sem.at[2],
        ),
        pltpu.make_async_copy(text_ref.at[0], text_v, load_sem.at[3]),
        pltpu.make_async_copy(wq_ref.at[0], wq_v.at[0], load_sem.at[4]),
        pltpu.make_async_copy(wo_ref.at[0], wo_v.at[0], load_sem.at[5]),
        pltpu.make_async_copy(qg_ref, query_gain, load_sem.at[6]),
        pltpu.make_async_copy(kg_ref, key_gain, load_sem.at[7]),
    ]
    for load in loads:
        load.start()

    barrier = pltpu.get_barrier_semaphore()
    peers = [(quad_peer(d), core) for d in range(1, QUAD)]
    peers += [(line_peer(d), side) for d in range(1, lines) for side in (core, other)]
    peers += [(place, other)]
    for peer in peers:
        pl.semaphore_signal(barrier, inc=1, device_id=peer, device_id_type=MESH)
    pl.semaphore_wait(barrier, len(peers))

    image_copies = []
    for distance in range(lines):
        target = (line + distance) % lines
        columns = pl.ds(pl.multiple_of(target * span, span), span)
        for turn in range(2):
            if distance == 0 and turn == 0:
                continue
            side = core if turn == 0 else other
            copy = pltpu.make_async_remote_copy(
                src_ref=image_ref.at[side, :, columns],
                dst_ref=img.at[line, pl.ds(pl.multiple_of(core * image_rows, image_rows), image_rows)],
                send_sem=i_send.at[distance, turn],
                recv_sem=i_recv.at[distance, turn],
                device_id=(line_peer(distance), side),
                device_id_type=MESH,
            )
            copy.start()
            image_copies.append(copy)

    weight_copies = []
    for distance in range(1, QUAD):
        for which, ref in enumerate((wk_ref, wv_ref)):
            copy = pltpu.make_async_remote_copy(
                src_ref=ref.at[0],
                dst_ref=wkv.at[0, rows_of(spot), pl.ds(which * head, head)],
                send_sem=w_send.at[distance, which],
                recv_sem=w_recv.at[distance, which],
                device_id=(quad_peer(distance), core),
                device_id_type=MESH,
            )
            copy.start()
            weight_copies.append(copy)

    def across(src, dst, send, recv):
        return pltpu.make_async_remote_copy(
            src_ref=src,
            dst_ref=dst,
            send_sem=send,
            recv_sem=recv,
            device_id=(place, other),
            device_id_type=MESH,
        )

    query_rows = width // PIECES
    out_rows = wo_ref.shape[1] // PIECES
    query_pieces = [
        across(
            wq_ref.at[0, pl.ds(i * query_rows, query_rows)],
            wq_v.at[1, pl.ds(i * query_rows, query_rows)],
            big_send.at[0, i],
            big_recv.at[0, i],
        )
        for i in range(PIECES)
    ]
    out_pieces = [
        across(
            wo_ref.at[0, pl.ds(i * out_rows, out_rows)],
            wo_v.at[1, pl.ds(i * out_rows, out_rows)],
            big_send.at[1, i],
            big_recv.at[1, i],
        )
        for i in range(PIECES)
    ]
    small_copy = across(small.at[0], small.at[1], small_send, small_recv)

    def relay(distance):
        rows = rows_of((spot + QUAD - distance) % QUAD)
        return across(wkv.at[0, rows], wkv.at[1, rows], relay_send.at[distance], relay_recv.at[distance])

    loads[6].wait()
    loads[7].wait()
    small[0, 0:1] = query_gain[...]
    small[0, 1:2] = key_gain[...]
    small[0, 2:3] = jnp.full((1, head), gate_ref[0], jnp.float32)

    loads[0].wait()
    loads[1].wait()

    @pl.when(core == 1)
    def _():
        small_copy.start()
        relay(0).start()
        for piece in query_pieces:
            piece.start()
        for distance in range(1, QUAD):
            weight_copies[2 * distance - 2].wait_recv()
            weight_copies[2 * distance - 1].wait_recv()
            relay(distance).start()
        for piece in out_pieces:
            piece.start()

    chunk = 512

    def project(source, slot):
        steps = width // chunk

        def step(i, total):
            at = pl.ds(pl.multiple_of(i * chunk, chunk), chunk)
            return total + jnp.dot(source[:, at], wq_v[slot, at, :], preferred_element_type=jnp.float32)

        sums = lax.fori_loop(0, steps, step, jnp.zeros((tokens, heads * head), jnp.float32))
        for h in range(heads):
            query_v[h * tokens : (h + 1) * tokens, :] = normalized(
                sums[:, h * head : (h + 1) * head], small[slot, 0:1]
            ).astype(jnp.bfloat16)

    loads[3].wait()
    loads[4].wait()
    project(text_v, 0)

    loads[2].wait()
    for copy in image_copies:
        copy.wait_recv()

    def partial_sums(slot):
        groups = 2 * image_rows
        sums = jnp.dot(
            img[...].reshape(lines * groups, span), wkv[slot], preferred_element_type=jnp.float32
        )
        sums = sums.reshape(lines, groups, 2 * head)
        part[:, slot] = sums
        part_out[:, slot] = sums.astype(jnp.bfloat16)

    def partial_copy(slot, distance):
        return pltpu.make_async_remote_copy(
            src_ref=part_out.at[(line + distance) % lines, slot],
            dst_ref=part_in.at[line, slot],
            send_sem=p_send.at[slot, distance],
            recv_sem=p_recv.at[slot, distance],
            device_id=(line_peer(distance), core),
            device_id_type=MESH,
        )

    @pl.when(core == 0)
    def _():
        for copy in weight_copies:
            copy.wait_recv()

    partial_sums(0)
    for distance in range(1, lines):
        partial_copy(0, distance).start()

    @pl.when(core == 0)
    def _():
        for distance in range(QUAD):
            relay(distance).wait_recv()
        partial_sums(1)
        for distance in range(1, lines):
            partial_copy(1, distance).start()

    positions = lax.broadcasted_iota(jnp.int32, (tokens, chunk), 0)
    seen = (positions >= start_ref[core]).astype(jnp.float32)
    root_size = math.sqrt(head)

    def attend(source, slot, ready):
        total = part[line, slot]
        for distance in range(1, lines):
            partial_copy(slot, distance).wait_recv()
            total += part_in[(line + lines - distance) % lines, slot].astype(jnp.float32)
        keys = normalized(total[:, :head], small[slot, 1:2]).astype(jnp.bfloat16)
        values = total[:, head:].astype(jnp.bfloat16)
        scores = (
            lax.dot_general(
                query_v[...], keys, (((1,), (1,)), ((), ())), preferred_element_type=jnp.float32
            )
            / root_size
        )
        exponent = jnp.exp(scores)
        probs = (exponent / jnp.sum(exponent, axis=-1, keepdims=True)).astype(jnp.bfloat16)
        attended = jnp.dot(probs, values, preferred_element_type=jnp.float32).astype(jnp.bfloat16)
        attended = jnp.concatenate(
            [attended[h * tokens : (h + 1) * tokens] for h in range(heads)], axis=1
        )
        factor = jnp.tanh(small[slot, 2:3])[:, 0:1] * seen
        ready()

        def step(i, carry):
            at = pl.ds(pl.multiple_of(i * chunk, chunk), chunk)
            update = jnp.dot(attended, wo_v[slot, :, at], preferred_element_type=jnp.float32)
            out_ref[0, :, at] = (source(at).astype(jnp.float32) + factor * update).astype(jnp.bfloat16)
            return carry

        lax.fori_loop(0, width // chunk, step, 0)

    attend(lambda at: text_v[:, at], 0, loads[5].wait)

    @pl.when(core == 0)
    def _():
        small_copy.wait_recv()
        for piece in query_pieces:
            piece.wait_recv()
        project(out_ref.at[0], 1)

        def ready():
            for piece in out_pieces:
                piece.wait_recv()

        attend(lambda at: out_ref[0, :, at], 1, ready)

    for copy in image_copies + weight_copies:
        copy.wait_send()
    for distance in range(1, lines):
        partial_copy(0, distance).wait_send()

    @pl.when(core == 0)
    def _():
        for distance in range(1, lines):
            partial_copy(1, distance).wait_send()

    @pl.when(core == 1)
    def _():
        small_copy.wait_send()
        for distance in range(QUAD):
            relay(distance).wait_send()
        for piece in query_pieces + out_pieces:
            piece.wait_send()


def local_fused(
    text_states,
    image_states,
    image_start,
    w_query,
    w_key,
    w_value,
    w_out,
    query_gain,
    key_gain,
    cross_gate,
):
    lines = lax.axis_size("dp") // QUAD
    tokens, width = text_states.shape[1:]
    image_rows = image_states.shape[1]
    depth, head = w_key.shape[1:]
    columns = w_query.shape[2]
    heads = columns // head
    span = QUAD * depth
    groups = 2 * image_rows
    hbm = pl.BlockSpec(memory_space=pltpu.HBM)
    vmem = pl.BlockSpec(memory_space=pltpu.VMEM)
    smem = pl.BlockSpec(memory_space=pltpu.SMEM)
    dma = pltpu.SemaphoreType.DMA
    return pl.pallas_call(
        functools.partial(kernel, lines),
        out_shape=jax.ShapeDtypeStruct((1, tokens, width), jnp.bfloat16),
        in_specs=[hbm, hbm, smem, hbm, hbm, hbm, hbm, hbm, hbm, smem],
        out_specs=vmem,
        scratch_shapes=[
            pltpu.VMEM((tokens, width), jnp.bfloat16),
            pltpu.VMEM((2, width, columns), jnp.bfloat16),
            pltpu.VMEM((2, columns, width), jnp.bfloat16),
            pltpu.VMEM((2, span, 2 * head), jnp.bfloat16),
            pltpu.VMEM((lines, groups, span), jnp.bfloat16),
            pltpu.VMEM((lines, 2, groups, 2 * head), jnp.float32),
            pltpu.VMEM((lines, 2, groups, 2 * head), jnp.bfloat16),
            pltpu.VMEM((lines, 2, groups, 2 * head), jnp.bfloat16),
            pltpu.VMEM((heads * tokens, head), jnp.bfloat16),
            pltpu.VMEM((2, 8, head), jnp.float32),
            pltpu.VMEM((1, head), jnp.float32),
            pltpu.VMEM((1, head), jnp.float32),
            dma((8,)),
            dma((QUAD, 2)),
            dma((QUAD, 2)),
            dma((lines, 2)),
            dma((lines, 2)),
            dma((QUAD,)),
            dma((QUAD,)),
            dma((2, PIECES)),
            dma((2, PIECES)),
            dma,
            dma,
            dma((2, lines)),
            dma((2, lines)),
        ],
        compiler_params=pltpu.CompilerParams(
            collective_id=0, has_side_effects=True, vmem_limit_bytes=60 * 2**20
        ),
    )(
        text_states,
        image_states,
        image_start.reshape(-1),
        w_query,
        w_key,
        w_value,
        w_out,
        query_gain,
        key_gain,
        cross_gate,
    )


def solution(mesh):
    placed = (
        P("pipe", "dp", None),
        P(None, ("dp", "pipe"), None),
        P(None, "dp"),
        P("pipe", None, None),
        P("pipe", "dp", None),
        P("pipe", "dp", None),
        P("pipe", None, None),
        P("pipe", None),
        P("pipe", None),
        P("pipe"),
    )
    fits = mesh.shape["pipe"] == 2 and mesh.shape["dp"] == QUAD * QUAD
    return jax.shard_map(
        local_fused if fits else local,
        mesh=mesh,
        in_specs=placed,
        out_specs=P("pipe", "dp", None),
        check_vma=False,
    )
```

```python
import functools
import math

import jax
import jax.numpy as jnp
from jax import lax
from jax.experimental import pallas as pl
from jax.experimental.pallas import tpu as pltpu
from jax.sharding import PartitionSpec as P

epsilon = 1e-06
MESH = pl.DeviceIdType.MESH
QUAD = 4
PIECES = 4


def shifted(block, axis, distance):
    devices = range(lax.axis_size(axis))
    route = [((i - distance) % len(devices), i) for i in devices]
    return lax.ppermute(block, axis, route)


def normalized(projected, scales):
    mean_square = jnp.mean(projected * projected, axis=-1, keepdims=True)
    return projected * lax.rsqrt(mean_square + epsilon) * scales


def keep_state(current, holding):
    return current


def local(
    text_states,
    image_states,
    image_start,
    w_query,
    w_key,
    w_value,
    w_out,
    query_gain,
    key_gain,
    cross_gate,
):
    sections = lax.axis_size("pipe")
    section_index = lax.axis_index("pipe")
    pictures = lax.all_gather(image_states, "pipe", axis=1, tiled=True)
    batches, image_rows, width = pictures.shape
    flattened = pictures.reshape(batches * image_rows, width)
    head_size = w_key.shape[2]
    head_count = w_query.shape[2] // head_size
    key_full, value_full = (
        lax.all_gather(w_key, "dp", axis=1, tiled=True),
        lax.all_gather(w_value, "dp", axis=1, tiled=True),
    )
    key_sums = jnp.dot(flattened, key_full[0], preferred_element_type=jnp.float32)
    value_sums = jnp.dot(flattened, value_full[0], preferred_element_type=jnp.float32)
    key_rows = (
        normalized(key_sums, key_gain[0])
        .astype(jnp.bfloat16)
        .reshape(batches, image_rows, head_size)
    )
    value_rows = value_sums.astype(jnp.bfloat16).reshape(batches, image_rows, head_size)
    query_weight = w_query[0]
    out_weight = w_out[0]
    factor = jnp.tanh(cross_gate[0])
    tok_rows = text_states.shape[1]
    positions = jnp.arange(tok_rows, dtype=jnp.int32)
    root_size = math.sqrt(head_size)

    def apply_layer(current, holding):
        own_keys = lax.dynamic_index_in_dim(key_rows, holding, 0, keepdims=False)
        own_values = lax.dynamic_index_in_dim(value_rows, holding, 0, keepdims=False)
        query_sums = jnp.dot(current, query_weight, preferred_element_type=jnp.float32)
        query_sums = query_sums.reshape(tok_rows * head_count, head_size)
        queries = normalized(query_sums, query_gain[0]).astype(jnp.bfloat16)
        scores = jnp.dot(queries, own_keys.T, preferred_element_type=jnp.float32) / root_size
        exponent = jnp.exp(scores)
        probs = (exponent / jnp.sum(exponent, axis=-1, keepdims=True)).astype(jnp.bfloat16)
        attended = jnp.dot(probs, own_values, preferred_element_type=jnp.float32).astype(
            jnp.bfloat16
        )
        attended = attended.reshape(tok_rows, head_count * head_size)
        update = jnp.dot(attended, out_weight, preferred_element_type=jnp.float32)
        first_seen = lax.dynamic_index_in_dim(image_start[:, 0], holding, 0, keepdims=False)
        seen = (positions >= first_seen).astype(jnp.float32)[:, None]
        return (current.astype(jnp.float32) + factor * seen * update).astype(jnp.bfloat16)

    current = text_states[0]
    for moment in range(sections):
        holding = jnp.mod(section_index - moment, sections)
        current = lax.cond(moment <= section_index, apply_layer, keep_state, current, holding)
        current = shifted(current, "pipe", 1)
    return current[None]


def kernel(
    lines,
    text_ref,
    image_ref,
    start_ref,
    wq_ref,
    wk_ref,
    wv_ref,
    wo_ref,
    qg_ref,
    kg_ref,
    gate_ref,
    out_ref,
    text_v,
    wq_v,
    wo_v,
    joint_sum,
    joint,
    first,
    wkv,
    img,
    part,
    part_out,
    part_in,
    query_v,
    small,
    query_gain,
    key_gain,
    starts,
    load_sem,
    w_send,
    w_recv,
    i_send,
    i_recv,
    relay_send,
    relay_recv,
    big_send,
    big_recv,
    one_send,
    one_recv,
    p_send,
    p_recv,
):
    place = lax.axis_index("dp")
    core = lax.axis_index("pipe")
    other = 1 - core
    line = place // QUAD
    spot = place % QUAD
    depth = wk_ref.shape[1]
    head = wk_ref.shape[2]
    tokens, width = text_v.shape[1:]
    heads = wq_ref.shape[2] // head
    image_rows = image_ref.shape[1]
    span = QUAD * depth

    def quad_peer(distance):
        return line * QUAD + (spot + distance) % QUAD

    def line_peer(distance):
        return ((line + distance) % lines) * QUAD + spot

    def rows_of(index):
        return pl.ds(pl.multiple_of(index * depth, depth), depth)

    loads = [
        pltpu.make_async_copy(wk_ref.at[0], wkv.at[0, rows_of(spot), pl.ds(0, head)], load_sem.at[0]),
        pltpu.make_async_copy(wv_ref.at[0], wkv.at[0, rows_of(spot), pl.ds(head, head)], load_sem.at[1]),
        pltpu.make_async_copy(
            image_ref.at[core, :, pl.ds(pl.multiple_of(line * span, span), span)],
            img.at[line, pl.ds(pl.multiple_of(core * image_rows, image_rows), image_rows)],
            load_sem.at[2],
        ),
        pltpu.make_async_copy(text_ref.at[0], text_v.at[0], load_sem.at[3]),
        pltpu.make_async_copy(wq_ref.at[0], wq_v, load_sem.at[4]),
        pltpu.make_async_copy(wo_ref.at[0], wo_v.at[0], load_sem.at[5]),
        pltpu.make_async_copy(qg_ref, query_gain, load_sem.at[6]),
        pltpu.make_async_copy(kg_ref, key_gain, load_sem.at[7]),
        pltpu.make_async_copy(start_ref, starts, load_sem.at[8]),
    ]
    for load in loads:
        load.start()

    barrier = pltpu.get_barrier_semaphore()
    peers = [(quad_peer(d), core) for d in range(1, QUAD)]
    peers += [(line_peer(d), side) for d in range(1, lines) for side in (core, other)]
    peers += [(place, other)]
    for peer in peers:
        pl.semaphore_signal(barrier, inc=1, device_id=peer, device_id_type=MESH)
    pl.semaphore_wait(barrier, len(peers))

    image_copies = []
    for distance in range(lines):
        target = (line + distance) % lines
        columns = pl.ds(pl.multiple_of(target * span, span), span)
        for turn in range(2):
            if distance == 0 and turn == 0:
                continue
            side = core if turn == 0 else other
            copy = pltpu.make_async_remote_copy(
                src_ref=image_ref.at[side, :, columns],
                dst_ref=img.at[line, pl.ds(pl.multiple_of(core * image_rows, image_rows), image_rows)],
                send_sem=i_send.at[distance, turn],
                recv_sem=i_recv.at[distance, turn],
                device_id=(line_peer(distance), side),
                device_id_type=MESH,
            )
            copy.start()
            image_copies.append(copy)

    weight_copies = []
    for distance in range(1, QUAD):
        for which, ref in enumerate((wk_ref, wv_ref)):
            copy = pltpu.make_async_remote_copy(
                src_ref=ref.at[0],
                dst_ref=wkv.at[0, rows_of(spot), pl.ds(which * head, head)],
                send_sem=w_send.at[distance, which],
                recv_sem=w_recv.at[distance, which],
                device_id=(quad_peer(distance), core),
                device_id_type=MESH,
            )
            copy.start()
            weight_copies.append(copy)

    def across(src, dst, send, recv):
        return pltpu.make_async_remote_copy(
            src_ref=src,
            dst_ref=dst,
            send_sem=send,
            recv_sem=recv,
            device_id=(place, other),
            device_id_type=MESH,
        )

    stretch = width // PIECES
    out_pieces = [
        across(
            wo_ref.at[0, :, pl.ds(i * stretch, stretch)],
            wo_v.at[1, :, pl.ds(i * stretch, stretch)],
            big_send.at[i],
            big_recv.at[i],
        )
        for i in range(PIECES)
    ]
    small_copy = across(small.at[0], small.at[1], one_send.at[0], one_recv.at[0])
    text_copy = across(text_ref.at[0], text_v.at[1], one_send.at[1], one_recv.at[1])
    first_copy = across(first.at[0], first.at[1], one_send.at[2], one_recv.at[2])
    joint_copy = across(joint.at[0], joint.at[1], one_send.at[3], one_recv.at[3])

    def relay(distance):
        rows = rows_of((spot + QUAD - distance) % QUAD)
        return across(wkv.at[0, rows], wkv.at[1, rows], relay_send.at[distance], relay_recv.at[distance])

    loads[6].wait()
    loads[7].wait()
    small[0, 0:1] = query_gain[...]
    small[0, 1:2] = key_gain[...]
    small[0, 2:3] = jnp.full((1, head), gate_ref[0], jnp.float32)

    loads[0].wait()
    loads[1].wait()

    @pl.when(core == 0)
    def _():
        text_copy.start()
        for piece in out_pieces:
            piece.start()

    @pl.when(core == 1)
    def _():
        small_copy.start()
        relay(0).start()
        for piece in out_pieces[: PIECES // 2]:
            piece.start()

    chunk = 512

    def project(slot):
        def step(i, total):
            at = pl.ds(pl.multiple_of(i * chunk, chunk), chunk)
            return total + jnp.dot(text_v[slot, :, at], wq_v[at, :], preferred_element_type=jnp.float32)

        return lax.fori_loop(0, width // chunk, step, jnp.zeros((tokens, heads * head), jnp.float32))

    def store_queries(sums, slot):
        for h in range(heads):
            query_v[h * tokens : (h + 1) * tokens, :] = normalized(
                sums[:, h * head : (h + 1) * head], small[slot, 0:1]
            ).astype(jnp.bfloat16)

    def join(i):
        out_pieces[i].wait_recv()
        at = pl.ds(i * stretch, stretch)
        product = jnp.dot(wo_v[1, :, at], wq_v[at, :], preferred_element_type=jnp.float32)
        joint_sum[...] = product if i == 0 else joint_sum[...] + product

    loads[3].wait()
    loads[4].wait()
    store_queries(project(0), 0)

    @pl.when(core == 1)
    def _():
        for distance in range(1, QUAD):
            weight_copies[2 * distance - 2].wait_recv()
            weight_copies[2 * distance - 1].wait_recv()
            relay(distance).start()
        for piece in out_pieces[PIECES // 2 :]:
            piece.start()
        text_copy.wait_recv()
        first[0] = project(1)
        first_copy.start()
        for i in range(PIECES // 2):
            join(i)

    loads[2].wait()
    for copy in image_copies:
        copy.wait_recv()

    def partial_sums(slot):
        groups = 2 * image_rows
        sums = jnp.dot(
            img[...].reshape(lines * groups, span), wkv[slot], preferred_element_type=jnp.float32
        )
        sums = sums.reshape(lines, groups, 2 * head)
        part[:, slot] = sums
        part_out[:, slot] = sums.astype(jnp.bfloat16)

    def partial_copy(slot, distance):
        return pltpu.make_async_remote_copy(
            src_ref=part_out.at[(line + distance) % lines, slot],
            dst_ref=part_in.at[line, slot],
            send_sem=p_send.at[slot, distance],
            recv_sem=p_recv.at[slot, distance],
            device_id=(line_peer(distance), core),
            device_id_type=MESH,
        )

    @pl.when(core == 0)
    def _():
        for copy in weight_copies:
            copy.wait_recv()

    partial_sums(0)
    for distance in range(1, lines):
        partial_copy(0, distance).start()

    @pl.when(core == 1)
    def _():
        for i in range(PIECES // 2, PIECES):
            join(i)
        joint[0] = joint_sum[...].astype(jnp.bfloat16)
        joint_copy.start()

    @pl.when(core == 0)
    def _():
        for distance in range(QUAD):
            relay(distance).wait_recv()
        partial_sums(1)
        for distance in range(1, lines):
            partial_copy(1, distance).start()

    positions = lax.broadcasted_iota(jnp.int32, (tokens, 1), 0)
    loads[8].wait()
    seen = (positions >= starts[core]).astype(jnp.float32)
    root_size = math.sqrt(head)

    def attend(slot):
        total = part[line, slot]
        for distance in range(1, lines):
            partial_copy(slot, distance).wait_recv()
            total += part_in[(line + lines - distance) % lines, slot].astype(jnp.float32)
        keys = normalized(total[:, :head], small[slot, 1:2]).astype(jnp.bfloat16)
        values = total[:, head:].astype(jnp.bfloat16)
        scores = (
            lax.dot_general(
                query_v[...], keys, (((1,), (1,)), ((), ())), preferred_element_type=jnp.float32
            )
            / root_size
        )
        exponent = jnp.exp(scores)
        probs = (exponent / jnp.sum(exponent, axis=-1, keepdims=True)).astype(jnp.bfloat16)
        attended = jnp.dot(probs, values, preferred_element_type=jnp.float32).astype(jnp.bfloat16)
        attended = jnp.concatenate(
            [attended[h * tokens : (h + 1) * tokens] for h in range(heads)], axis=1
        )
        return attended, jnp.tanh(small[slot, 2:3])[:, 0:1] * seen

    def advance(source, slot, attended, factor):
        def step(i, carry):
            at = pl.ds(pl.multiple_of(i * chunk, chunk), chunk)
            update = jnp.dot(attended, wo_v[slot, :, at], preferred_element_type=jnp.float32)
            out_ref[0, :, at] = (source[:, at].astype(jnp.float32) + factor * update).astype(jnp.bfloat16)
            return carry

        lax.fori_loop(0, width // chunk, step, 0)

    attended, factor = attend(0)
    loads[5].wait()
    advance(text_v.at[0], 0, attended, factor)

    @pl.when(core == 0)
    def _():
        small_copy.wait_recv()
        first_copy.wait_recv()
        joint_copy.wait_recv()
        change = jnp.dot(attended, joint[1], preferred_element_type=jnp.float32)
        store_queries(first[1] + factor * change, 1)
        later, later_factor = attend(1)
        for piece in out_pieces:
            piece.wait_recv()
        advance(out_ref.at[0], 1, later, later_factor)

    for copy in image_copies + weight_copies:
        copy.wait_send()
    for distance in range(1, lines):
        partial_copy(0, distance).wait_send()

    for piece in out_pieces:
        piece.wait_send()

    @pl.when(core == 0)
    def _():
        for distance in range(1, lines):
            partial_copy(1, distance).wait_send()
        text_copy.wait_send()

    @pl.when(core == 1)
    def _():
        for distance in range(QUAD):
            relay(distance).wait_send()
        for copy in (small_copy, first_copy, joint_copy):
            copy.wait_send()


def local_fused(
    text_states,
    image_states,
    image_start,
    w_query,
    w_key,
    w_value,
    w_out,
    query_gain,
    key_gain,
    cross_gate,
):
    lines = lax.axis_size("dp") // QUAD
    tokens, width = text_states.shape[1:]
    image_rows = image_states.shape[1]
    depth, head = w_key.shape[1:]
    columns = w_query.shape[2]
    heads = columns // head
    span = QUAD * depth
    groups = 2 * image_rows
    hbm = pl.BlockSpec(memory_space=pltpu.HBM)
    vmem = pl.BlockSpec(memory_space=pltpu.VMEM)
    smem = pl.BlockSpec(memory_space=pltpu.SMEM)
    dma = pltpu.SemaphoreType.DMA
    return pl.pallas_call(
        functools.partial(kernel, lines),
        out_shape=jax.ShapeDtypeStruct((1, tokens, width), jnp.bfloat16),
        in_specs=[hbm, hbm, hbm, hbm, hbm, hbm, hbm, hbm, hbm, smem],
        out_specs=vmem,
        scratch_shapes=[
            pltpu.VMEM((2, tokens, width), jnp.bfloat16),
            pltpu.VMEM((width, columns), jnp.bfloat16),
            pltpu.VMEM((2, columns, width), jnp.bfloat16),
            pltpu.VMEM((columns, columns), jnp.float32),
            pltpu.VMEM((2, columns, columns), jnp.bfloat16),
            pltpu.VMEM((2, tokens, columns), jnp.float32),
            pltpu.VMEM((2, span, 2 * head), jnp.bfloat16),
            pltpu.VMEM((lines, groups, span), jnp.bfloat16),
            pltpu.VMEM((lines, 2, groups, 2 * head), jnp.float32),
            pltpu.VMEM((lines, 2, groups, 2 * head), jnp.bfloat16),
            pltpu.VMEM((lines, 2, groups, 2 * head), jnp.bfloat16),
            pltpu.VMEM((heads * tokens, head), jnp.bfloat16),
            pltpu.VMEM((2, 8, head), jnp.float32),
            pltpu.VMEM((1, head), jnp.float32),
            pltpu.VMEM((1, head), jnp.float32),
            pltpu.SMEM(image_start.shape[:1], jnp.int32),
            dma((9,)),
            dma((QUAD, 2)),
            dma((QUAD, 2)),
            dma((lines, 2)),
            dma((lines, 2)),
            dma((QUAD,)),
            dma((QUAD,)),
            dma((PIECES,)),
            dma((PIECES,)),
            dma((4,)),
            dma((4,)),
            dma((2, lines)),
            dma((2, lines)),
        ],
        compiler_params=pltpu.CompilerParams(
            collective_id=0, has_side_effects=True, vmem_limit_bytes=48 * 2**20
        ),
    )(
        pltpu.with_memory_space_constraint(text_states, pltpu.HBM),
        pltpu.with_memory_space_constraint(image_states, pltpu.HBM),
        pltpu.with_memory_space_constraint(image_start.reshape(-1), pltpu.HBM),
        pltpu.with_memory_space_constraint(w_query, pltpu.HBM),
        pltpu.with_memory_space_constraint(w_key, pltpu.HBM),
        pltpu.with_memory_space_constraint(w_value, pltpu.HBM),
        pltpu.with_memory_space_constraint(w_out, pltpu.HBM),
        pltpu.with_memory_space_constraint(query_gain, pltpu.HBM),
        pltpu.with_memory_space_constraint(key_gain, pltpu.HBM),
        cross_gate,
    )


def solution(mesh):
    placed = (
        P("pipe", "dp", None),
        P(None, ("dp", "pipe"), None),
        P(None, "dp"),
        P("pipe", None, None),
        P("pipe", "dp", None),
        P("pipe", "dp", None),
        P("pipe", None, None),
        P("pipe", None),
        P("pipe", None),
        P("pipe"),
    )
    fits = mesh.shape["pipe"] == 2 and mesh.shape["dp"] == QUAD * QUAD
    return jax.shard_map(
        local_fused if fits else local,
        mesh=mesh,
        in_specs=placed,
        out_specs=P("pipe", "dp", None),
        check_vma=False,
    )
```

```python
import functools
import math

import jax
import jax.numpy as jnp
from jax import lax
from jax.experimental import pallas as pl
from jax.experimental.pallas import tpu as pltpu
from jax.sharding import PartitionSpec as P

epsilon = 1e-06
MESH = pl.DeviceIdType.MESH
QUAD = 4
PIECES = 4


def shifted(block, axis, distance):
    devices = range(lax.axis_size(axis))
    route = [((i - distance) % len(devices), i) for i in devices]
    return lax.ppermute(block, axis, route)


def normalized(projected, scales):
    mean_square = jnp.mean(projected * projected, axis=-1, keepdims=True)
    return projected * lax.rsqrt(mean_square + epsilon) * scales


def keep_state(current, holding):
    return current


def local(
    text_states,
    image_states,
    image_start,
    w_query,
    w_key,
    w_value,
    w_out,
    query_gain,
    key_gain,
    cross_gate,
):
    sections = lax.axis_size("pipe")
    section_index = lax.axis_index("pipe")
    pictures = lax.all_gather(image_states, "pipe", axis=1, tiled=True)
    batches, image_rows, width = pictures.shape
    flattened = pictures.reshape(batches * image_rows, width)
    head_size = w_key.shape[2]
    head_count = w_query.shape[2] // head_size
    key_full, value_full = (
        lax.all_gather(w_key, "dp", axis=1, tiled=True),
        lax.all_gather(w_value, "dp", axis=1, tiled=True),
    )
    key_sums = jnp.dot(flattened, key_full[0], preferred_element_type=jnp.float32)
    value_sums = jnp.dot(flattened, value_full[0], preferred_element_type=jnp.float32)
    key_rows = (
        normalized(key_sums, key_gain[0])
        .astype(jnp.bfloat16)
        .reshape(batches, image_rows, head_size)
    )
    value_rows = value_sums.astype(jnp.bfloat16).reshape(batches, image_rows, head_size)
    query_weight = w_query[0]
    out_weight = w_out[0]
    factor = jnp.tanh(cross_gate[0])
    tok_rows = text_states.shape[1]
    positions = jnp.arange(tok_rows, dtype=jnp.int32)
    root_size = math.sqrt(head_size)

    def apply_layer(current, holding):
        own_keys = lax.dynamic_index_in_dim(key_rows, holding, 0, keepdims=False)
        own_values = lax.dynamic_index_in_dim(value_rows, holding, 0, keepdims=False)
        query_sums = jnp.dot(current, query_weight, preferred_element_type=jnp.float32)
        query_sums = query_sums.reshape(tok_rows * head_count, head_size)
        queries = normalized(query_sums, query_gain[0]).astype(jnp.bfloat16)
        scores = jnp.dot(queries, own_keys.T, preferred_element_type=jnp.float32) / root_size
        exponent = jnp.exp(scores)
        probs = (exponent / jnp.sum(exponent, axis=-1, keepdims=True)).astype(jnp.bfloat16)
        attended = jnp.dot(probs, own_values, preferred_element_type=jnp.float32).astype(
            jnp.bfloat16
        )
        attended = attended.reshape(tok_rows, head_count * head_size)
        update = jnp.dot(attended, out_weight, preferred_element_type=jnp.float32)
        first_seen = lax.dynamic_index_in_dim(image_start[:, 0], holding, 0, keepdims=False)
        seen = (positions >= first_seen).astype(jnp.float32)[:, None]
        return (current.astype(jnp.float32) + factor * seen * update).astype(jnp.bfloat16)

    current = text_states[0]
    for moment in range(sections):
        holding = jnp.mod(section_index - moment, sections)
        current = lax.cond(moment <= section_index, apply_layer, keep_state, current, holding)
        current = shifted(current, "pipe", 1)
    return current[None]


def kernel(
    lines,
    text_ref,
    image_ref,
    start_ref,
    wq_ref,
    wk_ref,
    wv_ref,
    wo_ref,
    qg_ref,
    kg_ref,
    gate_ref,
    out_ref,
    text_v,
    wq_v,
    wq_half,
    wo_v,
    joint_sum,
    joint,
    first,
    wkv,
    img,
    part,
    part_out,
    part_in,
    query_v,
    small,
    query_gain,
    key_gain,
    starts,
    load_sem,
    w_send,
    w_recv,
    i_send,
    i_recv,
    relay_send,
    relay_recv,
    big_send,
    big_recv,
    one_send,
    one_recv,
    p_send,
    p_recv,
):
    place = lax.axis_index("dp")
    core = lax.axis_index("pipe")
    other = 1 - core
    line = place // QUAD
    spot = place % QUAD
    depth = wk_ref.shape[1]
    head = wk_ref.shape[2]
    tokens, width = text_v.shape[1:]
    heads = wq_ref.shape[2] // head
    image_rows = image_ref.shape[1]
    span = QUAD * depth

    def quad_peer(distance):
        return line * QUAD + (spot + distance) % QUAD

    def line_peer(distance):
        return ((line + distance) % lines) * QUAD + spot

    def rows_of(index):
        return pl.ds(pl.multiple_of(index * depth, depth), depth)

    loads = [
        pltpu.make_async_copy(wk_ref.at[0], wkv.at[0, rows_of(spot), pl.ds(0, head)], load_sem.at[0]),
        pltpu.make_async_copy(wv_ref.at[0], wkv.at[0, rows_of(spot), pl.ds(head, head)], load_sem.at[1]),
        pltpu.make_async_copy(
            image_ref.at[core, :, pl.ds(pl.multiple_of(line * span, span), span)],
            img.at[line, pl.ds(pl.multiple_of(core * image_rows, image_rows), image_rows)],
            load_sem.at[2],
        ),
        pltpu.make_async_copy(text_ref.at[0], text_v.at[0], load_sem.at[3]),
        pltpu.make_async_copy(wq_ref.at[0], wq_v, load_sem.at[4]),
        pltpu.make_async_copy(wo_ref.at[0], wo_v.at[0], load_sem.at[5]),
        pltpu.make_async_copy(qg_ref, query_gain, load_sem.at[6]),
        pltpu.make_async_copy(kg_ref, key_gain, load_sem.at[7]),
        pltpu.make_async_copy(start_ref, starts, load_sem.at[8]),
    ]
    for load in loads:
        load.start()

    barrier = pltpu.get_barrier_semaphore()
    peers = [(quad_peer(d), core) for d in range(1, QUAD)]
    peers += [(line_peer(d), side) for d in range(1, lines) for side in (core, other)]
    peers += [(place, other)]
    for peer in peers:
        pl.semaphore_signal(barrier, inc=1, device_id=peer, device_id_type=MESH)
    pl.semaphore_wait(barrier, len(peers))

    image_copies = []
    for distance in range(lines):
        target = (line + distance) % lines
        columns = pl.ds(pl.multiple_of(target * span, span), span)
        for turn in range(2):
            if distance == 0 and turn == 0:
                continue
            side = core if turn == 0 else other
            copy = pltpu.make_async_remote_copy(
                src_ref=image_ref.at[side, :, columns],
                dst_ref=img.at[line, pl.ds(pl.multiple_of(core * image_rows, image_rows), image_rows)],
                send_sem=i_send.at[distance, turn],
                recv_sem=i_recv.at[distance, turn],
                device_id=(line_peer(distance), side),
                device_id_type=MESH,
            )
            copy.start()
            image_copies.append(copy)

    weight_copies = []
    for distance in range(1, QUAD):
        for which, ref in enumerate((wk_ref, wv_ref)):
            copy = pltpu.make_async_remote_copy(
                src_ref=ref.at[0],
                dst_ref=wkv.at[0, rows_of(spot), pl.ds(which * head, head)],
                send_sem=w_send.at[distance, which],
                recv_sem=w_recv.at[distance, which],
                device_id=(quad_peer(distance), core),
                device_id_type=MESH,
            )
            copy.start()
            weight_copies.append(copy)

    def across(src, dst, send, recv):
        return pltpu.make_async_remote_copy(
            src_ref=src,
            dst_ref=dst,
            send_sem=send,
            recv_sem=recv,
            device_id=(place, other),
            device_id_type=MESH,
        )

    stretch = width // PIECES
    out_pieces = [
        across(
            wo_ref.at[0, :, pl.ds(i * stretch, stretch)],
            wo_v.at[1, :, pl.ds(i * stretch, stretch)],
            big_send.at[0, i],
            big_recv.at[0, i],
        )
        for i in range(PIECES)
    ]
    half = PIECES // 2
    query_pieces = [
        across(
            wq_ref.at[0, pl.ds(i * stretch, stretch)],
            wq_half.at[pl.ds(i * stretch, stretch)],
            big_send.at[1, i],
            big_recv.at[1, i],
        )
        for i in range(half)
    ]
    small_copy = across(small.at[0], small.at[1], one_send.at[0], one_recv.at[0])
    text_copy = across(text_ref.at[0], text_v.at[1], one_send.at[1], one_recv.at[1])
    first_copy = across(first.at[0], first.at[1], one_send.at[2], one_recv.at[2])
    joint_copy = across(joint.at[0], joint.at[1], one_send.at[3], one_recv.at[3])

    def relay(distance):
        rows = rows_of((spot + QUAD - distance) % QUAD)
        return across(wkv.at[0, rows], wkv.at[1, rows], relay_send.at[distance], relay_recv.at[distance])

    loads[6].wait()
    loads[7].wait()
    small[0, 0:1] = query_gain[...]
    small[0, 1:2] = key_gain[...]
    small[0, 2:3] = jnp.full((1, head), gate_ref[0], jnp.float32)

    loads[0].wait()
    loads[1].wait()

    @pl.when(core == 0)
    def _():
        text_copy.start()
        for piece in out_pieces[half:]:
            piece.start()

    @pl.when(core == 1)
    def _():
        small_copy.start()
        relay(0).start()
        for piece in query_pieces:
            piece.start()

    chunk = 512

    def project(slots):
        rows = slots * tokens

        def step(i, total):
            at = pl.ds(pl.multiple_of(i * chunk, chunk), chunk)
            return total + jnp.dot(
                text_v[:slots, :, at].reshape(rows, chunk), wq_v[at, :], preferred_element_type=jnp.float32
            )

        return lax.fori_loop(0, width // chunk, step, jnp.zeros((rows, heads * head), jnp.float32))

    def store_queries(sums, slot):
        for h in range(heads):
            query_v[h * tokens : (h + 1) * tokens, :] = normalized(
                sums[:, h * head : (h + 1) * head], small[slot, 0:1]
            ).astype(jnp.bfloat16)

    def join(i, left, right):
        product = jnp.dot(left, right, preferred_element_type=jnp.float32)
        joint_sum[...] = product if i == 0 else joint_sum[...] + product

    loads[3].wait()
    loads[4].wait()

    @pl.when(core == 0)
    def _():
        store_queries(project(1), 0)
        loads[5].wait()
        for i in range(half):
            query_pieces[i].wait_recv()
            at = pl.ds(i * stretch, stretch)
            join(i, wo_v[0, :, at], wq_half[at, :])

    @pl.when(core == 1)
    def _():
        text_copy.wait_recv()
        sums = project(2)
        store_queries(sums[:tokens], 0)
        first[0] = sums[tokens:]
        first_copy.start()
        for piece in out_pieces[:half]:
            piece.start()
        for i in range(half):
            out_pieces[half + i].wait_recv()
            at = pl.ds((half + i) * stretch, stretch)
            join(i, wo_v[1, :, at], wq_v[at, :])
        joint[0] = joint_sum[...].astype(jnp.bfloat16)
        joint_copy.start()
        for distance in range(1, QUAD):
            weight_copies[2 * distance - 2].wait_recv()
            weight_copies[2 * distance - 1].wait_recv()
            relay(distance).start()
        for piece in out_pieces[half:]:
            piece.start()
        loads[5].wait()

    loads[2].wait()
    for copy in image_copies:
        copy.wait_recv()

    def partial_sums(slot):
        groups = 2 * image_rows
        sums = jnp.dot(
            img[...].reshape(lines * groups, span), wkv[slot], preferred_element_type=jnp.float32
        )
        sums = sums.reshape(lines, groups, 2 * head)
        part[:, slot] = sums
        part_out[:, slot] = sums.astype(jnp.bfloat16)

    def partial_copy(slot, distance):
        return pltpu.make_async_remote_copy(
            src_ref=part_out.at[(line + distance) % lines, slot],
            dst_ref=part_in.at[line, slot],
            send_sem=p_send.at[slot, distance],
            recv_sem=p_recv.at[slot, distance],
            device_id=(line_peer(distance), core),
            device_id_type=MESH,
        )

    @pl.when(core == 0)
    def _():
        for copy in weight_copies:
            copy.wait_recv()

    partial_sums(0)
    for distance in range(1, lines):
        partial_copy(0, distance).start()

    @pl.when(core == 0)
    def _():
        for distance in range(QUAD):
            relay(distance).wait_recv()
        partial_sums(1)
        for distance in range(1, lines):
            partial_copy(1, distance).start()
        small_copy.wait_recv()
        first_copy.wait_recv()
        joint_copy.wait_recv()
        joint[0] = (joint_sum[...] + joint[1].astype(jnp.float32)).astype(jnp.bfloat16)

    positions = lax.broadcasted_iota(jnp.int32, (tokens, 1), 0)
    loads[8].wait()
    seen = (positions >= starts[core]).astype(jnp.float32)
    root_size = math.sqrt(head)

    def attend(slot):
        total = part[line, slot]
        for distance in range(1, lines):
            partial_copy(slot, distance).wait_recv()
            total += part_in[(line + lines - distance) % lines, slot].astype(jnp.float32)
        keys = normalized(total[:, :head], small[slot, 1:2]).astype(jnp.bfloat16)
        values = total[:, head:].astype(jnp.bfloat16)
        scores = (
            lax.dot_general(
                query_v[...], keys, (((1,), (1,)), ((), ())), preferred_element_type=jnp.float32
            )
            / root_size
        )
        exponent = jnp.exp(scores)
        probs = (exponent / jnp.sum(exponent, axis=-1, keepdims=True)).astype(jnp.bfloat16)
        attended = jnp.dot(probs, values, preferred_element_type=jnp.float32).astype(jnp.bfloat16)
        attended = jnp.concatenate(
            [attended[h * tokens : (h + 1) * tokens] for h in range(heads)], axis=1
        )
        return attended, jnp.tanh(small[slot, 2:3])[:, 0:1] * seen

    def advance(source, slot, attended, factor):
        def step(i, carry):
            at = pl.ds(pl.multiple_of(i * chunk, chunk), chunk)
            update = jnp.dot(attended, wo_v[slot, :, at], preferred_element_type=jnp.float32)
            out_ref[0, :, at] = (source[:, at].astype(jnp.float32) + factor * update).astype(jnp.bfloat16)
            return carry

        lax.fori_loop(0, width // chunk, step, 0)

    attended, factor = attend(0)

    @pl.when(core == 0)
    def _():
        change = jnp.dot(attended, joint[0], preferred_element_type=jnp.float32)
        store_queries(first[1] + factor * change, 1)
        later, later_factor = attend(1)
        advance(text_v.at[0], 0, attended, factor)
        for piece in out_pieces:
            piece.wait_recv()
        advance(out_ref.at[0], 1, later, later_factor)

    @pl.when(core == 1)
    def _():
        advance(text_v.at[0], 0, attended, factor)

    for copy in image_copies + weight_copies:
        copy.wait_send()
    for distance in range(1, lines):
        partial_copy(0, distance).wait_send()

    for piece in out_pieces[half:]:
        piece.wait_send()

    @pl.when(core == 0)
    def _():
        for distance in range(1, lines):
            partial_copy(1, distance).wait_send()
        text_copy.wait_send()

    @pl.when(core == 1)
    def _():
        for distance in range(QUAD):
            relay(distance).wait_send()
        for copy in [small_copy, first_copy, joint_copy] + query_pieces + out_pieces[:half]:
            copy.wait_send()


def local_fused(
    text_states,
    image_states,
    image_start,
    w_query,
    w_key,
    w_value,
    w_out,
    query_gain,
    key_gain,
    cross_gate,
):
    lines = lax.axis_size("dp") // QUAD
    tokens, width = text_states.shape[1:]
    image_rows = image_states.shape[1]
    depth, head = w_key.shape[1:]
    columns = w_query.shape[2]
    heads = columns // head
    span = QUAD * depth
    groups = 2 * image_rows
    hbm = pl.BlockSpec(memory_space=pltpu.HBM)
    vmem = pl.BlockSpec(memory_space=pltpu.VMEM)
    smem = pl.BlockSpec(memory_space=pltpu.SMEM)
    dma = pltpu.SemaphoreType.DMA
    return pl.pallas_call(
        functools.partial(kernel, lines),
        out_shape=jax.ShapeDtypeStruct((1, tokens, width), jnp.bfloat16),
        in_specs=[hbm, hbm, hbm, hbm, hbm, hbm, hbm, hbm, hbm, smem],
        out_specs=vmem,
        scratch_shapes=[
            pltpu.VMEM((2, tokens, width), jnp.bfloat16),
            pltpu.VMEM((width, columns), jnp.bfloat16),
            pltpu.VMEM((width // 2, columns), jnp.bfloat16),
            pltpu.VMEM((2, columns, width), jnp.bfloat16),
            pltpu.VMEM((columns, columns), jnp.float32),
            pltpu.VMEM((2, columns, columns), jnp.bfloat16),
            pltpu.VMEM((2, tokens, columns), jnp.float32),
            pltpu.VMEM((2, span, 2 * head), jnp.bfloat16),
            pltpu.VMEM((lines, groups, span), jnp.bfloat16),
            pltpu.VMEM((lines, 2, groups, 2 * head), jnp.float32),
            pltpu.VMEM((lines, 2, groups, 2 * head), jnp.bfloat16),
            pltpu.VMEM((lines, 2, groups, 2 * head), jnp.bfloat16),
            pltpu.VMEM((heads * tokens, head), jnp.bfloat16),
            pltpu.VMEM((2, 8, head), jnp.float32),
            pltpu.VMEM((1, head), jnp.float32),
            pltpu.VMEM((1, head), jnp.float32),
            pltpu.SMEM(image_start.shape[:1], jnp.int32),
            dma((9,)),
            dma((QUAD, 2)),
            dma((QUAD, 2)),
            dma((lines, 2)),
            dma((lines, 2)),
            dma((QUAD,)),
            dma((QUAD,)),
            dma((2, PIECES)),
            dma((2, PIECES)),
            dma((4,)),
            dma((4,)),
            dma((2, lines)),
            dma((2, lines)),
        ],
        compiler_params=pltpu.CompilerParams(
            collective_id=0, has_side_effects=True, vmem_limit_bytes=48 * 2**20
        ),
    )(
        pltpu.with_memory_space_constraint(text_states, pltpu.HBM),
        pltpu.with_memory_space_constraint(image_states, pltpu.HBM),
        pltpu.with_memory_space_constraint(image_start.reshape(-1), pltpu.HBM),
        pltpu.with_memory_space_constraint(w_query, pltpu.HBM),
        pltpu.with_memory_space_constraint(w_key, pltpu.HBM),
        pltpu.with_memory_space_constraint(w_value, pltpu.HBM),
        pltpu.with_memory_space_constraint(w_out, pltpu.HBM),
        pltpu.with_memory_space_constraint(query_gain, pltpu.HBM),
        pltpu.with_memory_space_constraint(key_gain, pltpu.HBM),
        cross_gate,
    )


def solution(mesh):
    placed = (
        P("pipe", "dp", None),
        P(None, ("dp", "pipe"), None),
        P(None, "dp"),
        P("pipe", None, None),
        P("pipe", "dp", None),
        P("pipe", "dp", None),
        P("pipe", None, None),
        P("pipe", None),
        P("pipe", None),
        P("pipe"),
    )
    fits = mesh.shape["pipe"] == 2 and mesh.shape["dp"] == QUAD * QUAD
    return jax.shard_map(
        local_fused if fits else local,
        mesh=mesh,
        in_specs=placed,
        out_specs=P("pipe", "dp", None),
        check_vma=False,
    )
```

```python
import functools
import math

import jax
import jax.numpy as jnp
from jax import lax
from jax.experimental import pallas as pl
from jax.experimental.pallas import tpu as pltpu
from jax.sharding import PartitionSpec as P

epsilon = 1e-06
MESH = pl.DeviceIdType.MESH
QUAD = 4
PIECES = 4


def shifted(block, axis, distance):
    devices = range(lax.axis_size(axis))
    route = [((i - distance) % len(devices), i) for i in devices]
    return lax.ppermute(block, axis, route)


def normalized(projected, scales):
    mean_square = jnp.mean(projected * projected, axis=-1, keepdims=True)
    return projected * lax.rsqrt(mean_square + epsilon) * scales


def keep_state(current, holding):
    return current


def local(
    text_states,
    image_states,
    image_start,
    w_query,
    w_key,
    w_value,
    w_out,
    query_gain,
    key_gain,
    cross_gate,
):
    sections = lax.axis_size("pipe")
    section_index = lax.axis_index("pipe")
    pictures = lax.all_gather(image_states, "pipe", axis=1, tiled=True)
    batches, image_rows, width = pictures.shape
    flattened = pictures.reshape(batches * image_rows, width)
    head_size = w_key.shape[2]
    head_count = w_query.shape[2] // head_size
    key_full, value_full = (
        lax.all_gather(w_key, "dp", axis=1, tiled=True),
        lax.all_gather(w_value, "dp", axis=1, tiled=True),
    )
    key_sums = jnp.dot(flattened, key_full[0], preferred_element_type=jnp.float32)
    value_sums = jnp.dot(flattened, value_full[0], preferred_element_type=jnp.float32)
    key_rows = (
        normalized(key_sums, key_gain[0])
        .astype(jnp.bfloat16)
        .reshape(batches, image_rows, head_size)
    )
    value_rows = value_sums.astype(jnp.bfloat16).reshape(batches, image_rows, head_size)
    query_weight = w_query[0]
    out_weight = w_out[0]
    factor = jnp.tanh(cross_gate[0])
    tok_rows = text_states.shape[1]
    positions = jnp.arange(tok_rows, dtype=jnp.int32)
    root_size = math.sqrt(head_size)

    def apply_layer(current, holding):
        own_keys = lax.dynamic_index_in_dim(key_rows, holding, 0, keepdims=False)
        own_values = lax.dynamic_index_in_dim(value_rows, holding, 0, keepdims=False)
        query_sums = jnp.dot(current, query_weight, preferred_element_type=jnp.float32)
        query_sums = query_sums.reshape(tok_rows * head_count, head_size)
        queries = normalized(query_sums, query_gain[0]).astype(jnp.bfloat16)
        scores = jnp.dot(queries, own_keys.T, preferred_element_type=jnp.float32) / root_size
        exponent = jnp.exp(scores)
        probs = (exponent / jnp.sum(exponent, axis=-1, keepdims=True)).astype(jnp.bfloat16)
        attended = jnp.dot(probs, own_values, preferred_element_type=jnp.float32).astype(
            jnp.bfloat16
        )
        attended = attended.reshape(tok_rows, head_count * head_size)
        update = jnp.dot(attended, out_weight, preferred_element_type=jnp.float32)
        first_seen = lax.dynamic_index_in_dim(image_start[:, 0], holding, 0, keepdims=False)
        seen = (positions >= first_seen).astype(jnp.float32)[:, None]
        return (current.astype(jnp.float32) + factor * seen * update).astype(jnp.bfloat16)

    current = text_states[0]
    for moment in range(sections):
        holding = jnp.mod(section_index - moment, sections)
        current = lax.cond(moment <= section_index, apply_layer, keep_state, current, holding)
        current = shifted(current, "pipe", 1)
    return current[None]


def kernel(
    lines,
    text_ref,
    image_ref,
    start_ref,
    wq_ref,
    wk_ref,
    wv_ref,
    wo_ref,
    qg_ref,
    kg_ref,
    gate_ref,
    out_ref,
    text_v,
    wq_v,
    wq_half,
    wo_v,
    joint_sum,
    joint,
    first,
    mixed,
    back,
    wkv,
    img,
    part,
    part_out,
    part_in,
    query_v,
    small,
    query_gain,
    key_gain,
    starts,
    load_sem,
    w_send,
    w_recv,
    i_send,
    i_recv,
    relay_send,
    relay_recv,
    big_send,
    big_recv,
    one_send,
    one_recv,
    back_send,
    back_recv,
    p_send,
    p_recv,
):
    place = lax.axis_index("dp")
    core = lax.axis_index("pipe")
    other = 1 - core
    line = place // QUAD
    spot = place % QUAD
    depth = wk_ref.shape[1]
    head = wk_ref.shape[2]
    tokens, width = text_v.shape[1:]
    heads = wq_ref.shape[2] // head
    image_rows = image_ref.shape[1]
    span = QUAD * depth

    def quad_peer(distance):
        return line * QUAD + (spot + distance) % QUAD

    def line_peer(distance):
        return ((line + distance) % lines) * QUAD + spot

    def rows_of(index):
        return pl.ds(pl.multiple_of(index * depth, depth), depth)

    loads = [
        pltpu.make_async_copy(wk_ref.at[0], wkv.at[0, rows_of(spot), pl.ds(0, head)], load_sem.at[0]),
        pltpu.make_async_copy(wv_ref.at[0], wkv.at[0, rows_of(spot), pl.ds(head, head)], load_sem.at[1]),
        pltpu.make_async_copy(
            image_ref.at[core, :, pl.ds(pl.multiple_of(line * span, span), span)],
            img.at[line, pl.ds(pl.multiple_of(core * image_rows, image_rows), image_rows)],
            load_sem.at[2],
        ),
        pltpu.make_async_copy(text_ref.at[0], text_v.at[0], load_sem.at[3]),
        pltpu.make_async_copy(wq_ref.at[0], wq_v, load_sem.at[4]),
        pltpu.make_async_copy(wo_ref.at[0], wo_v.at[0], load_sem.at[5]),
        pltpu.make_async_copy(qg_ref, query_gain, load_sem.at[6]),
        pltpu.make_async_copy(kg_ref, key_gain, load_sem.at[7]),
        pltpu.make_async_copy(start_ref, starts, load_sem.at[8]),
    ]
    for load in loads:
        load.start()

    barrier = pltpu.get_barrier_semaphore()
    peers = [(quad_peer(d), core) for d in range(1, QUAD)]
    peers += [(line_peer(d), side) for d in range(1, lines) for side in (core, other)]
    peers += [(place, other)]
    for peer in peers:
        pl.semaphore_signal(barrier, inc=1, device_id=peer, device_id_type=MESH)
    pl.semaphore_wait(barrier, len(peers))

    image_copies = []
    for distance in range(lines):
        target = (line + distance) % lines
        columns = pl.ds(pl.multiple_of(target * span, span), span)
        for turn in range(2):
            if distance == 0 and turn == 0:
                continue
            side = core if turn == 0 else other
            copy = pltpu.make_async_remote_copy(
                src_ref=image_ref.at[side, :, columns],
                dst_ref=img.at[line, pl.ds(pl.multiple_of(core * image_rows, image_rows), image_rows)],
                send_sem=i_send.at[distance, turn],
                recv_sem=i_recv.at[distance, turn],
                device_id=(line_peer(distance), side),
                device_id_type=MESH,
            )
            copy.start()
            image_copies.append(copy)

    weight_copies = []
    for distance in range(1, QUAD):
        for which, ref in enumerate((wk_ref, wv_ref)):
            copy = pltpu.make_async_remote_copy(
                src_ref=ref.at[0],
                dst_ref=wkv.at[0, rows_of(spot), pl.ds(which * head, head)],
                send_sem=w_send.at[distance, which],
                recv_sem=w_recv.at[distance, which],
                device_id=(quad_peer(distance), core),
                device_id_type=MESH,
            )
            copy.start()
            weight_copies.append(copy)

    def across(src, dst, send, recv):
        return pltpu.make_async_remote_copy(
            src_ref=src,
            dst_ref=dst,
            send_sem=send,
            recv_sem=recv,
            device_id=(place, other),
            device_id_type=MESH,
        )

    stretch = width // PIECES
    out_pieces = [
        across(
            wo_ref.at[0, :, pl.ds(i * stretch, stretch)],
            wo_v.at[1, :, pl.ds(i * stretch, stretch)],
            big_send.at[0, i],
            big_recv.at[0, i],
        )
        for i in range(PIECES)
    ]
    half = PIECES // 2
    query_pieces = [
        across(
            wq_ref.at[0, pl.ds(i * stretch, stretch)],
            wq_half.at[pl.ds(i * stretch, stretch)],
            big_send.at[1, i],
            big_recv.at[1, i],
        )
        for i in range(half)
    ]
    small_copy = across(small.at[0], small.at[1], one_send.at[0], one_recv.at[0])
    text_copy = across(text_ref.at[0], text_v.at[1], one_send.at[1], one_recv.at[1])
    first_copy = across(first.at[0], first.at[1], one_send.at[2], one_recv.at[2])
    joint_copy = across(joint.at[0], joint.at[1], one_send.at[3], one_recv.at[3])
    mixed_copies = [across(mixed.at[i], mixed.at[2 + i], one_send.at[4 + i], one_recv.at[4 + i]) for i in range(2)]
    quarter = stretch // 2
    back_copies = [
        across(
            back.at[:, pl.ds(i * quarter, quarter)],
            out_ref.at[0, :, pl.ds((PIECES + i) * quarter, quarter)],
            back_send.at[i],
            back_recv.at[i],
        )
        for i in range(PIECES)
    ]

    def relay(distance):
        rows = rows_of((spot + QUAD - distance) % QUAD)
        return across(wkv.at[0, rows], wkv.at[1, rows], relay_send.at[distance], relay_recv.at[distance])

    loads[6].wait()
    loads[7].wait()
    small[0, 0:1] = query_gain[...]
    small[0, 1:2] = key_gain[...]
    small[0, 2:3] = jnp.full((1, head), gate_ref[0], jnp.float32)

    loads[0].wait()
    loads[1].wait()

    small_copy.start()

    @pl.when(core == 0)
    def _():
        text_copy.start()
        for piece in out_pieces[half:]:
            piece.start()

    @pl.when(core == 1)
    def _():
        relay(0).start()
        for piece in query_pieces:
            piece.start()

    chunk = 512

    def project(slots):
        rows = slots * tokens

        def step(i, total):
            at = pl.ds(pl.multiple_of(i * chunk, chunk), chunk)
            return total + jnp.dot(
                text_v[:slots, :, at].reshape(rows, chunk), wq_v[at, :], preferred_element_type=jnp.float32
            )

        return lax.fori_loop(0, width // chunk, step, jnp.zeros((rows, heads * head), jnp.float32))

    def store_queries(sums, slot):
        for h in range(heads):
            query_v[h * tokens : (h + 1) * tokens, :] = normalized(
                sums[:, h * head : (h + 1) * head], small[slot, 0:1]
            ).astype(jnp.bfloat16)

    def join(i, left, right):
        product = jnp.dot(left, right, preferred_element_type=jnp.float32)
        joint_sum[...] = product if i == 0 else joint_sum[...] + product

    loads[3].wait()
    loads[4].wait()

    def partial_sums(slot):
        groups = 2 * image_rows
        sums = jnp.dot(
            img[...].reshape(lines * groups, span), wkv[slot], preferred_element_type=jnp.float32
        )
        sums = sums.reshape(lines, groups, 2 * head)
        part[:, slot] = sums
        part_out[:, slot] = sums.astype(jnp.bfloat16)

    def partial_copy(slot, distance):
        return pltpu.make_async_remote_copy(
            src_ref=part_out.at[(line + distance) % lines, slot],
            dst_ref=part_in.at[line, slot],
            send_sem=p_send.at[slot, distance],
            recv_sem=p_recv.at[slot, distance],
            device_id=(line_peer(distance), core),
            device_id_type=MESH,
        )

    def arrived():
        loads[2].wait()
        for copy in image_copies:
            copy.wait_recv()

    def return_partials(slot):
        partial_sums(slot)
        for distance in range(1, lines):
            partial_copy(slot, distance).start()

    @pl.when(core == 0)
    def _():
        def join_own(i):
            query_pieces[i].wait_recv()
            at = pl.ds(i * stretch, stretch)
            join(i, wo_v[0, :, at], wq_half[at, :])

        store_queries(project(1), 0)
        loads[5].wait()
        for i in range(half - 1):
            join_own(i)
        for copy in weight_copies:
            copy.wait_recv()
        arrived()
        return_partials(0)
        for distance in range(QUAD):
            relay(distance).wait_recv()
        return_partials(1)
        join_own(half - 1)
        small_copy.wait_recv()
        first_copy.wait_recv()
        joint_copy.wait_recv()
        joint[0] = (joint_sum[...] + joint[1].astype(jnp.float32)).astype(jnp.bfloat16)

    @pl.when(core == 1)
    def _():
        def join_own(i):
            out_pieces[half + i].wait_recv()
            at = pl.ds((half + i) * stretch, stretch)
            join(i, wo_v[1, :, at], wq_v[at, :])

        text_copy.wait_recv()
        sums = project(2)
        store_queries(sums[:tokens], 0)
        first[0] = sums[tokens:]
        first_copy.start()
        for i in range(half - 1):
            join_own(i)
        for distance in range(1, QUAD):
            weight_copies[2 * distance - 2].wait_recv()
            weight_copies[2 * distance - 1].wait_recv()
            relay(distance).start()
        for piece in out_pieces[:half]:
            piece.start()
        arrived()
        return_partials(0)
        join_own(half - 1)
        joint[0] = joint_sum[...].astype(jnp.bfloat16)
        joint_copy.start()
        loads[5].wait()
        small_copy.wait_recv()

    positions = lax.broadcasted_iota(jnp.int32, (tokens, 1), 0)
    loads[8].wait()
    seen = (positions >= starts[core]).astype(jnp.float32)
    seen_other = (positions >= starts[other]).astype(jnp.float32)
    root_size = math.sqrt(head)

    def attend(slot):
        total = part[line, slot]
        for distance in range(1, lines):
            partial_copy(slot, distance).wait_recv()
            total += part_in[(line + lines - distance) % lines, slot].astype(jnp.float32)
        keys = normalized(total[:, :head], small[slot, 1:2]).astype(jnp.bfloat16)
        values = total[:, head:].astype(jnp.bfloat16)
        scores = (
            lax.dot_general(
                query_v[...], keys, (((1,), (1,)), ((), ())), preferred_element_type=jnp.float32
            )
            / root_size
        )
        exponent = jnp.exp(scores)
        probs = (exponent / jnp.sum(exponent, axis=-1, keepdims=True)).astype(jnp.bfloat16)
        attended = jnp.dot(probs, values, preferred_element_type=jnp.float32).astype(jnp.bfloat16)
        attended = jnp.concatenate(
            [attended[h * tokens : (h + 1) * tokens] for h in range(heads)], axis=1
        )
        return attended

    def gate(slot):
        return jnp.tanh(small[slot, 2:3])[:, 0:1]

    def update(values, slot, at):
        return jnp.dot(values, wo_v[slot, :, at], preferred_element_type=jnp.float32)

    def advance(source, slot, attended, factor):
        for i in range(PIECES):
            at = pl.ds(i * quarter, quarter)
            out_ref[0, :, at] = (source[:, at].astype(jnp.float32) + factor * update(attended, slot, at)).astype(
                jnp.bfloat16
            )

    attended = attend(0)
    factor = gate(0) * seen

    @pl.when(core == 0)
    def _():
        mixed[0] = attended
        mixed_copies[0].start()
        change = jnp.dot(attended, joint[0], preferred_element_type=jnp.float32)
        store_queries(first[1] + factor * change, 1)
        later = attend(1)
        mixed[1] = later
        mixed_copies[1].start()
        advance(text_v.at[0], 0, attended, factor)
        for piece in out_pieces[:half]:
            piece.wait_recv()
        advance(out_ref.at[0], 1, later, gate(1) * seen)
        for copy in back_copies:
            copy.wait_recv()

    @pl.when(core == 1)
    def _():
        advance(text_v.at[0], 0, attended, factor)
        mixed_copies[0].wait_recv()
        before = gate(1) * seen_other
        for i in range(PIECES):
            at = pl.ds((PIECES + i) * quarter, quarter)
            back[:, i * quarter : (i + 1) * quarter] = (
                text_v[1, :, at].astype(jnp.float32) + before * update(mixed[2], 1, at)
            ).astype(jnp.bfloat16)
        mixed_copies[1].wait_recv()
        both = jnp.concatenate([attended, mixed[3]], axis=0)
        after = gate(0) * seen_other
        for i in range(PIECES):
            at = pl.ds((PIECES + i) * quarter, quarter)
            here = pl.ds(i * quarter, quarter)
            sums = update(both, 0, at)
            back[:, here] = (back[:, here].astype(jnp.float32) + after * sums[tokens:]).astype(jnp.bfloat16)
            back_copies[i].start()
            out_ref[0, :, at] = (text_v[0, :, at].astype(jnp.float32) + factor * sums[:tokens]).astype(jnp.bfloat16)

    for copy in image_copies + weight_copies:
        copy.wait_send()
    for distance in range(1, lines):
        partial_copy(0, distance).wait_send()

    small_copy.wait_send()

    @pl.when(core == 0)
    def _():
        for distance in range(1, lines):
            partial_copy(1, distance).wait_send()
        for copy in [text_copy] + mixed_copies + out_pieces[half:]:
            copy.wait_send()

    @pl.when(core == 1)
    def _():
        for distance in range(QUAD):
            relay(distance).wait_send()
        for copy in [first_copy, joint_copy] + query_pieces + out_pieces[:half] + back_copies:
            copy.wait_send()


def local_fused(
    text_states,
    image_states,
    image_start,
    w_query,
    w_key,
    w_value,
    w_out,
    query_gain,
    key_gain,
    cross_gate,
):
    lines = lax.axis_size("dp") // QUAD
    tokens, width = text_states.shape[1:]
    image_rows = image_states.shape[1]
    depth, head = w_key.shape[1:]
    columns = w_query.shape[2]
    heads = columns // head
    span = QUAD * depth
    groups = 2 * image_rows
    hbm = pl.BlockSpec(memory_space=pltpu.HBM)
    vmem = pl.BlockSpec(memory_space=pltpu.VMEM)
    smem = pl.BlockSpec(memory_space=pltpu.SMEM)
    dma = pltpu.SemaphoreType.DMA
    return pl.pallas_call(
        functools.partial(kernel, lines),
        out_shape=jax.ShapeDtypeStruct((1, tokens, width), jnp.bfloat16),
        in_specs=[hbm, hbm, hbm, hbm, hbm, hbm, hbm, hbm, hbm, smem],
        out_specs=vmem,
        scratch_shapes=[
            pltpu.VMEM((2, tokens, width), jnp.bfloat16),
            pltpu.VMEM((width, columns), jnp.bfloat16),
            pltpu.VMEM((width // 2, columns), jnp.bfloat16),
            pltpu.VMEM((2, columns, width), jnp.bfloat16),
            pltpu.VMEM((columns, columns), jnp.float32),
            pltpu.VMEM((2, columns, columns), jnp.bfloat16),
            pltpu.VMEM((2, tokens, columns), jnp.float32),
            pltpu.VMEM((4, tokens, columns), jnp.bfloat16),
            pltpu.VMEM((tokens, width // 2), jnp.bfloat16),
            pltpu.VMEM((2, span, 2 * head), jnp.bfloat16),
            pltpu.VMEM((lines, groups, span), jnp.bfloat16),
            pltpu.VMEM((lines, 2, groups, 2 * head), jnp.float32),
            pltpu.VMEM((lines, 2, groups, 2 * head), jnp.bfloat16),
            pltpu.VMEM((lines, 2, groups, 2 * head), jnp.bfloat16),
            pltpu.VMEM((heads * tokens, head), jnp.bfloat16),
            pltpu.VMEM((2, 8, head), jnp.float32),
            pltpu.VMEM((1, head), jnp.float32),
            pltpu.VMEM((1, head), jnp.float32),
            pltpu.SMEM(image_start.shape[:1], jnp.int32),
            dma((9,)),
            dma((QUAD, 2)),
            dma((QUAD, 2)),
            dma((lines, 2)),
            dma((lines, 2)),
            dma((QUAD,)),
            dma((QUAD,)),
            dma((2, PIECES)),
            dma((2, PIECES)),
            dma((6,)),
            dma((6,)),
            dma((PIECES,)),
            dma((PIECES,)),
            dma((2, lines)),
            dma((2, lines)),
        ],
        compiler_params=pltpu.CompilerParams(
            collective_id=0, has_side_effects=True, vmem_limit_bytes=48 * 2**20
        ),
    )(
        pltpu.with_memory_space_constraint(text_states, pltpu.HBM),
        pltpu.with_memory_space_constraint(image_states, pltpu.HBM),
        pltpu.with_memory_space_constraint(image_start.reshape(-1), pltpu.HBM),
        pltpu.with_memory_space_constraint(w_query, pltpu.HBM),
        pltpu.with_memory_space_constraint(w_key, pltpu.HBM),
        pltpu.with_memory_space_constraint(w_value, pltpu.HBM),
        pltpu.with_memory_space_constraint(w_out, pltpu.HBM),
        pltpu.with_memory_space_constraint(query_gain, pltpu.HBM),
        pltpu.with_memory_space_constraint(key_gain, pltpu.HBM),
        cross_gate,
    )


def solution(mesh):
    placed = (
        P("pipe", "dp", None),
        P(None, ("dp", "pipe"), None),
        P(None, "dp"),
        P("pipe", None, None),
        P("pipe", "dp", None),
        P("pipe", "dp", None),
        P("pipe", None, None),
        P("pipe", None),
        P("pipe", None),
        P("pipe"),
    )
    fits = mesh.shape["pipe"] == 2 and mesh.shape["dp"] == QUAD * QUAD
    return jax.shard_map(
        local_fused if fits else local,
        mesh=mesh,
        in_specs=placed,
        out_specs=P("pipe", "dp", None),
        check_vma=False,
    )
```

```python
import functools
import math

import jax
import jax.numpy as jnp
from jax import lax
from jax.experimental import pallas as pl
from jax.experimental.pallas import tpu as pltpu
from jax.sharding import PartitionSpec as P

epsilon = 1e-06
MESH = pl.DeviceIdType.MESH
QUAD = 4
PIECES = 4


def shifted(block, axis, distance):
    devices = range(lax.axis_size(axis))
    route = [((i - distance) % len(devices), i) for i in devices]
    return lax.ppermute(block, axis, route)


def normalized(projected, scales):
    mean_square = jnp.mean(projected * projected, axis=-1, keepdims=True)
    return projected * lax.rsqrt(mean_square + epsilon) * scales


def keep_state(current, holding):
    return current


def local(
    text_states,
    image_states,
    image_start,
    w_query,
    w_key,
    w_value,
    w_out,
    query_gain,
    key_gain,
    cross_gate,
):
    sections = lax.axis_size("pipe")
    section_index = lax.axis_index("pipe")
    pictures = lax.all_gather(image_states, "pipe", axis=1, tiled=True)
    batches, image_rows, width = pictures.shape
    flattened = pictures.reshape(batches * image_rows, width)
    head_size = w_key.shape[2]
    head_count = w_query.shape[2] // head_size
    key_full, value_full = (
        lax.all_gather(w_key, "dp", axis=1, tiled=True),
        lax.all_gather(w_value, "dp", axis=1, tiled=True),
    )
    key_sums = jnp.dot(flattened, key_full[0], preferred_element_type=jnp.float32)
    value_sums = jnp.dot(flattened, value_full[0], preferred_element_type=jnp.float32)
    key_rows = (
        normalized(key_sums, key_gain[0])
        .astype(jnp.bfloat16)
        .reshape(batches, image_rows, head_size)
    )
    value_rows = value_sums.astype(jnp.bfloat16).reshape(batches, image_rows, head_size)
    query_weight = w_query[0]
    out_weight = w_out[0]
    factor = jnp.tanh(cross_gate[0])
    tok_rows = text_states.shape[1]
    positions = jnp.arange(tok_rows, dtype=jnp.int32)
    root_size = math.sqrt(head_size)

    def apply_layer(current, holding):
        own_keys = lax.dynamic_index_in_dim(key_rows, holding, 0, keepdims=False)
        own_values = lax.dynamic_index_in_dim(value_rows, holding, 0, keepdims=False)
        query_sums = jnp.dot(current, query_weight, preferred_element_type=jnp.float32)
        query_sums = query_sums.reshape(tok_rows * head_count, head_size)
        queries = normalized(query_sums, query_gain[0]).astype(jnp.bfloat16)
        scores = jnp.dot(queries, own_keys.T, preferred_element_type=jnp.float32) / root_size
        exponent = jnp.exp(scores)
        probs = (exponent / jnp.sum(exponent, axis=-1, keepdims=True)).astype(jnp.bfloat16)
        attended = jnp.dot(probs, own_values, preferred_element_type=jnp.float32).astype(
            jnp.bfloat16
        )
        attended = attended.reshape(tok_rows, head_count * head_size)
        update = jnp.dot(attended, out_weight, preferred_element_type=jnp.float32)
        first_seen = lax.dynamic_index_in_dim(image_start[:, 0], holding, 0, keepdims=False)
        seen = (positions >= first_seen).astype(jnp.float32)[:, None]
        return (current.astype(jnp.float32) + factor * seen * update).astype(jnp.bfloat16)

    current = text_states[0]
    for moment in range(sections):
        holding = jnp.mod(section_index - moment, sections)
        current = lax.cond(moment <= section_index, apply_layer, keep_state, current, holding)
        current = shifted(current, "pipe", 1)
    return current[None]


def kernel(
    lines,
    text_ref,
    image_ref,
    start_ref,
    wq_ref,
    wk_ref,
    wv_ref,
    wo_ref,
    qg_ref,
    kg_ref,
    gate_ref,
    out_ref,
    text_v,
    wq_v,
    wq_half,
    wo_v,
    joint_sum,
    joint,
    first,
    mixed,
    back,
    wkv,
    image_v,
    img,
    part,
    part_out,
    part_in,
    query_v,
    small,
    query_gain,
    key_gain,
    starts,
    load_sem,
    w_send,
    w_recv,
    i_send,
    i_recv,
    relay_send,
    relay_recv,
    big_send,
    big_recv,
    one_send,
    one_recv,
    back_send,
    back_recv,
    p_send,
    p_recv,
):
    place = lax.axis_index("dp")
    core = lax.axis_index("pipe")
    other = 1 - core
    line = place // QUAD
    spot = place % QUAD
    depth = wk_ref.shape[1]
    head = wk_ref.shape[2]
    tokens, width = text_v.shape[1:]
    heads = wq_ref.shape[2] // head
    image_rows = image_ref.shape[1]
    span = QUAD * depth

    def quad_peer(distance):
        return line * QUAD + (spot + distance) % QUAD

    def line_peer(distance):
        return ((line + distance) % lines) * QUAD + spot

    def rows_of(index):
        return pl.ds(pl.multiple_of(index * depth, depth), depth)

    own_rows = pl.ds(pl.multiple_of(core * image_rows, image_rows), image_rows)

    def columns_of(index):
        return pl.ds(pl.multiple_of(index * span, span), span)

    loads = [
        pltpu.make_async_copy(wk_ref.at[0], wkv.at[0, rows_of(spot), pl.ds(0, head)], load_sem.at[0]),
        pltpu.make_async_copy(wv_ref.at[0], wkv.at[0, rows_of(spot), pl.ds(head, head)], load_sem.at[1]),
        pltpu.make_async_copy(image_ref, image_v, load_sem.at[2]),
        pltpu.make_async_copy(image_ref.at[core, :, columns_of(line)], img.at[line, own_rows], load_sem.at[3]),
        pltpu.make_async_copy(qg_ref, query_gain, load_sem.at[4]),
        pltpu.make_async_copy(kg_ref, key_gain, load_sem.at[5]),
        pltpu.make_async_copy(start_ref, starts, load_sem.at[6]),
        pltpu.make_async_copy(text_ref.at[0], text_v.at[0], load_sem.at[7]),
        pltpu.make_async_copy(wq_ref.at[0], wq_v, load_sem.at[8]),
    ]
    for load in loads:
        load.start()

    barrier = pltpu.get_barrier_semaphore()
    peers = [(quad_peer(d), core) for d in range(1, QUAD)]
    peers += [(line_peer(d), side) for d in range(1, lines) for side in (core, other)]
    peers += [(place, other)]
    for peer in peers:
        pl.semaphore_signal(barrier, inc=1, device_id=peer, device_id_type=MESH)
    for load in loads[:3]:
        load.wait()
    pl.semaphore_wait(barrier, len(peers))

    weight_copies = [
        pltpu.make_async_remote_copy(
            src_ref=wkv.at[0, rows_of(spot)],
            dst_ref=wkv.at[0, rows_of(spot)],
            send_sem=w_send.at[distance],
            recv_sem=w_recv.at[distance],
            device_id=(quad_peer(distance), core),
            device_id_type=MESH,
        )
        for distance in range(1, QUAD)
    ]
    image_copies = [
        pltpu.make_async_remote_copy(
            src_ref=image_v.at[side, :, columns_of((line + distance) % lines)],
            dst_ref=img.at[line, own_rows],
            send_sem=i_send.at[distance, turn],
            recv_sem=i_recv.at[distance, turn],
            device_id=(line_peer(distance), side),
            device_id_type=MESH,
        )
        for distance in (*range(1, lines), 0)
        for turn, side in enumerate((core, other))
        if distance + turn > 0
    ]
    for i in range(QUAD - 1):
        weight_copies[i].start()
        for copy in image_copies[2 * i : 2 * i + 2]:
            copy.start()
    for copy in image_copies[2 * QUAD - 2 :]:
        copy.start()

    def across(src, dst, send, recv):
        return pltpu.make_async_remote_copy(
            src_ref=src,
            dst_ref=dst,
            send_sem=send,
            recv_sem=recv,
            device_id=(place, other),
            device_id_type=MESH,
        )

    stretch = width // PIECES
    out_pieces = [
        across(
            wo_ref.at[0, :, pl.ds(i * stretch, stretch)],
            wo_v.at[1, :, pl.ds(i * stretch, stretch)],
            big_send.at[0, i],
            big_recv.at[0, i],
        )
        for i in range(PIECES)
    ]
    half = PIECES // 2
    query_pieces = [
        across(
            wq_ref.at[0, pl.ds(i * stretch, stretch)],
            wq_half.at[pl.ds(i * stretch, stretch)],
            big_send.at[1, i],
            big_recv.at[1, i],
        )
        for i in range(half)
    ]
    small_copy = across(small.at[0], small.at[1], one_send.at[0], one_recv.at[0])
    text_copy = across(text_ref.at[0], text_v.at[1], one_send.at[1], one_recv.at[1])
    first_copy = across(first.at[0], first.at[1], one_send.at[2], one_recv.at[2])
    joint_copy = across(joint.at[0], joint.at[1], one_send.at[3], one_recv.at[3])
    mixed_copies = [across(mixed.at[i], mixed.at[2 + i], one_send.at[4 + i], one_recv.at[4 + i]) for i in range(2)]
    quarter = stretch // 2
    back_copies = [
        across(
            back.at[:, pl.ds(i * quarter, quarter)],
            out_ref.at[0, :, pl.ds((PIECES + i) * quarter, quarter)],
            back_send.at[i],
            back_recv.at[i],
        )
        for i in range(PIECES)
    ]

    def relay(distance):
        rows = rows_of((spot + QUAD - distance) % QUAD)
        return across(wkv.at[0, rows], wkv.at[1, rows], relay_send.at[distance], relay_recv.at[distance])

    loads[4].wait()
    loads[5].wait()
    small[0, 0:1] = query_gain[...]
    small[0, 1:2] = key_gain[...]
    small[0, 2:3] = jnp.full((1, head), gate_ref[0], jnp.float32)

    small_copy.start()
    middle = width // 2
    out_loads = [
        pltpu.make_async_copy(
            wo_ref.at[0, :, pl.ds(i * middle, middle)], wo_v.at[0, :, pl.ds(i * middle, middle)], load_sem.at[9 + i]
        )
        for i in range(2)
    ]

    @pl.when(core == 0)
    def _():
        text_copy.start()
        for piece in out_pieces[half:]:
            piece.start()
        out_loads[0].start()

    @pl.when(core == 1)
    def _():
        for piece in query_pieces:
            piece.start()
        relay(0).start()

    chunk = 512

    def project(slots):
        rows = slots * tokens

        def step(i, total):
            at = pl.ds(pl.multiple_of(i * chunk, chunk), chunk)
            return total + jnp.dot(
                text_v[:slots, :, at].reshape(rows, chunk), wq_v[at, :], preferred_element_type=jnp.float32
            )

        return lax.fori_loop(0, width // chunk, step, jnp.zeros((rows, heads * head), jnp.float32))

    def store_queries(sums, slot):
        for h in range(heads):
            query_v[h * tokens : (h + 1) * tokens, :] = normalized(
                sums[:, h * head : (h + 1) * head], small[slot, 0:1]
            ).astype(jnp.bfloat16)

    def join(i, left, right):
        product = jnp.dot(left, right, preferred_element_type=jnp.float32)
        joint_sum[...] = product if i == 0 else joint_sum[...] + product

    loads[7].wait()
    loads[8].wait()

    def partial_sums(slot):
        groups = 2 * image_rows
        sums = jnp.dot(
            img[...].reshape(lines * groups, span), wkv[slot], preferred_element_type=jnp.float32
        )
        sums = sums.reshape(lines, groups, 2 * head)
        part[:, slot] = sums
        part_out[:, slot] = sums.astype(jnp.bfloat16)

    def partial_copy(slot, distance):
        return pltpu.make_async_remote_copy(
            src_ref=part_out.at[(line + distance) % lines, slot],
            dst_ref=part_in.at[line, slot],
            send_sem=p_send.at[slot, distance],
            recv_sem=p_recv.at[slot, distance],
            device_id=(line_peer(distance), core),
            device_id_type=MESH,
        )

    def arrived():
        loads[3].wait()
        for copy in image_copies:
            copy.wait_recv()

    def return_partials(slot):
        partial_sums(slot)
        for distance in range(1, lines):
            partial_copy(slot, distance).start()

    @pl.when(core == 0)
    def _():
        def join_own(i):
            query_pieces[i].wait_recv()
            at = pl.ds(i * stretch, stretch)
            join(i, wo_v[0, :, at], wq_half[at, :])

        store_queries(project(1), 0)
        out_loads[0].wait()
        for i in range(half - 1):
            join_own(i)
        for copy in weight_copies:
            copy.wait_recv()
        arrived()
        return_partials(0)
        for distance in range(QUAD):
            relay(distance).wait_recv()
        return_partials(1)
        join_own(half - 1)
        small_copy.wait_recv()
        first_copy.wait_recv()
        joint_copy.wait_recv()
        joint[0] = (joint_sum[...] + joint[1].astype(jnp.float32)).astype(jnp.bfloat16)

    @pl.when(core == 1)
    def _():
        def join_own(i):
            out_pieces[half + i].wait_recv()
            at = pl.ds((half + i) * stretch, stretch)
            join(i, wo_v[1, :, at], wq_v[at, :])

        text_copy.wait_recv()
        sums = project(2)
        store_queries(sums[:tokens], 0)
        first[0] = sums[tokens:]
        first_copy.start()
        for load in out_loads:
            load.start()
        for i in range(half - 1):
            join_own(i)
        for distance in range(1, QUAD):
            weight_copies[distance - 1].wait_recv()
            relay(distance).start()
        for piece in out_pieces[:half]:
            piece.start()
        arrived()
        return_partials(0)
        join_own(half - 1)
        joint[0] = joint_sum[...].astype(jnp.bfloat16)
        joint_copy.start()
        for load in out_loads:
            load.wait()
        small_copy.wait_recv()

    positions = lax.broadcasted_iota(jnp.int32, (tokens, 1), 0)
    loads[6].wait()
    seen = (positions >= starts[core]).astype(jnp.float32)
    seen_other = (positions >= starts[other]).astype(jnp.float32)
    root_size = math.sqrt(head)

    def attend(slot):
        total = part[line, slot]
        for distance in range(1, lines):
            partial_copy(slot, distance).wait_recv()
            total += part_in[(line + lines - distance) % lines, slot].astype(jnp.float32)
        keys = normalized(total[:, :head], small[slot, 1:2]).astype(jnp.bfloat16)
        values = total[:, head:].astype(jnp.bfloat16)
        scores = (
            lax.dot_general(
                query_v[...], keys, (((1,), (1,)), ((), ())), preferred_element_type=jnp.float32
            )
            / root_size
        )
        exponent = jnp.exp(scores)
        probs = (exponent / jnp.sum(exponent, axis=-1, keepdims=True)).astype(jnp.bfloat16)
        attended = jnp.dot(probs, values, preferred_element_type=jnp.float32).astype(jnp.bfloat16)
        attended = jnp.concatenate(
            [attended[h * tokens : (h + 1) * tokens] for h in range(heads)], axis=1
        )
        return attended

    def gate(slot):
        return jnp.tanh(small[slot, 2:3])[:, 0:1]

    def update(values, slot, at):
        return jnp.dot(values, wo_v[slot, :, at], preferred_element_type=jnp.float32)

    def advance(source, slot, attended, factor):
        for i in range(PIECES):
            at = pl.ds(i * quarter, quarter)
            out_ref[0, :, at] = (source[:, at].astype(jnp.float32) + factor * update(attended, slot, at)).astype(
                jnp.bfloat16
            )

    attended = attend(0)
    factor = gate(0) * seen

    @pl.when(core == 0)
    def _():
        mixed[0] = attended
        mixed_copies[0].start()
        change = jnp.dot(attended, joint[0], preferred_element_type=jnp.float32)
        store_queries(first[1] + factor * change, 1)
        later = attend(1)
        mixed[1] = later
        mixed_copies[1].start()
        advance(text_v.at[0], 0, attended, factor)
        for piece in out_pieces[:half]:
            piece.wait_recv()
        advance(out_ref.at[0], 1, later, gate(1) * seen)
        for copy in back_copies:
            copy.wait_recv()

    @pl.when(core == 1)
    def _():
        advance(text_v.at[0], 0, attended, factor)
        mixed_copies[0].wait_recv()
        before = gate(1) * seen_other
        for i in range(PIECES):
            at = pl.ds((PIECES + i) * quarter, quarter)
            back[:, i * quarter : (i + 1) * quarter] = (
                text_v[1, :, at].astype(jnp.float32) + before * update(mixed[2], 1, at)
            ).astype(jnp.bfloat16)
        mixed_copies[1].wait_recv()
        both = jnp.concatenate([attended, mixed[3]], axis=0)
        after = gate(0) * seen_other
        for i in range(PIECES):
            at = pl.ds((PIECES + i) * quarter, quarter)
            here = pl.ds(i * quarter, quarter)
            sums = update(both, 0, at)
            back[:, here] = (back[:, here].astype(jnp.float32) + after * sums[tokens:]).astype(jnp.bfloat16)
            back_copies[i].start()
            out_ref[0, :, at] = (text_v[0, :, at].astype(jnp.float32) + factor * sums[:tokens]).astype(jnp.bfloat16)

    for copy in image_copies + weight_copies:
        copy.wait_send()
    for distance in range(1, lines):
        partial_copy(0, distance).wait_send()

    small_copy.wait_send()

    @pl.when(core == 0)
    def _():
        for distance in range(1, lines):
            partial_copy(1, distance).wait_send()
        for copy in [text_copy] + mixed_copies + out_pieces[half:]:
            copy.wait_send()

    @pl.when(core == 1)
    def _():
        for distance in range(QUAD):
            relay(distance).wait_send()
        for copy in [first_copy, joint_copy] + query_pieces + out_pieces[:half] + back_copies:
            copy.wait_send()


def local_fused(
    text_states,
    image_states,
    image_start,
    w_query,
    w_key,
    w_value,
    w_out,
    query_gain,
    key_gain,
    cross_gate,
):
    lines = lax.axis_size("dp") // QUAD
    tokens, width = text_states.shape[1:]
    image_rows = image_states.shape[1]
    depth, head = w_key.shape[1:]
    columns = w_query.shape[2]
    heads = columns // head
    span = QUAD * depth
    groups = 2 * image_rows
    hbm = pl.BlockSpec(memory_space=pltpu.HBM)
    vmem = pl.BlockSpec(memory_space=pltpu.VMEM)
    smem = pl.BlockSpec(memory_space=pltpu.SMEM)
    dma = pltpu.SemaphoreType.DMA
    return pl.pallas_call(
        functools.partial(kernel, lines),
        out_shape=jax.ShapeDtypeStruct((1, tokens, width), jnp.bfloat16),
        in_specs=[hbm, hbm, hbm, hbm, hbm, hbm, hbm, hbm, hbm, smem],
        out_specs=vmem,
        scratch_shapes=[
            pltpu.VMEM((2, tokens, width), jnp.bfloat16),
            pltpu.VMEM((width, columns), jnp.bfloat16),
            pltpu.VMEM((width // 2, columns), jnp.bfloat16),
            pltpu.VMEM((2, columns, width), jnp.bfloat16),
            pltpu.VMEM((columns, columns), jnp.float32),
            pltpu.VMEM((2, columns, columns), jnp.bfloat16),
            pltpu.VMEM((2, tokens, columns), jnp.float32),
            pltpu.VMEM((4, tokens, columns), jnp.bfloat16),
            pltpu.VMEM((tokens, width // 2), jnp.bfloat16),
            pltpu.VMEM((2, span, 2 * head), jnp.bfloat16),
            pltpu.VMEM((2, image_rows, width), jnp.bfloat16),
            pltpu.VMEM((lines, groups, span), jnp.bfloat16),
            pltpu.VMEM((lines, 2, groups, 2 * head), jnp.float32),
            pltpu.VMEM((lines, 2, groups, 2 * head), jnp.bfloat16),
            pltpu.VMEM((lines, 2, groups, 2 * head), jnp.bfloat16),
            pltpu.VMEM((heads * tokens, head), jnp.bfloat16),
            pltpu.VMEM((2, 8, head), jnp.float32),
            pltpu.VMEM((1, head), jnp.float32),
            pltpu.VMEM((1, head), jnp.float32),
            pltpu.SMEM(image_start.shape[:1], jnp.int32),
            dma((11,)),
            dma((QUAD,)),
            dma((QUAD,)),
            dma((lines, 2)),
            dma((lines, 2)),
            dma((QUAD,)),
            dma((QUAD,)),
            dma((2, PIECES)),
            dma((2, PIECES)),
            dma((6,)),
            dma((6,)),
            dma((PIECES,)),
            dma((PIECES,)),
            dma((2, lines)),
            dma((2, lines)),
        ],
        compiler_params=pltpu.CompilerParams(
            collective_id=0, has_side_effects=True, vmem_limit_bytes=48 * 2**20
        ),
    )(
        pltpu.with_memory_space_constraint(text_states, pltpu.HBM),
        pltpu.with_memory_space_constraint(image_states, pltpu.HBM),
        pltpu.with_memory_space_constraint(image_start.reshape(-1), pltpu.HBM),
        pltpu.with_memory_space_constraint(w_query, pltpu.HBM),
        pltpu.with_memory_space_constraint(w_key, pltpu.HBM),
        pltpu.with_memory_space_constraint(w_value, pltpu.HBM),
        pltpu.with_memory_space_constraint(w_out, pltpu.HBM),
        pltpu.with_memory_space_constraint(query_gain, pltpu.HBM),
        pltpu.with_memory_space_constraint(key_gain, pltpu.HBM),
        cross_gate,
    )


def solution(mesh):
    placed = (
        P("pipe", "dp", None),
        P(None, ("dp", "pipe"), None),
        P(None, "dp"),
        P("pipe", None, None),
        P("pipe", "dp", None),
        P("pipe", "dp", None),
        P("pipe", None, None),
        P("pipe", None),
        P("pipe", None),
        P("pipe"),
    )
    fits = mesh.shape["pipe"] == 2 and mesh.shape["dp"] == QUAD * QUAD
    return jax.shard_map(
        local_fused if fits else local,
        mesh=mesh,
        in_specs=placed,
        out_specs=P("pipe", "dp", None),
        check_vma=False,
    )
```

```python
import functools
import math

import jax
import jax.numpy as jnp
from jax import lax
from jax.experimental import pallas as pl
from jax.experimental.pallas import tpu as pltpu
from jax.sharding import PartitionSpec as P

epsilon = 1e-06
MESH = pl.DeviceIdType.MESH
QUAD = 4
PIECES = 4


def shifted(block, axis, distance):
    devices = range(lax.axis_size(axis))
    route = [((i - distance) % len(devices), i) for i in devices]
    return lax.ppermute(block, axis, route)


def normalized(projected, scales):
    mean_square = jnp.mean(projected * projected, axis=-1, keepdims=True)
    return projected * lax.rsqrt(mean_square + epsilon) * scales


def keep_state(current, holding):
    return current


def local(
    text_states,
    image_states,
    image_start,
    w_query,
    w_key,
    w_value,
    w_out,
    query_gain,
    key_gain,
    cross_gate,
):
    sections = lax.axis_size("pipe")
    section_index = lax.axis_index("pipe")
    pictures = lax.all_gather(image_states, "pipe", axis=1, tiled=True)
    batches, image_rows, width = pictures.shape
    flattened = pictures.reshape(batches * image_rows, width)
    head_size = w_key.shape[2]
    head_count = w_query.shape[2] // head_size
    key_full, value_full = (
        lax.all_gather(w_key, "dp", axis=1, tiled=True),
        lax.all_gather(w_value, "dp", axis=1, tiled=True),
    )
    key_sums = jnp.dot(flattened, key_full[0], preferred_element_type=jnp.float32)
    value_sums = jnp.dot(flattened, value_full[0], preferred_element_type=jnp.float32)
    key_rows = (
        normalized(key_sums, key_gain[0])
        .astype(jnp.bfloat16)
        .reshape(batches, image_rows, head_size)
    )
    value_rows = value_sums.astype(jnp.bfloat16).reshape(batches, image_rows, head_size)
    query_weight = w_query[0]
    out_weight = w_out[0]
    factor = jnp.tanh(cross_gate[0])
    tok_rows = text_states.shape[1]
    positions = jnp.arange(tok_rows, dtype=jnp.int32)
    root_size = math.sqrt(head_size)

    def apply_layer(current, holding):
        own_keys = lax.dynamic_index_in_dim(key_rows, holding, 0, keepdims=False)
        own_values = lax.dynamic_index_in_dim(value_rows, holding, 0, keepdims=False)
        query_sums = jnp.dot(current, query_weight, preferred_element_type=jnp.float32)
        query_sums = query_sums.reshape(tok_rows * head_count, head_size)
        queries = normalized(query_sums, query_gain[0]).astype(jnp.bfloat16)
        scores = jnp.dot(queries, own_keys.T, preferred_element_type=jnp.float32) / root_size
        exponent = jnp.exp(scores)
        probs = (exponent / jnp.sum(exponent, axis=-1, keepdims=True)).astype(jnp.bfloat16)
        attended = jnp.dot(probs, own_values, preferred_element_type=jnp.float32).astype(
            jnp.bfloat16
        )
        attended = attended.reshape(tok_rows, head_count * head_size)
        update = jnp.dot(attended, out_weight, preferred_element_type=jnp.float32)
        first_seen = lax.dynamic_index_in_dim(image_start[:, 0], holding, 0, keepdims=False)
        seen = (positions >= first_seen).astype(jnp.float32)[:, None]
        return (current.astype(jnp.float32) + factor * seen * update).astype(jnp.bfloat16)

    current = text_states[0]
    for moment in range(sections):
        holding = jnp.mod(section_index - moment, sections)
        current = lax.cond(moment <= section_index, apply_layer, keep_state, current, holding)
        current = shifted(current, "pipe", 1)
    return current[None]


def kernel(
    lines,
    text_ref,
    image_ref,
    start_ref,
    wq_ref,
    wk_ref,
    wv_ref,
    wo_ref,
    qg_ref,
    kg_ref,
    gate_ref,
    out_ref,
    text_v,
    wq_v,
    wq_half,
    wo_v,
    joint_sum,
    joint,
    first,
    mixed,
    back,
    wkv,
    image_v,
    img,
    part,
    part_out,
    part_in,
    query_v,
    small,
    query_gain,
    key_gain,
    starts,
    load_sem,
    w_send,
    w_recv,
    i_send,
    i_recv,
    relay_send,
    relay_recv,
    big_send,
    big_recv,
    one_send,
    one_recv,
    back_send,
    back_recv,
    p_send,
    p_recv,
):
    place = lax.axis_index("dp")
    core = lax.axis_index("pipe")
    other = 1 - core
    line = place // QUAD
    spot = place % QUAD
    depth = wk_ref.shape[1]
    head = wk_ref.shape[2]
    tokens, width = text_v.shape[1:]
    heads = wq_ref.shape[2] // head
    image_rows = image_ref.shape[1]
    span = QUAD * depth

    def quad_peer(distance):
        return line * QUAD + (spot + distance) % QUAD

    def line_peer(distance):
        return ((line + distance) % lines) * QUAD + spot

    def rows_of(index):
        return pl.ds(pl.multiple_of(index * depth, depth), depth)

    own_rows = pl.ds(pl.multiple_of(core * image_rows, image_rows), image_rows)

    def columns_of(index):
        return pl.ds(pl.multiple_of(index * span, span), span)

    loads = [
        pltpu.make_async_copy(wk_ref.at[0], wkv.at[0, rows_of(spot), pl.ds(0, head)], load_sem.at[0]),
        pltpu.make_async_copy(wv_ref.at[0], wkv.at[0, rows_of(spot), pl.ds(head, head)], load_sem.at[1]),
        pltpu.make_async_copy(image_ref, image_v, load_sem.at[2]),
        pltpu.make_async_copy(image_ref.at[core, :, columns_of(line)], img.at[line, own_rows], load_sem.at[3]),
        pltpu.make_async_copy(qg_ref, query_gain, load_sem.at[4]),
        pltpu.make_async_copy(kg_ref, key_gain, load_sem.at[5]),
        pltpu.make_async_copy(start_ref, starts, load_sem.at[6]),
        pltpu.make_async_copy(text_ref.at[0], text_v.at[0], load_sem.at[7]),
        pltpu.make_async_copy(wq_ref.at[0], wq_v, load_sem.at[8]),
    ]
    for load in loads:
        load.start()

    barrier = pltpu.get_barrier_semaphore()
    peers = [(quad_peer(d), core) for d in range(1, QUAD)]
    peers += [(line_peer(d), side) for d in range(1, lines) for side in (core, other)]
    peers += [(place, other)]
    for peer in peers:
        pl.semaphore_signal(barrier, inc=1, device_id=peer, device_id_type=MESH)
    for load in loads[:3]:
        load.wait()
    pl.semaphore_wait(barrier, len(peers))

    weight_copies = [
        pltpu.make_async_remote_copy(
            src_ref=wkv.at[0, rows_of(spot)],
            dst_ref=wkv.at[0, rows_of(spot)],
            send_sem=w_send.at[distance],
            recv_sem=w_recv.at[distance],
            device_id=(quad_peer(distance), core),
            device_id_type=MESH,
        )
        for distance in range(1, QUAD)
    ]
    image_copies = [
        pltpu.make_async_remote_copy(
            src_ref=image_v.at[side, :, columns_of((line + distance) % lines)],
            dst_ref=img.at[line, own_rows],
            send_sem=i_send.at[distance, turn],
            recv_sem=i_recv.at[distance, turn],
            device_id=(line_peer(distance), side),
            device_id_type=MESH,
        )
        for distance in (*range(1, lines), 0)
        for turn, side in enumerate((core, other))
        if distance + turn > 0
    ]
    for i in range(QUAD - 1):
        weight_copies[i].start()
        for copy in image_copies[2 * i : 2 * i + 2]:
            copy.start()
    for copy in image_copies[2 * QUAD - 2 :]:
        copy.start()

    def across(src, dst, send, recv):
        return pltpu.make_async_remote_copy(
            src_ref=src,
            dst_ref=dst,
            send_sem=send,
            recv_sem=recv,
            device_id=(place, other),
            device_id_type=MESH,
        )

    stretch = width // PIECES
    out_pieces = [
        across(
            wo_ref.at[0, :, pl.ds(i * stretch, stretch)],
            wo_v.at[1, :, pl.ds(i * stretch, stretch)],
            big_send.at[0, i],
            big_recv.at[0, i],
        )
        for i in range(PIECES)
    ]
    half = PIECES // 2
    most = PIECES - 1
    query_pieces = [
        across(
            wq_ref.at[0, pl.ds(i * stretch, stretch)],
            wq_half.at[pl.ds(i * stretch, stretch)],
            big_send.at[1, i],
            big_recv.at[1, i],
        )
        for i in range(most)
    ]
    small_copy = across(small.at[0], small.at[1], one_send.at[0], one_recv.at[0])
    text_copy = across(text_ref.at[0], text_v.at[1], one_send.at[1], one_recv.at[1])
    first_copy = across(first.at[0], first.at[1], one_send.at[2], one_recv.at[2])
    joint_copy = across(joint.at[0], joint.at[1], one_send.at[3], one_recv.at[3])
    mixed_copies = [across(mixed.at[i], mixed.at[2 + i], one_send.at[4 + i], one_recv.at[4 + i]) for i in range(2)]
    quarter = stretch // 2
    back_copies = [
        across(
            back.at[:, pl.ds(i * quarter, quarter)],
            out_ref.at[0, :, pl.ds((PIECES + i) * quarter, quarter)],
            back_send.at[i],
            back_recv.at[i],
        )
        for i in range(PIECES)
    ]

    def relay(distance):
        rows = rows_of((spot + QUAD - distance) % QUAD)
        return across(wkv.at[0, rows], wkv.at[1, rows], relay_send.at[distance], relay_recv.at[distance])

    loads[4].wait()
    loads[5].wait()
    small[0, 0:1] = query_gain[...]
    small[0, 1:2] = key_gain[...]
    small[0, 2:3] = jnp.full((1, head), gate_ref[0], jnp.float32)

    small_copy.start()
    out_loads = [
        pltpu.make_async_copy(
            wo_ref.at[0, :, pl.ds(i * stretch, stretch)], wo_v.at[0, :, pl.ds(i * stretch, stretch)], load_sem.at[9 + i]
        )
        for i in range(PIECES)
    ]

    @pl.when(core == 0)
    def _():
        text_copy.start()
        for piece in reversed(out_pieces[half:]):
            piece.start()
        for load in out_loads[:most]:
            load.start()

    @pl.when(core == 1)
    def _():
        query_pieces[0].start()
        relay(0).start()
        for piece in query_pieces[1:]:
            piece.start()

    chunk = 512

    def project(slots):
        rows = slots * tokens

        def step(i, total):
            at = pl.ds(pl.multiple_of(i * chunk, chunk), chunk)
            return total + jnp.dot(
                text_v[:slots, :, at].reshape(rows, chunk), wq_v[at, :], preferred_element_type=jnp.float32
            )

        return lax.fori_loop(0, width // chunk, step, jnp.zeros((rows, heads * head), jnp.float32))

    def store_queries(sums, slot):
        for h in range(heads):
            query_v[h * tokens : (h + 1) * tokens, :] = normalized(
                sums[:, h * head : (h + 1) * head], small[slot, 0:1]
            ).astype(jnp.bfloat16)

    def join(left, right):
        return jnp.dot(left, right, preferred_element_type=jnp.float32)

    loads[7].wait()
    loads[8].wait()

    def partial_sums(slot):
        groups = 2 * image_rows
        sums = jnp.dot(
            img[...].reshape(lines * groups, span), wkv[slot], preferred_element_type=jnp.float32
        )
        sums = sums.reshape(lines, groups, 2 * head)
        part[:, slot] = sums
        part_out[:, slot] = sums.astype(jnp.bfloat16)

    def partial_copy(slot, distance):
        return pltpu.make_async_remote_copy(
            src_ref=part_out.at[(line + distance) % lines, slot],
            dst_ref=part_in.at[line, slot],
            send_sem=p_send.at[slot, distance],
            recv_sem=p_recv.at[slot, distance],
            device_id=(line_peer(distance), core),
            device_id_type=MESH,
        )

    def arrived():
        loads[3].wait()
        for copy in image_copies:
            copy.wait_recv()

    def return_partials(slot):
        partial_sums(slot)
        for distance in range(1, lines):
            partial_copy(slot, distance).start()

    @pl.when(core == 0)
    def _():
        def join_own(i):
            out_loads[i].wait()
            query_pieces[i].wait_recv()
            at = pl.ds(i * stretch, stretch)
            return join(wo_v[0, :, at], wq_half[at, :])

        store_queries(project(1), 0)
        joint_sum[...] = join_own(0)
        for copy in weight_copies:
            copy.wait_recv()
        arrived()
        return_partials(0)
        for distance in range(QUAD):
            relay(distance).wait_recv()
        return_partials(1)
        for i in range(1, most - 1):
            joint_sum[...] += join_own(i)
        joint_copy.wait_recv()
        joint[0] = (joint_sum[...] + joint[1].astype(jnp.float32) + join_own(most - 1)).astype(jnp.bfloat16)
        small_copy.wait_recv()
        first_copy.wait_recv()

    @pl.when(core == 1)
    def _():
        text_copy.wait_recv()
        sums = project(2)
        store_queries(sums[:tokens], 0)
        first[0] = sums[tokens:]
        first_copy.start()
        for load in out_loads:
            load.start()
        out_pieces[most].wait_recv()
        at = pl.ds(most * stretch, stretch)
        joint[0] = join(wo_v[1, :, at], wq_v[at, :]).astype(jnp.bfloat16)
        joint_copy.start()
        for distance in range(1, QUAD):
            weight_copies[distance - 1].wait_recv()
            relay(distance).start()
        for piece in out_pieces[:half]:
            piece.start()
        arrived()
        return_partials(0)
        for load in out_loads:
            load.wait()
        small_copy.wait_recv()

    positions = lax.broadcasted_iota(jnp.int32, (tokens, 1), 0)
    loads[6].wait()
    seen = (positions >= starts[core]).astype(jnp.float32)
    seen_other = (positions >= starts[other]).astype(jnp.float32)
    root_size = math.sqrt(head)

    def attend(slot):
        total = part[line, slot]
        for distance in range(1, lines):
            partial_copy(slot, distance).wait_recv()
            total += part_in[(line + lines - distance) % lines, slot].astype(jnp.float32)
        keys = normalized(total[:, :head], small[slot, 1:2]).astype(jnp.bfloat16)
        values = total[:, head:].astype(jnp.bfloat16)
        scores = (
            lax.dot_general(
                query_v[...], keys, (((1,), (1,)), ((), ())), preferred_element_type=jnp.float32
            )
            / root_size
        )
        exponent = jnp.exp(scores)
        probs = (exponent / jnp.sum(exponent, axis=-1, keepdims=True)).astype(jnp.bfloat16)
        attended = jnp.dot(probs, values, preferred_element_type=jnp.float32).astype(jnp.bfloat16)
        attended = jnp.concatenate(
            [attended[h * tokens : (h + 1) * tokens] for h in range(heads)], axis=1
        )
        return attended

    def gate(slot):
        return jnp.tanh(small[slot, 2:3])[:, 0:1]

    def update(values, slot, at):
        return jnp.dot(values, wo_v[slot, :, at], preferred_element_type=jnp.float32)

    def advance(source, slot, attended, factor):
        for i in range(PIECES):
            at = pl.ds(i * quarter, quarter)
            out_ref[0, :, at] = (source[:, at].astype(jnp.float32) + factor * update(attended, slot, at)).astype(
                jnp.bfloat16
            )

    attended = attend(0)
    factor = gate(0) * seen

    @pl.when(core == 0)
    def _():
        mixed[0] = attended
        mixed_copies[0].start()
        change = jnp.dot(attended, joint[0], preferred_element_type=jnp.float32)
        store_queries(first[1] + factor * change, 1)
        later = attend(1)
        mixed[1] = later
        mixed_copies[1].start()
        advance(text_v.at[0], 0, attended, factor)
        for piece in out_pieces[:half]:
            piece.wait_recv()
        advance(out_ref.at[0], 1, later, gate(1) * seen)
        for copy in back_copies:
            copy.wait_recv()

    @pl.when(core == 1)
    def _():
        advance(text_v.at[0], 0, attended, factor)
        for piece in out_pieces[half:most]:
            piece.wait_recv()
        mixed_copies[0].wait_recv()
        before = gate(1) * seen_other
        for i in range(PIECES):
            at = pl.ds((PIECES + i) * quarter, quarter)
            back[:, i * quarter : (i + 1) * quarter] = (
                text_v[1, :, at].astype(jnp.float32) + before * update(mixed[2], 1, at)
            ).astype(jnp.bfloat16)
        mixed_copies[1].wait_recv()
        both = jnp.concatenate([attended, mixed[3]], axis=0)
        after = gate(0) * seen_other
        for i in range(PIECES):
            at = pl.ds((PIECES + i) * quarter, quarter)
            here = pl.ds(i * quarter, quarter)
            sums = update(both, 0, at)
            back[:, here] = (back[:, here].astype(jnp.float32) + after * sums[tokens:]).astype(jnp.bfloat16)
            back_copies[i].start()
            out_ref[0, :, at] = (text_v[0, :, at].astype(jnp.float32) + factor * sums[:tokens]).astype(jnp.bfloat16)

    for copy in image_copies + weight_copies:
        copy.wait_send()
    for distance in range(1, lines):
        partial_copy(0, distance).wait_send()

    small_copy.wait_send()

    @pl.when(core == 0)
    def _():
        for distance in range(1, lines):
            partial_copy(1, distance).wait_send()
        for copy in [text_copy] + mixed_copies + out_pieces[half:]:
            copy.wait_send()

    @pl.when(core == 1)
    def _():
        for distance in range(QUAD):
            relay(distance).wait_send()
        for copy in [first_copy, joint_copy] + query_pieces + out_pieces[:half] + back_copies:
            copy.wait_send()


def local_fused(
    text_states,
    image_states,
    image_start,
    w_query,
    w_key,
    w_value,
    w_out,
    query_gain,
    key_gain,
    cross_gate,
):
    lines = lax.axis_size("dp") // QUAD
    tokens, width = text_states.shape[1:]
    image_rows = image_states.shape[1]
    depth, head = w_key.shape[1:]
    columns = w_query.shape[2]
    heads = columns // head
    span = QUAD * depth
    groups = 2 * image_rows
    hbm = pl.BlockSpec(memory_space=pltpu.HBM)
    vmem = pl.BlockSpec(memory_space=pltpu.VMEM)
    smem = pl.BlockSpec(memory_space=pltpu.SMEM)
    dma = pltpu.SemaphoreType.DMA
    return pl.pallas_call(
        functools.partial(kernel, lines),
        out_shape=jax.ShapeDtypeStruct((1, tokens, width), jnp.bfloat16),
        in_specs=[hbm, hbm, hbm, hbm, hbm, hbm, hbm, hbm, hbm, smem],
        out_specs=vmem,
        scratch_shapes=[
            pltpu.VMEM((2, tokens, width), jnp.bfloat16),
            pltpu.VMEM((width, columns), jnp.bfloat16),
            pltpu.VMEM((width - width // PIECES, columns), jnp.bfloat16),
            pltpu.VMEM((2, columns, width), jnp.bfloat16),
            pltpu.VMEM((columns, columns), jnp.float32),
            pltpu.VMEM((2, columns, columns), jnp.bfloat16),
            pltpu.VMEM((2, tokens, columns), jnp.float32),
            pltpu.VMEM((4, tokens, columns), jnp.bfloat16),
            pltpu.VMEM((tokens, width // 2), jnp.bfloat16),
            pltpu.VMEM((2, span, 2 * head), jnp.bfloat16),
            pltpu.VMEM((2, image_rows, width), jnp.bfloat16),
            pltpu.VMEM((lines, groups, span), jnp.bfloat16),
            pltpu.VMEM((lines, 2, groups, 2 * head), jnp.float32),
            pltpu.VMEM((lines, 2, groups, 2 * head), jnp.bfloat16),
            pltpu.VMEM((lines, 2, groups, 2 * head), jnp.bfloat16),
            pltpu.VMEM((heads * tokens, head), jnp.bfloat16),
            pltpu.VMEM((2, 8, head), jnp.float32),
            pltpu.VMEM((1, head), jnp.float32),
            pltpu.VMEM((1, head), jnp.float32),
            pltpu.SMEM(image_start.shape[:1], jnp.int32),
            dma((9 + PIECES,)),
            dma((QUAD,)),
            dma((QUAD,)),
            dma((lines, 2)),
            dma((lines, 2)),
            dma((QUAD,)),
            dma((QUAD,)),
            dma((2, PIECES)),
            dma((2, PIECES)),
            dma((6,)),
            dma((6,)),
            dma((PIECES,)),
            dma((PIECES,)),
            dma((2, lines)),
            dma((2, lines)),
        ],
        compiler_params=pltpu.CompilerParams(
            collective_id=0, has_side_effects=True, vmem_limit_bytes=48 * 2**20
        ),
    )(
        pltpu.with_memory_space_constraint(text_states, pltpu.HBM),
        pltpu.with_memory_space_constraint(image_states, pltpu.HBM),
        pltpu.with_memory_space_constraint(image_start.reshape(-1), pltpu.HBM),
        pltpu.with_memory_space_constraint(w_query, pltpu.HBM),
        pltpu.with_memory_space_constraint(w_key, pltpu.HBM),
        pltpu.with_memory_space_constraint(w_value, pltpu.HBM),
        pltpu.with_memory_space_constraint(w_out, pltpu.HBM),
        pltpu.with_memory_space_constraint(query_gain, pltpu.HBM),
        pltpu.with_memory_space_constraint(key_gain, pltpu.HBM),
        cross_gate,
    )


def solution(mesh):
    placed = (
        P("pipe", "dp", None),
        P(None, ("dp", "pipe"), None),
        P(None, "dp"),
        P("pipe", None, None),
        P("pipe", "dp", None),
        P("pipe", "dp", None),
        P("pipe", None, None),
        P("pipe", None),
        P("pipe", None),
        P("pipe"),
    )
    fits = mesh.shape["pipe"] == 2 and mesh.shape["dp"] == QUAD * QUAD
    return jax.shard_map(
        local_fused if fits else local,
        mesh=mesh,
        in_specs=placed,
        out_specs=P("pipe", "dp", None),
        check_vma=False,
    )
```

```python
import functools
import math

import jax
import jax.numpy as jnp
from jax import lax
from jax.experimental import pallas as pl
from jax.experimental.pallas import tpu as pltpu
from jax.sharding import PartitionSpec as P

epsilon = 1e-06
MESH = pl.DeviceIdType.MESH
QUAD = 4
PIECES = 4


def shifted(block, axis, distance):
    devices = range(lax.axis_size(axis))
    route = [((i - distance) % len(devices), i) for i in devices]
    return lax.ppermute(block, axis, route)


def normalized(projected, scales):
    mean_square = jnp.mean(projected * projected, axis=-1, keepdims=True)
    return projected * lax.rsqrt(mean_square + epsilon) * scales


def keep_state(current, holding):
    return current


def local(
    text_states,
    image_states,
    image_start,
    w_query,
    w_key,
    w_value,
    w_out,
    query_gain,
    key_gain,
    cross_gate,
):
    sections = lax.axis_size("pipe")
    section_index = lax.axis_index("pipe")
    pictures = lax.all_gather(image_states, "pipe", axis=1, tiled=True)
    batches, image_rows, width = pictures.shape
    flattened = pictures.reshape(batches * image_rows, width)
    head_size = w_key.shape[2]
    head_count = w_query.shape[2] // head_size
    key_full, value_full = (
        lax.all_gather(w_key, "dp", axis=1, tiled=True),
        lax.all_gather(w_value, "dp", axis=1, tiled=True),
    )
    key_sums = jnp.dot(flattened, key_full[0], preferred_element_type=jnp.float32)
    value_sums = jnp.dot(flattened, value_full[0], preferred_element_type=jnp.float32)
    key_rows = (
        normalized(key_sums, key_gain[0])
        .astype(jnp.bfloat16)
        .reshape(batches, image_rows, head_size)
    )
    value_rows = value_sums.astype(jnp.bfloat16).reshape(batches, image_rows, head_size)
    query_weight = w_query[0]
    out_weight = w_out[0]
    factor = jnp.tanh(cross_gate[0])
    tok_rows = text_states.shape[1]
    positions = jnp.arange(tok_rows, dtype=jnp.int32)
    root_size = math.sqrt(head_size)

    def apply_layer(current, holding):
        own_keys = lax.dynamic_index_in_dim(key_rows, holding, 0, keepdims=False)
        own_values = lax.dynamic_index_in_dim(value_rows, holding, 0, keepdims=False)
        query_sums = jnp.dot(current, query_weight, preferred_element_type=jnp.float32)
        query_sums = query_sums.reshape(tok_rows * head_count, head_size)
        queries = normalized(query_sums, query_gain[0]).astype(jnp.bfloat16)
        scores = jnp.dot(queries, own_keys.T, preferred_element_type=jnp.float32) / root_size
        exponent = jnp.exp(scores)
        probs = (exponent / jnp.sum(exponent, axis=-1, keepdims=True)).astype(jnp.bfloat16)
        attended = jnp.dot(probs, own_values, preferred_element_type=jnp.float32).astype(
            jnp.bfloat16
        )
        attended = attended.reshape(tok_rows, head_count * head_size)
        update = jnp.dot(attended, out_weight, preferred_element_type=jnp.float32)
        first_seen = lax.dynamic_index_in_dim(image_start[:, 0], holding, 0, keepdims=False)
        seen = (positions >= first_seen).astype(jnp.float32)[:, None]
        return (current.astype(jnp.float32) + factor * seen * update).astype(jnp.bfloat16)

    current = text_states[0]
    for moment in range(sections):
        holding = jnp.mod(section_index - moment, sections)
        current = lax.cond(moment <= section_index, apply_layer, keep_state, current, holding)
        current = shifted(current, "pipe", 1)
    return current[None]


def kernel(
    lines,
    text_ref,
    image_ref,
    start_ref,
    wq_ref,
    wk_ref,
    wv_ref,
    wo_ref,
    qg_ref,
    kg_ref,
    gate_ref,
    out_ref,
    text_v,
    wq_v,
    wq_half,
    wo_v,
    joint_sum,
    joint,
    first,
    mixed,
    back,
    wkv,
    image_v,
    img,
    part,
    part_out,
    part_in,
    query_v,
    small,
    query_gain,
    key_gain,
    starts,
    load_sem,
    w_send,
    w_recv,
    i_send,
    i_recv,
    relay_send,
    relay_recv,
    big_send,
    big_recv,
    one_send,
    one_recv,
    back_send,
    back_recv,
    p_send,
    p_recv,
):
    place = lax.axis_index("dp")
    core = lax.axis_index("pipe")
    other = 1 - core
    line = place // QUAD
    spot = place % QUAD
    depth = wk_ref.shape[1]
    head = wk_ref.shape[2]
    tokens, width = text_v.shape[1:]
    heads = wq_ref.shape[2] // head
    image_rows = image_ref.shape[1]
    span = QUAD * depth

    def quad_peer(distance):
        return line * QUAD + (spot + distance) % QUAD

    def line_peer(distance):
        return ((line + distance) % lines) * QUAD + spot

    def rows_of(index):
        return pl.ds(pl.multiple_of(index * depth, depth), depth)

    own_rows = pl.ds(pl.multiple_of(core * image_rows, image_rows), image_rows)

    def columns_of(index):
        return pl.ds(pl.multiple_of(index * span, span), span)

    loads = [
        pltpu.make_async_copy(wk_ref.at[0], wkv.at[0, rows_of(spot), pl.ds(0, head)], load_sem.at[0]),
        pltpu.make_async_copy(wv_ref.at[0], wkv.at[0, rows_of(spot), pl.ds(head, head)], load_sem.at[1]),
        pltpu.make_async_copy(image_ref, image_v, load_sem.at[2]),
        pltpu.make_async_copy(image_ref.at[core, :, columns_of(line)], img.at[line, own_rows], load_sem.at[3]),
        pltpu.make_async_copy(qg_ref, query_gain, load_sem.at[4]),
        pltpu.make_async_copy(kg_ref, key_gain, load_sem.at[5]),
        pltpu.make_async_copy(start_ref, starts, load_sem.at[6]),
        pltpu.make_async_copy(text_ref.at[0], text_v.at[0], load_sem.at[7]),
        pltpu.make_async_copy(wq_ref.at[0], wq_v, load_sem.at[8]),
    ]
    for load in loads:
        load.start()

    barrier = pltpu.get_barrier_semaphore()
    peers = [(quad_peer(d), core) for d in range(1, QUAD)]
    peers += [(line_peer(d), side) for d in range(1, lines) for side in (core, other)]
    peers += [(place, other)]
    for peer in peers:
        pl.semaphore_signal(barrier, inc=1, device_id=peer, device_id_type=MESH)
    for load in loads[:3]:
        load.wait()
    pl.semaphore_wait(barrier, len(peers))

    weight_copies = [
        pltpu.make_async_remote_copy(
            src_ref=wkv.at[0, rows_of(spot)],
            dst_ref=wkv.at[0, rows_of(spot)],
            send_sem=w_send.at[distance],
            recv_sem=w_recv.at[distance],
            device_id=(quad_peer(distance), core),
            device_id_type=MESH,
        )
        for distance in range(1, QUAD)
    ]
    image_copies = [
        pltpu.make_async_remote_copy(
            src_ref=image_v.at[side, :, columns_of((line + distance) % lines)],
            dst_ref=img.at[line, own_rows],
            send_sem=i_send.at[distance, turn],
            recv_sem=i_recv.at[distance, turn],
            device_id=(line_peer(distance), side),
            device_id_type=MESH,
        )
        for distance in (*range(1, lines), 0)
        for turn, side in enumerate((core, other))
        if distance + turn > 0
    ]
    for i in range(QUAD - 1):
        weight_copies[i].start()
        for copy in image_copies[2 * i : 2 * i + 2]:
            copy.start()
    for copy in image_copies[2 * QUAD - 2 :]:
        copy.start()

    def across(src, dst, send, recv):
        return pltpu.make_async_remote_copy(
            src_ref=src,
            dst_ref=dst,
            send_sem=send,
            recv_sem=recv,
            device_id=(place, other),
            device_id_type=MESH,
        )

    stretch = width // PIECES
    out_pieces = [
        across(
            wo_ref.at[0, :, pl.ds(i * stretch, stretch)],
            wo_v.at[1, :, pl.ds(i * stretch, stretch)],
            big_send.at[0, i],
            big_recv.at[0, i],
        )
        for i in range(PIECES)
    ]
    half = PIECES // 2
    most = PIECES - 1
    query_pieces = [
        across(
            wq_ref.at[0, pl.ds(i * stretch, stretch)],
            wq_half.at[pl.ds(i * stretch, stretch)],
            big_send.at[1, i],
            big_recv.at[1, i],
        )
        for i in range(most)
    ]
    small_copy = across(small.at[0], small.at[1], one_send.at[0], one_recv.at[0])
    text_copy = across(text_ref.at[0], text_v.at[1], one_send.at[1], one_recv.at[1])
    first_copy = across(first.at[0], first.at[1], one_send.at[2], one_recv.at[2])
    joint_copy = across(joint.at[0], joint.at[1], one_send.at[3], one_recv.at[3])
    mixed_copies = [across(mixed.at[i], mixed.at[2 + i], one_send.at[4 + i], one_recv.at[4 + i]) for i in range(2)]
    quarter = stretch // 2
    back_copies = [
        across(
            back.at[:, pl.ds(i * quarter, quarter)],
            out_ref.at[0, :, pl.ds((PIECES + i) * quarter, quarter)],
            back_send.at[i],
            back_recv.at[i],
        )
        for i in range(PIECES)
    ]

    def relay(distance):
        rows = rows_of((spot + QUAD - distance) % QUAD)
        return across(wkv.at[0, rows], wkv.at[1, rows], relay_send.at[distance], relay_recv.at[distance])

    loads[4].wait()
    loads[5].wait()
    small[0, 0:1] = query_gain[...]
    small[0, 1:2] = key_gain[...]
    small[0, 2:3] = jnp.full((1, head), gate_ref[0], jnp.float32)

    small_copy.start()
    out_loads = [
        pltpu.make_async_copy(
            wo_ref.at[0, :, pl.ds(i * stretch, stretch)], wo_v.at[0, :, pl.ds(i * stretch, stretch)], load_sem.at[9 + i]
        )
        for i in range(PIECES)
    ]

    @pl.when(core == 0)
    def _():
        text_copy.start()
        for piece in reversed(out_pieces[half:]):
            piece.start()
        for load in out_loads[:most]:
            load.start()

    @pl.when(core == 1)
    def _():
        query_pieces[0].start()
        relay(0).start()
        for piece in query_pieces[1:]:
            piece.start()

    chunk = 512

    def project(slots):
        rows = slots * tokens

        def step(i, total):
            at = pl.ds(pl.multiple_of(i * chunk, chunk), chunk)
            return total + jnp.dot(
                text_v[:slots, :, at].reshape(rows, chunk), wq_v[at, :], preferred_element_type=jnp.float32
            )

        return lax.fori_loop(0, width // chunk, step, jnp.zeros((rows, heads * head), jnp.float32))

    def store_queries(sums, slot):
        for h in range(heads):
            query_v[h * tokens : (h + 1) * tokens, :] = normalized(
                sums[:, h * head : (h + 1) * head], small[slot, 0:1]
            ).astype(jnp.bfloat16)

    def join(left, right):
        return jnp.dot(left, right, preferred_element_type=jnp.float32)

    loads[7].wait()
    loads[8].wait()

    def partial_sums(slot):
        groups = 2 * image_rows
        sums = jnp.dot(
            img[...].reshape(lines * groups, span), wkv[slot], preferred_element_type=jnp.float32
        )
        sums = sums.reshape(lines, groups, 2 * head)
        part[:, slot] = sums
        part_out[:, slot] = sums.astype(jnp.bfloat16)

    def partial_copy(slot, distance):
        return pltpu.make_async_remote_copy(
            src_ref=part_out.at[(line + distance) % lines, slot],
            dst_ref=part_in.at[line, slot],
            send_sem=p_send.at[slot, distance],
            recv_sem=p_recv.at[slot, distance],
            device_id=(line_peer(distance), core),
            device_id_type=MESH,
        )

    def arrived():
        loads[3].wait()
        for copy in image_copies:
            copy.wait_recv()

    def return_partials(slot):
        partial_sums(slot)
        for distance in range(1, lines):
            partial_copy(slot, distance).start()

    @pl.when(core == 0)
    def _():
        def join_own(i):
            out_loads[i].wait()
            query_pieces[i].wait_recv()
            at = pl.ds(i * stretch, stretch)
            return join(wo_v[0, :, at], wq_half[at, :])

        store_queries(project(1), 0)
        joint_sum[...] = join_own(0)
        for copy in weight_copies:
            copy.wait_recv()
        arrived()
        return_partials(0)
        for i in range(1, most - 1):
            joint_sum[...] += join_own(i)
        for distance in range(QUAD):
            relay(distance).wait_recv()
        return_partials(1)
        joint[0] = (joint_sum[...] + join_own(most - 1)).astype(jnp.bfloat16)
        small_copy.wait_recv()
        first_copy.wait_recv()

    @pl.when(core == 1)
    def _():
        text_copy.wait_recv()
        sums = project(2)
        store_queries(sums[:tokens], 0)
        first[0] = sums[tokens:]
        first_copy.start()
        for load in out_loads:
            load.start()
        for distance in range(1, QUAD):
            weight_copies[distance - 1].wait_recv()
            relay(distance).start()
        for piece in out_pieces[:half]:
            piece.start()
        arrived()
        return_partials(0)
        out_pieces[most].wait_recv()
        at = pl.ds(most * stretch, stretch)
        joint[0] = join(wo_v[1, :, at], wq_v[at, :]).astype(jnp.bfloat16)
        joint_copy.start()
        for load in out_loads:
            load.wait()
        small_copy.wait_recv()

    positions = lax.broadcasted_iota(jnp.int32, (tokens, 1), 0)
    loads[6].wait()
    seen = (positions >= starts[core]).astype(jnp.float32)
    seen_other = (positions >= starts[other]).astype(jnp.float32)
    root_size = math.sqrt(head)

    def attend(slot):
        total = part[line, slot]
        for distance in range(1, lines):
            partial_copy(slot, distance).wait_recv()
            total += part_in[(line + lines - distance) % lines, slot].astype(jnp.float32)
        keys = normalized(total[:, :head], small[slot, 1:2]).astype(jnp.bfloat16)
        values = total[:, head:].astype(jnp.bfloat16)
        scores = (
            lax.dot_general(
                query_v[...], keys, (((1,), (1,)), ((), ())), preferred_element_type=jnp.float32
            )
            / root_size
        )
        exponent = jnp.exp(scores)
        probs = (exponent / jnp.sum(exponent, axis=-1, keepdims=True)).astype(jnp.bfloat16)
        attended = jnp.dot(probs, values, preferred_element_type=jnp.float32).astype(jnp.bfloat16)
        attended = jnp.concatenate(
            [attended[h * tokens : (h + 1) * tokens] for h in range(heads)], axis=1
        )
        return attended

    def gate(slot):
        return jnp.tanh(small[slot, 2:3])[:, 0:1]

    def update(values, slot, at):
        return jnp.dot(values, wo_v[slot, :, at], preferred_element_type=jnp.float32)

    def advance(source, slot, attended, factor):
        for i in range(PIECES):
            at = pl.ds(i * quarter, quarter)
            out_ref[0, :, at] = (source[:, at].astype(jnp.float32) + factor * update(attended, slot, at)).astype(
                jnp.bfloat16
            )

    attended = attend(0)
    factor = gate(0) * seen

    @pl.when(core == 0)
    def _():
        mixed[0] = attended
        mixed_copies[0].start()
        change = jnp.dot(attended, joint[0], preferred_element_type=jnp.float32)
        joint_copy.wait_recv()
        change += jnp.dot(attended, joint[1], preferred_element_type=jnp.float32)
        store_queries(first[1] + factor * change, 1)
        later = attend(1)
        mixed[1] = later
        mixed_copies[1].start()
        advance(text_v.at[0], 0, attended, factor)
        for piece in out_pieces[:half]:
            piece.wait_recv()
        advance(out_ref.at[0], 1, later, gate(1) * seen)
        for copy in back_copies:
            copy.wait_recv()

    @pl.when(core == 1)
    def _():
        advance(text_v.at[0], 0, attended, factor)
        for piece in out_pieces[half:most]:
            piece.wait_recv()
        mixed_copies[0].wait_recv()
        before = gate(1) * seen_other
        for i in range(PIECES):
            at = pl.ds((PIECES + i) * quarter, quarter)
            back[:, i * quarter : (i + 1) * quarter] = (
                text_v[1, :, at].astype(jnp.float32) + before * update(mixed[2], 1, at)
            ).astype(jnp.bfloat16)
        mixed_copies[1].wait_recv()
        both = jnp.concatenate([attended, mixed[3]], axis=0)
        after = gate(0) * seen_other
        for i in range(PIECES):
            at = pl.ds((PIECES + i) * quarter, quarter)
            here = pl.ds(i * quarter, quarter)
            sums = update(both, 0, at)
            back[:, here] = (back[:, here].astype(jnp.float32) + after * sums[tokens:]).astype(jnp.bfloat16)
            back_copies[i].start()
            out_ref[0, :, at] = (text_v[0, :, at].astype(jnp.float32) + factor * sums[:tokens]).astype(jnp.bfloat16)

    for copy in image_copies + weight_copies:
        copy.wait_send()
    for distance in range(1, lines):
        partial_copy(0, distance).wait_send()

    small_copy.wait_send()

    @pl.when(core == 0)
    def _():
        for distance in range(1, lines):
            partial_copy(1, distance).wait_send()
        for copy in [text_copy] + mixed_copies + out_pieces[half:]:
            copy.wait_send()

    @pl.when(core == 1)
    def _():
        for distance in range(QUAD):
            relay(distance).wait_send()
        for copy in [first_copy, joint_copy] + query_pieces + out_pieces[:half] + back_copies:
            copy.wait_send()


def local_fused(
    text_states,
    image_states,
    image_start,
    w_query,
    w_key,
    w_value,
    w_out,
    query_gain,
    key_gain,
    cross_gate,
):
    lines = lax.axis_size("dp") // QUAD
    tokens, width = text_states.shape[1:]
    image_rows = image_states.shape[1]
    depth, head = w_key.shape[1:]
    columns = w_query.shape[2]
    heads = columns // head
    span = QUAD * depth
    groups = 2 * image_rows
    hbm = pl.BlockSpec(memory_space=pltpu.HBM)
    vmem = pl.BlockSpec(memory_space=pltpu.VMEM)
    smem = pl.BlockSpec(memory_space=pltpu.SMEM)
    dma = pltpu.SemaphoreType.DMA
    return pl.pallas_call(
        functools.partial(kernel, lines),
        out_shape=jax.ShapeDtypeStruct((1, tokens, width), jnp.bfloat16),
        in_specs=[hbm, hbm, hbm, hbm, hbm, hbm, hbm, hbm, hbm, smem],
        out_specs=vmem,
        scratch_shapes=[
            pltpu.VMEM((2, tokens, width), jnp.bfloat16),
            pltpu.VMEM((width, columns), jnp.bfloat16),
            pltpu.VMEM((width - width // PIECES, columns), jnp.bfloat16),
            pltpu.VMEM((2, columns, width), jnp.bfloat16),
            pltpu.VMEM((columns, columns), jnp.float32),
            pltpu.VMEM((2, columns, columns), jnp.bfloat16),
            pltpu.VMEM((2, tokens, columns), jnp.float32),
            pltpu.VMEM((4, tokens, columns), jnp.bfloat16),
            pltpu.VMEM((tokens, width // 2), jnp.bfloat16),
            pltpu.VMEM((2, span, 2 * head), jnp.bfloat16),
            pltpu.VMEM((2, image_rows, width), jnp.bfloat16),
            pltpu.VMEM((lines, groups, span), jnp.bfloat16),
            pltpu.VMEM((lines, 2, groups, 2 * head), jnp.float32),
            pltpu.VMEM((lines, 2, groups, 2 * head), jnp.bfloat16),
            pltpu.VMEM((lines, 2, groups, 2 * head), jnp.bfloat16),
            pltpu.VMEM((heads * tokens, head), jnp.bfloat16),
            pltpu.VMEM((2, 8, head), jnp.float32),
            pltpu.VMEM((1, head), jnp.float32),
            pltpu.VMEM((1, head), jnp.float32),
            pltpu.SMEM(image_start.shape[:1], jnp.int32),
            dma((9 + PIECES,)),
            dma((QUAD,)),
            dma((QUAD,)),
            dma((lines, 2)),
            dma((lines, 2)),
            dma((QUAD,)),
            dma((QUAD,)),
            dma((2, PIECES)),
            dma((2, PIECES)),
            dma((6,)),
            dma((6,)),
            dma((PIECES,)),
            dma((PIECES,)),
            dma((2, lines)),
            dma((2, lines)),
        ],
        compiler_params=pltpu.CompilerParams(
            collective_id=0, has_side_effects=True, vmem_limit_bytes=48 * 2**20
        ),
    )(
        pltpu.with_memory_space_constraint(text_states, pltpu.HBM),
        pltpu.with_memory_space_constraint(image_states, pltpu.HBM),
        pltpu.with_memory_space_constraint(image_start.reshape(-1), pltpu.HBM),
        pltpu.with_memory_space_constraint(w_query, pltpu.HBM),
        pltpu.with_memory_space_constraint(w_key, pltpu.HBM),
        pltpu.with_memory_space_constraint(w_value, pltpu.HBM),
        pltpu.with_memory_space_constraint(w_out, pltpu.HBM),
        pltpu.with_memory_space_constraint(query_gain, pltpu.HBM),
        pltpu.with_memory_space_constraint(key_gain, pltpu.HBM),
        cross_gate,
    )


def solution(mesh):
    placed = (
        P("pipe", "dp", None),
        P(None, ("dp", "pipe"), None),
        P(None, "dp"),
        P("pipe", None, None),
        P("pipe", "dp", None),
        P("pipe", "dp", None),
        P("pipe", None, None),
        P("pipe", None),
        P("pipe", None),
        P("pipe"),
    )
    fits = mesh.shape["pipe"] == 2 and mesh.shape["dp"] == QUAD * QUAD
    return jax.shard_map(
        local_fused if fits else local,
        mesh=mesh,
        in_specs=placed,
        out_specs=P("pipe", "dp", None),
        check_vma=False,
    )
```

```python
import functools
import math

import jax
import jax.numpy as jnp
from jax import lax
from jax.experimental import pallas as pl
from jax.experimental.pallas import tpu as pltpu
from jax.sharding import PartitionSpec as P

epsilon = 1e-06
MESH = pl.DeviceIdType.MESH
QUAD = 4
PIECES = 4


def shifted(block, axis, distance):
    devices = range(lax.axis_size(axis))
    route = [((i - distance) % len(devices), i) for i in devices]
    return lax.ppermute(block, axis, route)


def normalized(projected, scales):
    mean_square = jnp.mean(projected * projected, axis=-1, keepdims=True)
    return projected * lax.rsqrt(mean_square + epsilon) * scales


def keep_state(current, holding):
    return current


def local(
    text_states,
    image_states,
    image_start,
    w_query,
    w_key,
    w_value,
    w_out,
    query_gain,
    key_gain,
    cross_gate,
):
    sections = lax.axis_size("pipe")
    section_index = lax.axis_index("pipe")
    pictures = lax.all_gather(image_states, "pipe", axis=1, tiled=True)
    batches, image_rows, width = pictures.shape
    flattened = pictures.reshape(batches * image_rows, width)
    head_size = w_key.shape[2]
    head_count = w_query.shape[2] // head_size
    key_full, value_full = (
        lax.all_gather(w_key, "dp", axis=1, tiled=True),
        lax.all_gather(w_value, "dp", axis=1, tiled=True),
    )
    key_sums = jnp.dot(flattened, key_full[0], preferred_element_type=jnp.float32)
    value_sums = jnp.dot(flattened, value_full[0], preferred_element_type=jnp.float32)
    key_rows = (
        normalized(key_sums, key_gain[0])
        .astype(jnp.bfloat16)
        .reshape(batches, image_rows, head_size)
    )
    value_rows = value_sums.astype(jnp.bfloat16).reshape(batches, image_rows, head_size)
    query_weight = w_query[0]
    out_weight = w_out[0]
    factor = jnp.tanh(cross_gate[0])
    tok_rows = text_states.shape[1]
    positions = jnp.arange(tok_rows, dtype=jnp.int32)
    root_size = math.sqrt(head_size)

    def apply_layer(current, holding):
        own_keys = lax.dynamic_index_in_dim(key_rows, holding, 0, keepdims=False)
        own_values = lax.dynamic_index_in_dim(value_rows, holding, 0, keepdims=False)
        query_sums = jnp.dot(current, query_weight, preferred_element_type=jnp.float32)
        query_sums = query_sums.reshape(tok_rows * head_count, head_size)
        queries = normalized(query_sums, query_gain[0]).astype(jnp.bfloat16)
        scores = jnp.dot(queries, own_keys.T, preferred_element_type=jnp.float32) / root_size
        exponent = jnp.exp(scores)
        probs = (exponent / jnp.sum(exponent, axis=-1, keepdims=True)).astype(jnp.bfloat16)
        attended = jnp.dot(probs, own_values, preferred_element_type=jnp.float32).astype(
            jnp.bfloat16
        )
        attended = attended.reshape(tok_rows, head_count * head_size)
        update = jnp.dot(attended, out_weight, preferred_element_type=jnp.float32)
        first_seen = lax.dynamic_index_in_dim(image_start[:, 0], holding, 0, keepdims=False)
        seen = (positions >= first_seen).astype(jnp.float32)[:, None]
        return (current.astype(jnp.float32) + factor * seen * update).astype(jnp.bfloat16)

    current = text_states[0]
    for moment in range(sections):
        holding = jnp.mod(section_index - moment, sections)
        current = lax.cond(moment <= section_index, apply_layer, keep_state, current, holding)
        current = shifted(current, "pipe", 1)
    return current[None]


def kernel(
    lines,
    text_ref,
    image_ref,
    start_ref,
    wq_ref,
    wk_ref,
    wv_ref,
    wo_ref,
    qg_ref,
    kg_ref,
    gate_ref,
    out_ref,
    text_v,
    wq_v,
    wq_half,
    wo_v,
    joint_sum,
    joint,
    first,
    mixed,
    back,
    wkv,
    image_v,
    img,
    part,
    part_out,
    part_in,
    query_v,
    small,
    query_gain,
    key_gain,
    starts,
    own_gate,
    load_sem,
    w_send,
    w_recv,
    i_send,
    i_recv,
    relay_send,
    relay_recv,
    big_send,
    big_recv,
    one_send,
    one_recv,
    back_send,
    back_recv,
    p_send,
    p_recv,
):
    place = lax.axis_index("dp")
    core = lax.axis_index("pipe")
    other = 1 - core
    line = place // QUAD
    spot = place % QUAD
    depth = wk_ref.shape[1]
    head = wk_ref.shape[2]
    tokens, width = text_v.shape[1:]
    heads = wq_ref.shape[2] // head
    image_rows = image_ref.shape[1]
    span = QUAD * depth

    def quad_peer(distance):
        return line * QUAD + (spot + distance) % QUAD

    def line_peer(distance):
        return ((line + distance) % lines) * QUAD + spot

    def rows_of(index):
        return pl.ds(pl.multiple_of(index * depth, depth), depth)

    own_rows = pl.ds(pl.multiple_of(core * image_rows, image_rows), image_rows)

    def columns_of(index):
        return pl.ds(pl.multiple_of(index * span, span), span)

    loads = [
        pltpu.make_async_copy(wk_ref.at[0], wkv.at[0, rows_of(spot), pl.ds(0, head)], load_sem.at[0]),
        pltpu.make_async_copy(wv_ref.at[0], wkv.at[0, rows_of(spot), pl.ds(head, head)], load_sem.at[1]),
        pltpu.make_async_copy(image_ref, image_v, load_sem.at[2]),
        pltpu.make_async_copy(image_ref.at[core, :, columns_of(line)], img.at[line, own_rows], load_sem.at[3]),
        pltpu.make_async_copy(qg_ref, query_gain, load_sem.at[4]),
        pltpu.make_async_copy(kg_ref, key_gain, load_sem.at[5]),
        pltpu.make_async_copy(start_ref, starts, load_sem.at[6]),
        pltpu.make_async_copy(text_ref.at[0], text_v.at[0], load_sem.at[7]),
        pltpu.make_async_copy(wq_ref.at[0], wq_v, load_sem.at[8]),
        pltpu.make_async_copy(gate_ref, own_gate, load_sem.at[9]),
    ]
    for load in loads:
        load.start()

    barrier = pltpu.get_barrier_semaphore()
    peers = [(quad_peer(d), core) for d in range(1, QUAD)]
    peers += [(line_peer(d), side) for d in range(1, lines) for side in (core, other)]
    peers += [(place, other)]
    for peer in peers:
        pl.semaphore_signal(barrier, inc=1, device_id=peer, device_id_type=MESH)
    for load in loads[:3]:
        load.wait()
    pl.semaphore_wait(barrier, len(peers))

    weight_copies = [
        pltpu.make_async_remote_copy(
            src_ref=wkv.at[0, rows_of(spot)],
            dst_ref=wkv.at[0, rows_of(spot)],
            send_sem=w_send.at[distance],
            recv_sem=w_recv.at[distance],
            device_id=(quad_peer(distance), core),
            device_id_type=MESH,
        )
        for distance in range(1, QUAD)
    ]
    image_copies = [
        pltpu.make_async_remote_copy(
            src_ref=image_v.at[side, :, columns_of((line + distance) % lines)],
            dst_ref=img.at[line, own_rows],
            send_sem=i_send.at[distance, turn],
            recv_sem=i_recv.at[distance, turn],
            device_id=(line_peer(distance), side),
            device_id_type=MESH,
        )
        for distance in (*range(1, lines), 0)
        for turn, side in enumerate((core, other))
        if distance + turn > 0
    ]
    for i in range(QUAD - 1):
        weight_copies[i].start()
        for copy in image_copies[2 * i : 2 * i + 2]:
            copy.start()
    for copy in image_copies[2 * QUAD - 2 :]:
        copy.start()

    def across(src, dst, send, recv):
        return pltpu.make_async_remote_copy(
            src_ref=src,
            dst_ref=dst,
            send_sem=send,
            recv_sem=recv,
            device_id=(place, other),
            device_id_type=MESH,
        )

    stretch = width // PIECES
    out_pieces = [
        across(
            wo_ref.at[0, :, pl.ds(i * stretch, stretch)],
            wo_v.at[1, :, pl.ds(i * stretch, stretch)],
            big_send.at[0, i],
            big_recv.at[0, i],
        )
        for i in range(PIECES)
    ]
    half = PIECES // 2
    most = PIECES - 1
    query_pieces = [
        across(
            wq_ref.at[0, pl.ds(i * stretch, stretch)],
            wq_half.at[pl.ds(i * stretch, stretch)],
            big_send.at[1, i],
            big_recv.at[1, i],
        )
        for i in range(most)
    ]
    small_copy = across(small.at[0], small.at[1], one_send.at[0], one_recv.at[0])
    text_copy = across(text_ref.at[0], text_v.at[1], one_send.at[1], one_recv.at[1])
    first_copy = across(first.at[0], first.at[1], one_send.at[2], one_recv.at[2])
    joint_copy = across(joint.at[0], joint.at[1], one_send.at[3], one_recv.at[3])
    mixed_copies = [across(mixed.at[i], mixed.at[2 + i], one_send.at[4 + i], one_recv.at[4 + i]) for i in range(2)]
    quarter = stretch // 2
    back_copies = [
        across(
            back.at[:, pl.ds(i * quarter, quarter)],
            out_ref.at[0, :, pl.ds((PIECES + i) * quarter, quarter)],
            back_send.at[i],
            back_recv.at[i],
        )
        for i in range(PIECES)
    ]

    def relay(distance):
        rows = rows_of((spot + QUAD - distance) % QUAD)
        return across(wkv.at[0, rows], wkv.at[1, rows], relay_send.at[distance], relay_recv.at[distance])

    loads[4].wait()
    loads[5].wait()
    loads[9].wait()
    small[0, 0:1] = query_gain[...]
    small[0, 1:2] = key_gain[...]
    small[0, 2:3] = own_gate[...]

    small_copy.start()
    out_loads = [
        pltpu.make_async_copy(
            wo_ref.at[0, :, pl.ds(i * stretch, stretch)], wo_v.at[0, :, pl.ds(i * stretch, stretch)], load_sem.at[10 + i]
        )
        for i in range(PIECES)
    ]

    @pl.when(core == 0)
    def _():
        text_copy.start()
        for piece in reversed(out_pieces[half:]):
            piece.start()
        for load in out_loads[:most]:
            load.start()

    @pl.when(core == 1)
    def _():
        query_pieces[0].start()
        relay(0).start()
        for piece in query_pieces[1:]:
            piece.start()

    chunk = 2048

    def project(slots):
        rows = slots * tokens

        def step(i, total):
            at = pl.ds(pl.multiple_of(i * chunk, chunk), chunk)
            return total + jnp.dot(
                text_v[:slots, :, at].reshape(rows, chunk), wq_v[at, :], preferred_element_type=jnp.float32
            )

        return lax.fori_loop(0, width // chunk, step, jnp.zeros((rows, heads * head), jnp.float32))

    def store_queries(sums, slot):
        for h in range(heads):
            query_v[h * tokens : (h + 1) * tokens, :] = normalized(
                sums[:, h * head : (h + 1) * head], small[slot, 0:1]
            ).astype(jnp.bfloat16)

    def join(left, right):
        return jnp.dot(left, right, preferred_element_type=jnp.float32)

    loads[7].wait()
    loads[8].wait()

    def partial_sums(slot):
        groups = 2 * image_rows
        sums = jnp.dot(
            img[...].reshape(lines * groups, span), wkv[slot], preferred_element_type=jnp.float32
        )
        sums = sums.reshape(lines, groups, 2 * head)
        part[:, slot] = sums
        part_out[:, slot] = sums.astype(jnp.bfloat16)

    def partial_copy(slot, distance):
        return pltpu.make_async_remote_copy(
            src_ref=part_out.at[(line + distance) % lines, slot],
            dst_ref=part_in.at[line, slot],
            send_sem=p_send.at[slot, distance],
            recv_sem=p_recv.at[slot, distance],
            device_id=(line_peer(distance), core),
            device_id_type=MESH,
        )

    def arrived():
        loads[3].wait()
        for copy in image_copies:
            copy.wait_recv()

    def return_partials(slot):
        partial_sums(slot)
        for distance in range(1, lines):
            partial_copy(slot, distance).start()

    @pl.when(core == 0)
    def _():
        def join_own(i):
            out_loads[i].wait()
            query_pieces[i].wait_recv()
            at = pl.ds(i * stretch, stretch)
            return join(wo_v[0, :, at], wq_half[at, :])

        store_queries(project(1), 0)
        joint_sum[...] = join_own(0)
        for copy in weight_copies:
            copy.wait_recv()
        arrived()
        return_partials(0)
        for i in range(1, most - 1):
            joint_sum[...] += join_own(i)
        for distance in range(QUAD):
            relay(distance).wait_recv()
        return_partials(1)
        joint[0] = (joint_sum[...] + join_own(most - 1)).astype(jnp.bfloat16)
        small_copy.wait_recv()
        first_copy.wait_recv()

    @pl.when(core == 1)
    def _():
        text_copy.wait_recv()
        sums = project(2)
        store_queries(sums[:tokens], 0)
        first[0] = sums[tokens:]
        first_copy.start()
        for load in out_loads:
            load.start()
        for distance in range(1, QUAD):
            weight_copies[distance - 1].wait_recv()
            relay(distance).start()
        for piece in out_pieces[:half]:
            piece.start()
        arrived()
        return_partials(0)
        out_pieces[most].wait_recv()
        at = pl.ds(most * stretch, stretch)
        joint[0] = join(wo_v[1, :, at], wq_v[at, :]).astype(jnp.bfloat16)
        joint_copy.start()
        for load in out_loads:
            load.wait()
        small_copy.wait_recv()

    positions = lax.broadcasted_iota(jnp.int32, (tokens, 1), 0)
    loads[6].wait()
    seen = (positions >= starts[core]).astype(jnp.float32)
    seen_other = (positions >= starts[other]).astype(jnp.float32)
    root_size = math.sqrt(head)

    def attend(slot):
        total = part[line, slot]
        for distance in range(1, lines):
            partial_copy(slot, distance).wait_recv()
            total += part_in[(line + lines - distance) % lines, slot].astype(jnp.float32)
        keys = normalized(total[:, :head], small[slot, 1:2]).astype(jnp.bfloat16)
        values = total[:, head:].astype(jnp.bfloat16)
        scores = (
            lax.dot_general(
                query_v[...], keys, (((1,), (1,)), ((), ())), preferred_element_type=jnp.float32
            )
            / root_size
        )
        exponent = jnp.exp(scores)
        probs = (exponent / jnp.sum(exponent, axis=-1, keepdims=True)).astype(jnp.bfloat16)
        attended = jnp.dot(probs, values, preferred_element_type=jnp.float32).astype(jnp.bfloat16)
        attended = jnp.concatenate(
            [attended[h * tokens : (h + 1) * tokens] for h in range(heads)], axis=1
        )
        return attended

    def gate(slot):
        return jnp.tanh(small[slot, 2:3])[:, 0:1]

    def update(values, slot, at):
        return jnp.dot(values, wo_v[slot, :, at], preferred_element_type=jnp.float32)

    def advance(source, slot, attended, factor):
        for i in range(PIECES):
            at = pl.ds(i * quarter, quarter)
            out_ref[0, :, at] = (source[:, at].astype(jnp.float32) + factor * update(attended, slot, at)).astype(
                jnp.bfloat16
            )

    attended = attend(0)
    factor = gate(0) * seen

    @pl.when(core == 0)
    def _():
        mixed[0] = attended
        mixed_copies[0].start()
        change = jnp.dot(attended, joint[0], preferred_element_type=jnp.float32)
        joint_copy.wait_recv()
        change += jnp.dot(attended, joint[1], preferred_element_type=jnp.float32)
        store_queries(first[1] + factor * change, 1)
        later = attend(1)
        mixed[1] = later
        mixed_copies[1].start()
        advance(text_v.at[0], 0, attended, factor)
        for piece in out_pieces[:half]:
            piece.wait_recv()
        advance(out_ref.at[0], 1, later, gate(1) * seen)
        for copy in back_copies:
            copy.wait_recv()

    @pl.when(core == 1)
    def _():
        advance(text_v.at[0], 0, attended, factor)
        for piece in out_pieces[half:most]:
            piece.wait_recv()
        mixed_copies[0].wait_recv()
        before = gate(1) * seen_other
        for i in range(PIECES):
            at = pl.ds((PIECES + i) * quarter, quarter)
            back[:, i * quarter : (i + 1) * quarter] = (
                text_v[1, :, at].astype(jnp.float32) + before * update(mixed[2], 1, at)
            ).astype(jnp.bfloat16)
        mixed_copies[1].wait_recv()
        both = jnp.concatenate([attended, mixed[3]], axis=0)
        after = gate(0) * seen_other
        for i in range(PIECES):
            at = pl.ds((PIECES + i) * quarter, quarter)
            here = pl.ds(i * quarter, quarter)
            sums = update(both, 0, at)
            back[:, here] = (back[:, here].astype(jnp.float32) + after * sums[tokens:]).astype(jnp.bfloat16)
            back_copies[i].start()
            out_ref[0, :, at] = (text_v[0, :, at].astype(jnp.float32) + factor * sums[:tokens]).astype(jnp.bfloat16)

    for copy in image_copies + weight_copies:
        copy.wait_send()
    for distance in range(1, lines):
        partial_copy(0, distance).wait_send()

    small_copy.wait_send()

    @pl.when(core == 0)
    def _():
        for distance in range(1, lines):
            partial_copy(1, distance).wait_send()
        for copy in [text_copy] + mixed_copies + out_pieces[half:]:
            copy.wait_send()

    @pl.when(core == 1)
    def _():
        for distance in range(QUAD):
            relay(distance).wait_send()
        for copy in [first_copy, joint_copy] + query_pieces + out_pieces[:half] + back_copies:
            copy.wait_send()


def local_fused(
    text_states,
    image_states,
    image_start,
    w_query,
    w_key,
    w_value,
    w_out,
    query_gain,
    key_gain,
    cross_gate,
):
    lines = lax.axis_size("dp") // QUAD
    tokens, width = text_states.shape[1:]
    image_rows = image_states.shape[1]
    depth, head = w_key.shape[1:]
    columns = w_query.shape[2]
    heads = columns // head
    span = QUAD * depth
    groups = 2 * image_rows
    hbm = pl.BlockSpec(memory_space=pltpu.HBM)
    vmem = pl.BlockSpec(memory_space=pltpu.VMEM)
    dma = pltpu.SemaphoreType.DMA
    return pl.pallas_call(
        functools.partial(kernel, lines),
        out_shape=jax.ShapeDtypeStruct((1, tokens, width), jnp.bfloat16),
        in_specs=[hbm] * 10,
        out_specs=vmem,
        scratch_shapes=[
            pltpu.VMEM((2, tokens, width), jnp.bfloat16),
            pltpu.VMEM((width, columns), jnp.bfloat16),
            pltpu.VMEM((width - width // PIECES, columns), jnp.bfloat16),
            pltpu.VMEM((2, columns, width), jnp.bfloat16),
            pltpu.VMEM((columns, columns), jnp.float32),
            pltpu.VMEM((2, columns, columns), jnp.bfloat16),
            pltpu.VMEM((2, tokens, columns), jnp.float32),
            pltpu.VMEM((4, tokens, columns), jnp.bfloat16),
            pltpu.VMEM((tokens, width // 2), jnp.bfloat16),
            pltpu.VMEM((2, span, 2 * head), jnp.bfloat16),
            pltpu.VMEM((2, image_rows, width), jnp.bfloat16),
            pltpu.VMEM((lines, groups, span), jnp.bfloat16),
            pltpu.VMEM((lines, 2, groups, 2 * head), jnp.float32),
            pltpu.VMEM((lines, 2, groups, 2 * head), jnp.bfloat16),
            pltpu.VMEM((lines, 2, groups, 2 * head), jnp.bfloat16),
            pltpu.VMEM((heads * tokens, head), jnp.bfloat16),
            pltpu.VMEM((2, 8, head), jnp.float32),
            pltpu.VMEM((1, head), jnp.float32),
            pltpu.VMEM((1, head), jnp.float32),
            pltpu.SMEM(image_start.shape[:1], jnp.int32),
            pltpu.VMEM((1, head), jnp.float32),
            dma((10 + PIECES,)),
            dma((QUAD,)),
            dma((QUAD,)),
            dma((lines, 2)),
            dma((lines, 2)),
            dma((QUAD,)),
            dma((QUAD,)),
            dma((2, PIECES)),
            dma((2, PIECES)),
            dma((6,)),
            dma((6,)),
            dma((PIECES,)),
            dma((PIECES,)),
            dma((2, lines)),
            dma((2, lines)),
        ],
        compiler_params=pltpu.CompilerParams(
            collective_id=0, has_side_effects=True, vmem_limit_bytes=48 * 2**20
        ),
    )(
        pltpu.with_memory_space_constraint(text_states, pltpu.HBM),
        pltpu.with_memory_space_constraint(image_states, pltpu.HBM),
        pltpu.with_memory_space_constraint(image_start.reshape(-1), pltpu.HBM),
        pltpu.with_memory_space_constraint(w_query, pltpu.HBM),
        pltpu.with_memory_space_constraint(w_key, pltpu.HBM),
        pltpu.with_memory_space_constraint(w_value, pltpu.HBM),
        pltpu.with_memory_space_constraint(w_out, pltpu.HBM),
        pltpu.with_memory_space_constraint(query_gain, pltpu.HBM),
        pltpu.with_memory_space_constraint(key_gain, pltpu.HBM),
        pltpu.with_memory_space_constraint(jnp.broadcast_to(cross_gate[:, None], (1, head)), pltpu.HBM),
    )


def solution(mesh):
    placed = (
        P("pipe", "dp", None),
        P(None, ("dp", "pipe"), None),
        P(None, "dp"),
        P("pipe", None, None),
        P("pipe", "dp", None),
        P("pipe", "dp", None),
        P("pipe", None, None),
        P("pipe", None),
        P("pipe", None),
        P("pipe"),
    )
    fits = mesh.shape["pipe"] == 2 and mesh.shape["dp"] == QUAD * QUAD
    return jax.shard_map(
        local_fused if fits else local,
        mesh=mesh,
        in_specs=placed,
        out_specs=P("pipe", "dp", None),
        check_vma=False,
    )
```

```python
import functools
import math

import jax
import jax.numpy as jnp
from jax import lax
from jax.experimental import pallas as pl
from jax.experimental.pallas import tpu as pltpu
from jax.sharding import PartitionSpec as P

epsilon = 1e-06
MESH = pl.DeviceIdType.MESH
QUAD = 4
PIECES = 4


def shifted(block, axis, distance):
    devices = range(lax.axis_size(axis))
    route = [((i - distance) % len(devices), i) for i in devices]
    return lax.ppermute(block, axis, route)


def normalized(projected, scales):
    mean_square = jnp.mean(projected * projected, axis=-1, keepdims=True)
    return projected * lax.rsqrt(mean_square + epsilon) * scales


def keep_state(current, holding):
    return current


def local(
    text_states,
    image_states,
    image_start,
    w_query,
    w_key,
    w_value,
    w_out,
    query_gain,
    key_gain,
    cross_gate,
):
    sections = lax.axis_size("pipe")
    section_index = lax.axis_index("pipe")
    pictures = lax.all_gather(image_states, "pipe", axis=1, tiled=True)
    batches, image_rows, width = pictures.shape
    flattened = pictures.reshape(batches * image_rows, width)
    head_size = w_key.shape[2]
    head_count = w_query.shape[2] // head_size
    key_full, value_full = (
        lax.all_gather(w_key, "dp", axis=1, tiled=True),
        lax.all_gather(w_value, "dp", axis=1, tiled=True),
    )
    key_sums = jnp.dot(flattened, key_full[0], preferred_element_type=jnp.float32)
    value_sums = jnp.dot(flattened, value_full[0], preferred_element_type=jnp.float32)
    key_rows = (
        normalized(key_sums, key_gain[0])
        .astype(jnp.bfloat16)
        .reshape(batches, image_rows, head_size)
    )
    value_rows = value_sums.astype(jnp.bfloat16).reshape(batches, image_rows, head_size)
    query_weight = w_query[0]
    out_weight = w_out[0]
    factor = jnp.tanh(cross_gate[0])
    tok_rows = text_states.shape[1]
    positions = jnp.arange(tok_rows, dtype=jnp.int32)
    root_size = math.sqrt(head_size)

    def apply_layer(current, holding):
        own_keys = lax.dynamic_index_in_dim(key_rows, holding, 0, keepdims=False)
        own_values = lax.dynamic_index_in_dim(value_rows, holding, 0, keepdims=False)
        query_sums = jnp.dot(current, query_weight, preferred_element_type=jnp.float32)
        query_sums = query_sums.reshape(tok_rows * head_count, head_size)
        queries = normalized(query_sums, query_gain[0]).astype(jnp.bfloat16)
        scores = jnp.dot(queries, own_keys.T, preferred_element_type=jnp.float32) / root_size
        exponent = jnp.exp(scores)
        probs = (exponent / jnp.sum(exponent, axis=-1, keepdims=True)).astype(jnp.bfloat16)
        attended = jnp.dot(probs, own_values, preferred_element_type=jnp.float32).astype(
            jnp.bfloat16
        )
        attended = attended.reshape(tok_rows, head_count * head_size)
        update = jnp.dot(attended, out_weight, preferred_element_type=jnp.float32)
        first_seen = lax.dynamic_index_in_dim(image_start[:, 0], holding, 0, keepdims=False)
        seen = (positions >= first_seen).astype(jnp.float32)[:, None]
        return (current.astype(jnp.float32) + factor * seen * update).astype(jnp.bfloat16)

    current = text_states[0]
    for moment in range(sections):
        holding = jnp.mod(section_index - moment, sections)
        current = lax.cond(moment <= section_index, apply_layer, keep_state, current, holding)
        current = shifted(current, "pipe", 1)
    return current[None]


def kernel(
    lines,
    text_ref,
    image_ref,
    start_ref,
    wq_ref,
    wk_ref,
    wv_ref,
    wo_ref,
    qg_ref,
    kg_ref,
    gate_ref,
    out_ref,
    text_v,
    wq_v,
    wq_half,
    wo_v,
    joint_sum,
    joint,
    first,
    mixed,
    back,
    wkv,
    image_v,
    img,
    part,
    part_out,
    part_in,
    query_v,
    small,
    query_gain,
    key_gain,
    starts,
    load_sem,
    w_send,
    w_recv,
    i_send,
    i_recv,
    relay_send,
    relay_recv,
    big_send,
    big_recv,
    one_send,
    one_recv,
    back_send,
    back_recv,
    p_send,
    p_recv,
):
    place = lax.axis_index("dp")
    core = lax.axis_index("pipe")
    other = 1 - core
    line = place // QUAD
    spot = place % QUAD
    depth = wk_ref.shape[1]
    head = wk_ref.shape[2]
    tokens, width = text_v.shape[1:]
    heads = wq_ref.shape[2] // head
    image_rows = image_ref.shape[1]
    span = QUAD * depth

    def quad_peer(distance):
        return line * QUAD + (spot + distance) % QUAD

    def line_peer(distance):
        return ((line + distance) % lines) * QUAD + spot

    def rows_of(index):
        return pl.ds(pl.multiple_of(index * depth, depth), depth)

    own_rows = pl.ds(pl.multiple_of(core * image_rows, image_rows), image_rows)

    def columns_of(index):
        return pl.ds(pl.multiple_of(index * span, span), span)

    loads = [
        pltpu.make_async_copy(wk_ref.at[0], wkv.at[0, rows_of(spot), pl.ds(0, head)], load_sem.at[0]),
        pltpu.make_async_copy(wv_ref.at[0], wkv.at[0, rows_of(spot), pl.ds(head, head)], load_sem.at[1]),
        pltpu.make_async_copy(image_ref, image_v, load_sem.at[2]),
        pltpu.make_async_copy(image_ref.at[core, :, columns_of(line)], img.at[line, own_rows], load_sem.at[3]),
        pltpu.make_async_copy(qg_ref, query_gain, load_sem.at[4]),
        pltpu.make_async_copy(kg_ref, key_gain, load_sem.at[5]),
        pltpu.make_async_copy(start_ref, starts, load_sem.at[6]),
        pltpu.make_async_copy(text_ref.at[0], text_v.at[0], load_sem.at[7]),
        pltpu.make_async_copy(wq_ref.at[0], wq_v, load_sem.at[8]),
    ]
    for load in loads:
        load.start()

    barrier = pltpu.get_barrier_semaphore()
    peers = [(quad_peer(d), core) for d in range(1, QUAD)]
    peers += [(line_peer(d), side) for d in range(1, lines) for side in (core, other)]
    peers += [(place, other)]
    for peer in peers:
        pl.semaphore_signal(barrier, inc=1, device_id=peer, device_id_type=MESH)
    for load in loads[:3]:
        load.wait()
    pl.semaphore_wait(barrier, len(peers))

    weight_copies = [
        pltpu.make_async_remote_copy(
            src_ref=wkv.at[0, rows_of(spot)],
            dst_ref=wkv.at[0, rows_of(spot)],
            send_sem=w_send.at[distance],
            recv_sem=w_recv.at[distance],
            device_id=(quad_peer(distance), core),
            device_id_type=MESH,
        )
        for distance in range(1, QUAD)
    ]
    image_copies = [
        pltpu.make_async_remote_copy(
            src_ref=image_v.at[side, :, columns_of((line + distance) % lines)],
            dst_ref=img.at[line, own_rows],
            send_sem=i_send.at[distance, turn],
            recv_sem=i_recv.at[distance, turn],
            device_id=(line_peer(distance), side),
            device_id_type=MESH,
        )
        for distance in (*range(1, lines), 0)
        for turn, side in enumerate((core, other))
        if distance + turn > 0
    ]
    for i in range(QUAD - 1):
        weight_copies[i].start()
        for copy in image_copies[2 * i : 2 * i + 2]:
            copy.start()
    for copy in image_copies[2 * QUAD - 2 :]:
        copy.start()

    def across(src, dst, send, recv):
        return pltpu.make_async_remote_copy(
            src_ref=src,
            dst_ref=dst,
            send_sem=send,
            recv_sem=recv,
            device_id=(place, other),
            device_id_type=MESH,
        )

    stretch = width // PIECES
    out_pieces = [
        across(
            wo_ref.at[0, :, pl.ds(i * stretch, stretch)],
            wo_v.at[1, :, pl.ds(i * stretch, stretch)],
            big_send.at[0, i],
            big_recv.at[0, i],
        )
        for i in range(PIECES)
    ]
    half = PIECES // 2
    most = PIECES - 1
    query_pieces = [
        across(
            wq_ref.at[0, pl.ds(i * stretch, stretch)],
            wq_half.at[pl.ds(i * stretch, stretch)],
            big_send.at[1, i],
            big_recv.at[1, i],
        )
        for i in range(most)
    ]
    small_copy = across(small.at[0], small.at[1], one_send.at[0], one_recv.at[0])
    text_copy = across(text_ref.at[0], text_v.at[1], one_send.at[1], one_recv.at[1])
    first_copy = across(first.at[0], first.at[1], one_send.at[2], one_recv.at[2])
    joint_copy = across(joint.at[0], joint.at[1], one_send.at[3], one_recv.at[3])
    mixed_copies = [across(mixed.at[i], mixed.at[2 + i], one_send.at[4 + i], one_recv.at[4 + i]) for i in range(2)]
    quarter = stretch // 2
    back_copies = [
        across(
            back.at[:, pl.ds(i * quarter, quarter)],
            out_ref.at[0, :, pl.ds((PIECES + i) * quarter, quarter)],
            back_send.at[i],
            back_recv.at[i],
        )
        for i in range(PIECES)
    ]

    def relay(distance):
        rows = rows_of((spot + QUAD - distance) % QUAD)
        return across(wkv.at[0, rows], wkv.at[1, rows], relay_send.at[distance], relay_recv.at[distance])

    loads[4].wait()
    loads[5].wait()
    small[0, 0:1] = query_gain[...]
    small[0, 1:2] = key_gain[...]
    small[0, 2:3] = jnp.full((1, head), gate_ref[0], jnp.float32)

    small_copy.start()
    out_loads = [
        pltpu.make_async_copy(
            wo_ref.at[0, :, pl.ds(i * stretch, stretch)], wo_v.at[0, :, pl.ds(i * stretch, stretch)], load_sem.at[9 + i]
        )
        for i in range(PIECES)
    ]

    @pl.when(core == 0)
    def _():
        text_copy.start()
        for piece in reversed(out_pieces[half:]):
            piece.start()
        for load in out_loads[:most]:
            load.start()

    @pl.when(core == 1)
    def _():
        query_pieces[0].start()
        relay(0).start()
        for piece in query_pieces[1:]:
            piece.start()

    chunk = 2048

    def project(slots):
        rows = slots * tokens

        def step(i, total):
            at = pl.ds(pl.multiple_of(i * chunk, chunk), chunk)
            return total + jnp.dot(
                text_v[:slots, :, at].reshape(rows, chunk), wq_v[at, :], preferred_element_type=jnp.float32
            )

        return lax.fori_loop(0, width // chunk, step, jnp.zeros((rows, heads * head), jnp.float32))

    def store_queries(sums, slot):
        for h in range(heads):
            query_v[h * tokens : (h + 1) * tokens, :] = normalized(
                sums[:, h * head : (h + 1) * head], small[slot, 0:1]
            ).astype(jnp.bfloat16)

    def join(left, right):
        return jnp.dot(left, right, preferred_element_type=jnp.float32)

    loads[7].wait()
    loads[8].wait()

    def partial_sums(slot):
        groups = 2 * image_rows
        sums = jnp.dot(
            img[...].reshape(lines * groups, span), wkv[slot], preferred_element_type=jnp.float32
        )
        sums = sums.reshape(lines, groups, 2 * head)
        part[:, slot] = sums
        part_out[:, slot] = sums.astype(jnp.bfloat16)

    def partial_copy(slot, distance):
        return pltpu.make_async_remote_copy(
            src_ref=part_out.at[(line + distance) % lines, slot],
            dst_ref=part_in.at[line, slot],
            send_sem=p_send.at[slot, distance],
            recv_sem=p_recv.at[slot, distance],
            device_id=(line_peer(distance), core),
            device_id_type=MESH,
        )

    def arrived():
        loads[3].wait()
        for copy in image_copies:
            copy.wait_recv()

    def return_partials(slot):
        partial_sums(slot)
        for distance in range(1, lines):
            partial_copy(slot, distance).start()

    @pl.when(core == 0)
    def _():
        def join_own(i):
            out_loads[i].wait()
            query_pieces[i].wait_recv()
            at = pl.ds(i * stretch, stretch)
            return join(wo_v[0, :, at], wq_half[at, :])

        store_queries(project(1), 0)
        joint_sum[...] = join_own(0)
        for copy in weight_copies:
            copy.wait_recv()
        arrived()
        return_partials(0)
        for i in range(1, most - 1):
            joint_sum[...] += join_own(i)
        for distance in range(QUAD):
            relay(distance).wait_recv()
        return_partials(1)
        joint[0] = (joint_sum[...] + join_own(most - 1)).astype(jnp.bfloat16)
        small_copy.wait_recv()
        first_copy.wait_recv()

    @pl.when(core == 1)
    def _():
        text_copy.wait_recv()
        sums = project(2)
        store_queries(sums[:tokens], 0)
        first[0] = sums[tokens:]
        first_copy.start()
        for load in out_loads:
            load.start()
        for distance in range(1, QUAD):
            weight_copies[distance - 1].wait_recv()
            relay(distance).start()
        for piece in out_pieces[:half]:
            piece.start()
        arrived()
        return_partials(0)
        out_pieces[most].wait_recv()
        at = pl.ds(most * stretch, stretch)
        joint[0] = join(wo_v[1, :, at], wq_v[at, :]).astype(jnp.bfloat16)
        joint_copy.start()
        for load in out_loads:
            load.wait()
        small_copy.wait_recv()

    positions = lax.broadcasted_iota(jnp.int32, (tokens, 1), 0)
    loads[6].wait()
    seen = (positions >= starts[core]).astype(jnp.float32)
    seen_other = (positions >= starts[other]).astype(jnp.float32)
    root_size = math.sqrt(head)

    def attend(slot):
        total = part[line, slot]
        for distance in range(1, lines):
            partial_copy(slot, distance).wait_recv()
            total += part_in[(line + lines - distance) % lines, slot].astype(jnp.float32)
        keys = normalized(total[:, :head], small[slot, 1:2]).astype(jnp.bfloat16)
        values = total[:, head:].astype(jnp.bfloat16)
        scores = (
            lax.dot_general(
                query_v[...], keys, (((1,), (1,)), ((), ())), preferred_element_type=jnp.float32
            )
            / root_size
        )
        exponent = jnp.exp(scores)
        probs = (exponent / jnp.sum(exponent, axis=-1, keepdims=True)).astype(jnp.bfloat16)
        attended = jnp.dot(probs, values, preferred_element_type=jnp.float32).astype(jnp.bfloat16)
        attended = jnp.concatenate(
            [attended[h * tokens : (h + 1) * tokens] for h in range(heads)], axis=1
        )
        return attended

    def gate(slot):
        return jnp.tanh(small[slot, 2:3])[:, 0:1]

    def update(values, slot, at):
        return jnp.dot(values, wo_v[slot, :, at], preferred_element_type=jnp.float32)

    def advance(source, slot, attended, factor):
        for i in range(PIECES):
            at = pl.ds(i * quarter, quarter)
            out_ref[0, :, at] = (source[:, at].astype(jnp.float32) + factor * update(attended, slot, at)).astype(
                jnp.bfloat16
            )

    attended = attend(0)
    factor = gate(0) * seen

    @pl.when(core == 0)
    def _():
        mixed[0] = attended
        mixed_copies[0].start()
        change = jnp.dot(attended, joint[0], preferred_element_type=jnp.float32)
        joint_copy.wait_recv()
        change += jnp.dot(attended, joint[1], preferred_element_type=jnp.float32)
        store_queries(first[1] + factor * change, 1)
        later = attend(1)
        mixed[1] = later
        mixed_copies[1].start()
        advance(text_v.at[0], 0, attended, factor)
        for piece in out_pieces[:half]:
            piece.wait_recv()
        advance(out_ref.at[0], 1, later, gate(1) * seen)
        for copy in back_copies:
            copy.wait_recv()

    @pl.when(core == 1)
    def _():
        advance(text_v.at[0], 0, attended, factor)
        for piece in out_pieces[half:most]:
            piece.wait_recv()
        mixed_copies[0].wait_recv()
        before = gate(1) * seen_other
        for i in range(PIECES):
            at = pl.ds((PIECES + i) * quarter, quarter)
            back[:, i * quarter : (i + 1) * quarter] = (
                text_v[1, :, at].astype(jnp.float32) + before * update(mixed[2], 1, at)
            ).astype(jnp.bfloat16)
        mixed_copies[1].wait_recv()
        both = jnp.concatenate([attended, mixed[3]], axis=0)
        after = gate(0) * seen_other
        for i in range(PIECES):
            at = pl.ds((PIECES + i) * quarter, quarter)
            here = pl.ds(i * quarter, quarter)
            sums = update(both, 0, at)
            back[:, here] = (back[:, here].astype(jnp.float32) + after * sums[tokens:]).astype(jnp.bfloat16)
            back_copies[i].start()
            out_ref[0, :, at] = (text_v[0, :, at].astype(jnp.float32) + factor * sums[:tokens]).astype(jnp.bfloat16)

    for copy in image_copies + weight_copies:
        copy.wait_send()
    for distance in range(1, lines):
        partial_copy(0, distance).wait_send()

    small_copy.wait_send()

    @pl.when(core == 0)
    def _():
        for distance in range(1, lines):
            partial_copy(1, distance).wait_send()
        for copy in [text_copy] + mixed_copies + out_pieces[half:]:
            copy.wait_send()

    @pl.when(core == 1)
    def _():
        for distance in range(QUAD):
            relay(distance).wait_send()
        for copy in [first_copy, joint_copy] + query_pieces + out_pieces[:half] + back_copies:
            copy.wait_send()


def local_fused(
    text_states,
    image_states,
    image_start,
    w_query,
    w_key,
    w_value,
    w_out,
    query_gain,
    key_gain,
    cross_gate,
):
    lines = lax.axis_size("dp") // QUAD
    tokens, width = text_states.shape[1:]
    image_rows = image_states.shape[1]
    depth, head = w_key.shape[1:]
    columns = w_query.shape[2]
    heads = columns // head
    span = QUAD * depth
    groups = 2 * image_rows
    hbm = pl.BlockSpec(memory_space=pltpu.HBM)
    vmem = pl.BlockSpec(memory_space=pltpu.VMEM)
    smem = pl.BlockSpec(memory_space=pltpu.SMEM)
    dma = pltpu.SemaphoreType.DMA
    return pl.pallas_call(
        functools.partial(kernel, lines),
        out_shape=jax.ShapeDtypeStruct((1, tokens, width), jnp.bfloat16),
        in_specs=[hbm, hbm, hbm, hbm, hbm, hbm, hbm, hbm, hbm, smem],
        out_specs=vmem,
        scratch_shapes=[
            pltpu.VMEM((2, tokens, width), jnp.bfloat16),
            pltpu.VMEM((width, columns), jnp.bfloat16),
            pltpu.VMEM((width - width // PIECES, columns), jnp.bfloat16),
            pltpu.VMEM((2, columns, width), jnp.bfloat16),
            pltpu.VMEM((columns, columns), jnp.float32),
            pltpu.VMEM((2, columns, columns), jnp.bfloat16),
            pltpu.VMEM((2, tokens, columns), jnp.float32),
            pltpu.VMEM((4, tokens, columns), jnp.bfloat16),
            pltpu.VMEM((tokens, width // 2), jnp.bfloat16),
            pltpu.VMEM((2, span, 2 * head), jnp.bfloat16),
            pltpu.VMEM((2, image_rows, width), jnp.bfloat16),
            pltpu.VMEM((lines, groups, span), jnp.bfloat16),
            pltpu.VMEM((lines, 2, groups, 2 * head), jnp.float32),
            pltpu.VMEM((lines, 2, groups, 2 * head), jnp.bfloat16),
            pltpu.VMEM((lines, 2, groups, 2 * head), jnp.bfloat16),
            pltpu.VMEM((heads * tokens, head), jnp.bfloat16),
            pltpu.VMEM((2, 8, head), jnp.float32),
            pltpu.VMEM((1, head), jnp.float32),
            pltpu.VMEM((1, head), jnp.float32),
            pltpu.SMEM(image_start.shape[:1], jnp.int32),
            dma((9 + PIECES,)),
            dma((QUAD,)),
            dma((QUAD,)),
            dma((lines, 2)),
            dma((lines, 2)),
            dma((QUAD,)),
            dma((QUAD,)),
            dma((2, PIECES)),
            dma((2, PIECES)),
            dma((6,)),
            dma((6,)),
            dma((PIECES,)),
            dma((PIECES,)),
            dma((2, lines)),
            dma((2, lines)),
        ],
        compiler_params=pltpu.CompilerParams(
            collective_id=0, has_side_effects=True, vmem_limit_bytes=48 * 2**20
        ),
    )(
        pltpu.with_memory_space_constraint(text_states, pltpu.HBM),
        pltpu.with_memory_space_constraint(image_states, pltpu.HBM),
        pltpu.with_memory_space_constraint(image_start.reshape(-1), pltpu.HBM),
        pltpu.with_memory_space_constraint(w_query, pltpu.HBM),
        pltpu.with_memory_space_constraint(w_key, pltpu.HBM),
        pltpu.with_memory_space_constraint(w_value, pltpu.HBM),
        pltpu.with_memory_space_constraint(w_out, pltpu.HBM),
        pltpu.with_memory_space_constraint(query_gain, pltpu.HBM),
        pltpu.with_memory_space_constraint(key_gain, pltpu.HBM),
        cross_gate,
    )


def solution(mesh):
    placed = (
        P("pipe", "dp", None),
        P(None, ("dp", "pipe"), None),
        P(None, "dp"),
        P("pipe", None, None),
        P("pipe", "dp", None),
        P("pipe", "dp", None),
        P("pipe", None, None),
        P("pipe", None),
        P("pipe", None),
        P("pipe"),
    )
    fits = mesh.shape["pipe"] == 2 and mesh.shape["dp"] == QUAD * QUAD
    return jax.shard_map(
        local_fused if fits else local,
        mesh=mesh,
        in_specs=placed,
        out_specs=P("pipe", "dp", None),
        check_vma=False,
    )
```
